128 devices in a mesh: dp: 16 (over y, z_lo, core), row: 2 (over z_hi), col: 4 (over x).
Axes of the slice: x: 4, y: 4, z: 4 (z_hi: 2, z_lo: 2; z = z_hi * 2 + z_lo), core: 2. Of those that a mesh axis runs over, the one named last changes fastest.
Arguments:
- hidden_in: bfloat16 [19456, 1152], P(('dp', 'row', 'col')), may hold values from -6 to 6
- segments: int32 [19456], P('dp'), may hold values from 0 to 1, as said below
- positions: int32 [19456], P('dp'), may hold values from 0 to 4095, as said below
- out_grad: bfloat16 [19456, 1152], P(('dp', 'row', 'col')), may hold values from -6 to 6
- w_query: bfloat16 [1152, 1024], P('row', ('col', 'dp')), may hold values from -0.1875 to 0.1875
- w_key: bfloat16 [1152, 256], P('row', 'dp'), may hold values from -0.1875 to 0.1875
- w_value: bfloat16 [1152, 256], P('row', 'dp'), may hold values from -0.1875 to 0.1875
- w_out: bfloat16 [1024, 1152], P('col', ('row', 'dp')), may hold values from -0.1875 to 0.1875
- w_gate: bfloat16 [1152, 6912], P('row', ('col', 'dp')), may hold values from -0.1875 to 0.1875
- w_up: bfloat16 [1152, 6912], P('row', ('col', 'dp')), may hold values from -0.1875 to 0.1875
- w_down: bfloat16 [6912, 1152], P('col', ('row', 'dp')), may hold values from -0.078125 to 0.078125
- norm_gains: bfloat16 [4, 1152], P(None, ('row', 'col', 'dp')), may hold values from 0.25 to 1.75
- head_gains: bfloat16 [2, 256], P(None, 'dp'), may hold values from 0.25 to 1.75
Outputs:
- result: bfloat16 [19456, 1152], P(('dp', 'row', 'col'))
- input_grad: bfloat16 [19456, 1152], P(('dp', 'row', 'col'))
- grad_query: float32 [1152, 1024], P('row', ('col', 'dp'))
- grad_key: float32 [1152, 256], P('row', 'dp')
- grad_value: float32 [1152, 256], P('row', 'dp')
- grad_out: float32 [1024, 1152], P('col', ('row', 'dp'))
- grad_gate: float32 [1152, 6912], P('row', ('col', 'dp'))
- grad_up: float32 [1152, 6912], P('row', ('col', 'dp'))
- grad_down: float32 [6912, 1152], P('col', ('row', 'dp'))
- grad_norm_gains: float32 [4, 1152], P(None, ('row', 'col', 'dp'))
- grad_head_gains: float32 [2, 256], P(None, 'dp')
The draws below stay inside these ranges and needn't reach their ends.
Inputs may be any that keep to these rules, and one draw needn't show every extreme that they name: `segments`: in each sequence of 1216 tokens, segment 0 comes first and segment 1 follows; the shorter document has 202 to 303 tokens and lies at either end. Within a document positions rise by one from a start drawn for that document; every draw holds position 0 and position 4095.
All inputs are finite; a program needn't handle non-finite values.
Results may differ from the reference program's by a relative error of at most 0.035.
Values may be sent and summed in bfloat16 or wider, within the bound.
No kernel may reach another device: no remote copies, remote signals or barrier semaphores. Data moves between devices by JAX's collectives and lax.ppermute only.
A program may use at most 128 MiB of HBM per device.

```python
import math
import jax
import jax.numpy as jnp
from jax import lax

D = 1152
H = 4
HD = 256
FF = 6912
LEN = 1216
TOKENS = 19456


def document_cuts(key):
    seq_total = TOKENS // LEN
    offset = jax.random.randint(jax.random.fold_in(key, 101), (seq_total,), LEN // 6, LEN // 4)
    flipped = jax.random.randint(jax.random.fold_in(key, 102), (seq_total,), 0, 2)
    cut_points = jnp.where(flipped == 1, LEN - offset, offset)
    starts = jax.random.randint(jax.random.fold_in(key, 103), (seq_total, 2), 0, 4096 - LEN)
    first_row = jnp.arange(seq_total, dtype=jnp.int32) == 0
    later_start = jnp.where(first_row, 4096 - (LEN - cut_points), starts[:, 1])
    early_start = jnp.where(first_row, 0, starts[:, 0])
    starts = jnp.stack([early_start, later_start], axis=1).astype(jnp.int32)
    return (cut_points, starts)


def draw_segments(key, part):
    cut_points, starts = document_cuts(key)
    places = jnp.arange(LEN, dtype=jnp.int32)
    return (places[None, :] >= cut_points[:, None]).astype(jnp.int32).reshape(-1)


def draw_positions(key, part):
    cut_points, starts = document_cuts(key)
    places = jnp.arange(LEN, dtype=jnp.int32)
    second_doc = places[None, :] >= cut_points[:, None]
    later_pos = starts[:, 1:2] + places[None, :] - cut_points[:, None]
    early_pos = starts[:, 0:1] + places[None, :]
    return jnp.where(second_doc, later_pos, early_pos).astype(jnp.int32).reshape(-1)


def block_scale(own_key, extent, split, least, largest):
    def one(dim, shards_of):
        draws = jax.random.uniform(jax.random.fold_in(jax.random.fold_in(own_key, 6), dim), (shards_of,), jnp.float32, least / len(split), largest / len(split))
        return jnp.repeat(jnp.exp(draws), extent[dim] // shards_of).reshape((-1,) + (1,) * (len(extent) - dim - 1))

    loudness = one(*split[0])
    for cut in split[1:]:
        loudness = loudness * one(*cut)
    return loudness


def gaussian(key, shape, scale, bound, pieces=(), kind=jnp.bfloat16):
    values = scale * jax.random.normal(key, shape, jnp.float32)
    if pieces:
        values = values * block_scale(key, shape, pieces, -0.22, 0.18)
    return jnp.clip(values, -bound, bound).astype(kind)


def setup_inputs(seed: int = 0) -> dict:
    arg_keys = jax.random.split(jax.random.key(seed), 14)
    return {
        "hidden_in": gaussian(arg_keys[0], (TOKENS, D), 1.0, 6.0, ((0, 128),)),
        "segments": draw_segments(jax.random.fold_in(arg_keys[13], 71), 0),
        "positions": draw_positions(jax.random.fold_in(arg_keys[13], 71), 0),
        "out_grad": gaussian(arg_keys[3], (TOKENS, D), 1.0, 6.0, ((0, 128),)),
        "w_query": gaussian(arg_keys[4], (D, H * HD), D ** -0.5, 0.1875, ((0, 2), (1, 64))),
        "w_key": gaussian(arg_keys[5], (D, HD), D ** -0.5, 0.1875, ((0, 2), (1, 16))),
        "w_value": gaussian(arg_keys[6], (D, HD), D ** -0.5, 0.1875, ((0, 2), (1, 16))),
        "w_out": gaussian(arg_keys[7], (H * HD, D), (H * HD) ** -0.5, 0.1875, ((0, 4), (1, 32))),
        "w_gate": gaussian(arg_keys[8], (D, FF), D ** -0.5, 0.1875, ((0, 2), (1, 64))),
        "w_up": gaussian(arg_keys[9], (D, FF), D ** -0.5, 0.1875, ((0, 2), (1, 64))),
        "w_down": gaussian(arg_keys[10], (FF, D), FF ** -0.5, 0.078125, ((0, 4), (1, 32))),
        "norm_gains": jnp.clip(1.0 + 0.15 * jax.random.normal(arg_keys[11], (4, D), jnp.float32), 0.25, 1.75).astype(jnp.bfloat16),
        "head_gains": jnp.clip(1.0 + 0.15 * jax.random.normal(arg_keys[12], (2, HD), jnp.float32), 0.25, 1.75).astype(jnp.bfloat16),
    }


EPSILON = 1e-06
ROPE_BASE = 1000000.0
MASKED = -1e+30

@jax.custom_vjp
def low(v):
    return lax.optimization_barrier(v.astype(jnp.bfloat16)).astype(jnp.float32)

@jax.custom_vjp
def low_back(v):
    return v

def low_keep(v):
    return (low(v), None)

def low_pass(kept, grad):
    return (grad,)

def back_keep(v):
    return (v, None)

def back_low(kept, grad):
    return (low(grad),)
low.defvjp(low_keep, low_pass)
low_back.defvjp(back_keep, back_low)

def matmul(left, right):
    return jnp.dot(left, right, preferred_element_type=jnp.float32, precision=lax.Precision.HIGHEST)

def inverse_rms(values):
    return lax.rsqrt(lax.optimization_barrier(jnp.mean(values * values, axis=-1, keepdims=True)) + EPSILON)

def rotary_tables(places, head_width):
    frequencies = jnp.exp(jnp.arange(head_width // 2, dtype=jnp.float32) * (-2.0 * math.log(ROPE_BASE) / head_width))
    angles = places.astype(jnp.float32)[:, None] * frequencies[None, :]
    return (jnp.cos(angles), jnp.sin(angles))

def rotate(values, cosine, sine_part):
    midpoint = values.shape[-1] // 2
    front_half = values[..., :midpoint]
    back_half = values[..., midpoint:]
    cos_rows = cosine[:, None, :]
    sin_rows = sine_part[:, None, :]
    return jnp.concatenate([front_half * cos_rows - back_half * sin_rows, back_half * cos_rows + front_half * sin_rows], axis=-1)

def norm_rotate(raw_values, gain_row, cosine, sine_part):
    return rotate(raw_values * inverse_rms(raw_values) * gain_row, cosine, sine_part)

def block_forward(stream, query_weight, key_weight, value_weight, out_weight, gate_weight, up_weight, down_weight, gain_rows, head_gain, segment_row, position_row):
    length = stream.shape[0]
    head_count = query_weight.shape[1] // HD
    cosine, sine_part = rotary_tables(position_row, HD)
    normed_one = low(stream * inverse_rms(stream) * gain_rows[0])
    query_raw = low_back(matmul(normed_one, query_weight)).reshape(length, head_count, HD)
    key_raw = low_back(matmul(normed_one, key_weight)).reshape(length, 1, HD)
    value_low = low(low_back(matmul(normed_one, value_weight)))
    query_rot = low(norm_rotate(query_raw, head_gain[0], cosine, sine_part))
    key_rot = low(norm_rotate(key_raw, head_gain[1], cosine, sine_part))[:, 0, :]
    scores = low_back(jnp.einsum('qhd,kd->hqk', query_rot, key_rot, precision=lax.Precision.HIGHEST) * HD ** (-0.5))
    places = jnp.arange(length, dtype=jnp.int32)
    allowed = (segment_row[:, None] == segment_row[None, :]) & (places[:, None] >= places[None, :])
    scores = jnp.where(allowed[None], scores, MASKED)
    probs = low(jax.nn.softmax(scores, axis=-1))
    context = low(low_back(jnp.einsum('hqk,kd->qhd', probs, value_low, precision=lax.Precision.HIGHEST))).reshape(length, head_count * HD)
    attn_raw = low_back(matmul(context, out_weight))
    middle = stream + attn_raw * inverse_rms(attn_raw) * gain_rows[1]
    normed_two = low(middle * inverse_rms(middle) * gain_rows[2])
    gate_raw = low_back(matmul(normed_two, gate_weight))
    up_raw = low_back(matmul(normed_two, up_weight))
    hidden = low(jax.nn.gelu(gate_raw, approximate=True) * up_raw)
    down_raw = low_back(matmul(hidden, down_weight))
    return middle + down_raw * inverse_rms(down_raw) * gain_rows[3]

def reference(hidden_in, segments, positions, out_grad, w_query, w_key, w_value, w_out, w_gate, w_up, w_down, norm_gains, head_gains):
    seq_count = hidden_in.shape[0] // LEN
    params = tuple((weight_item.astype(jnp.float32) for weight_item in (w_query, w_key, w_value, w_out, w_gate, w_up, w_down, norm_gains, head_gains)))
    streams = hidden_in.astype(jnp.float32).reshape(seq_count, LEN, D)
    upstreams = out_grad.astype(jnp.float32).reshape(seq_count, LEN, D)
    segment_rows = segments.reshape(seq_count, LEN)
    position_rows = positions.reshape(seq_count, LEN)

    def one_sequence(totals, sequence_items):
        stream, upstream, segment_row, position_row = sequence_items

        def forward_fn(stream_in, *weights_in):
            return block_forward(stream_in, *weights_in, segment_row, position_row)
        output_row, pullback = jax.vjp(forward_fn, stream, *params)
        gradients = pullback(upstream)
        totals = tuple((running + fresh for running, fresh in zip(totals, gradients[1:])))
        return (totals, (output_row, gradients[0]))
    zero_totals = tuple((jnp.zeros_like(weight_item) for weight_item in params))
    totals, (outputs, input_grads) = lax.scan(one_sequence, zero_totals, (streams, upstreams, segment_rows, position_rows))
    output_low = outputs.reshape(seq_count * LEN, D).astype(jnp.bfloat16)
    grad_low = input_grads.reshape(seq_count * LEN, D).astype(jnp.bfloat16)
    return (output_low, grad_low, totals[0], totals[1], totals[2], totals[3], totals[4], totals[5], totals[6], totals[7], totals[8])
```

```python
import math

import jax
import jax.numpy as jnp
from jax import lax
from jax.experimental import pallas as pl
from jax.experimental.pallas import tpu as pltpu
from jax.sharding import Mesh, PartitionSpec as P

D = 1152
HALF = 576
H = 4
HD = 256
FF = 6912
LEN = 1216
OWN = 152
UNITS = 54
PADDED = 56
DOWN_A = 32
DOWN_B = PADDED - DOWN_A
EPSILON = 1e-06
ROPE_BASE = 1000000.0
MASKED = -1e30
SCALE = HD ** (-0.5)
Z = ("zl", "zh")
LOW = jnp.bfloat16
F32 = jnp.float32


def shift(v, axis, step):
    if axis == Z:
        own = [(i % 2) * 2 + i // 2 for i in range(4)]
        return lax.ppermute(v, axis, [(own[i], own[(i + step) % 4]) for i in range(4)])
    size = lax.axis_size(axis)
    return lax.ppermute(v, axis, [(i, (i + step) % size) for i in range(size)])


def swap(v, axis):
    return shift(v, axis, 1)


def gather_direct(v, axis):
    return [v, shift(v, axis, -1), shift(v, axis, -2), shift(v, axis, 1)]


def half_of(v):
    if v.ndim > 2:
        return v.shape[0] // 2
    return (v.shape[0] // 2 + 7) // 8 * 8


def gather_ring(v, axis):
    half = half_of(v)
    before = shift(v, axis, 1)
    after = shift(v, axis, -1)
    opposite = jnp.concatenate(
        [shift(before[:half], axis, 1), shift(after[half:], axis, -1)], axis=0
    )
    return [v, after, opposite, before]


def add(*parts):
    total = parts[0].astype(F32)
    for part in parts[1:]:
        total = total + part.astype(F32)
    return total


def scatter_ring(blocks, axis):
    own, after, opposite, before = blocks
    half = half_of(own)
    passed_up = shift(opposite[:half], axis, 1)
    passed_down = shift(opposite[half:], axis, -1)
    up = jnp.concatenate([add(after[:half], passed_up).astype(LOW), after[half:]], axis=0)
    down = jnp.concatenate([before[:half], add(before[half:], passed_down).astype(LOW)], axis=0)
    return add(own, shift(up, axis, 1), shift(down, axis, -1))


def scatter_direct(blocks, axis):
    own, after, opposite, before = blocks
    return add(own, shift(after, axis, 1), shift(opposite, axis, 2), shift(before, axis, -1))


def whole(shape, dtype):
    return jax.ShapeDtypeStruct(shape, dtype)


VMEM = pl.BlockSpec(memory_space=pltpu.VMEM)
SMEM = pl.BlockSpec(memory_space=pltpu.SMEM)
BIG = pltpu.CompilerParams(vmem_limit_bytes=32 * 1024 * 1024)


def row_blocks(place_ref):
    for y in range(4):
        for zl in range(2):
            first = place_ref[(y * 2 + zl) * 2]
            second = place_ref[(y * 2 + zl) * 2 + 1]
            for side in range(2):
                row = y * 64 + zl * 32 + place_ref[16 + side] * 16
                yield side, first, second, pl.multiple_of(row, 16)


def joined(ref, first, second):
    pair = [ref[first].astype(F32), ref[second].astype(F32)]
    return jnp.concatenate(pair, axis=0).astype(LOW)


def assemble_heads(place, mine, other):
    heads = mine.shape[0]

    def kernel(place_ref, mine_ref, other_ref, out_ref):
        for side, first, second, row in row_blocks(place_ref):
            ref = other_ref if side else mine_ref
            for h in range(heads):
                out_ref[pl.ds(row + h * HD, 16), :] = joined(ref.at[h], first, second)

    return pl.pallas_call(
        kernel,
        out_shape=whole((heads * HD, D), LOW),
        in_specs=[SMEM, VMEM, VMEM],
        out_specs=VMEM,
        compiler_params=BIG,
    )(place, mine, other)


def assemble_pair(place, mine, other):
    def kernel(place_ref, mine_ref, other_ref, key_ref, value_ref, gain_ref):
        for side, first, second, row in row_blocks(place_ref):
            ref = other_ref if side else mine_ref
            key_ref[pl.ds(row, 16), :] = joined(ref.at[0], first, second)
            value_ref[pl.ds(row, 16), :] = joined(ref.at[1], first, second)
        total = mine_ref[2, 0].astype(F32) + other_ref[2, 0].astype(F32)
        for k in range(1, 16):
            total = total + mine_ref[2, k].astype(F32) + other_ref[2, k].astype(F32)
        gain_ref[...] = total

    return pl.pallas_call(
        kernel,
        out_shape=(whole((HD, D), LOW), whole((HD, D), LOW), whole((8, D), F32)),
        in_specs=[SMEM, VMEM, VMEM],
        out_specs=(VMEM, VMEM, VMEM),
        compiler_params=BIG,
    )(place, mine, other)


def divide_heads(place, grad):
    heads = grad.shape[0] // HD

    def kernel(place_ref, grad_ref, mine_ref, other_ref):
        for side, first, second, row in row_blocks(place_ref):
            ref = other_ref if side else mine_ref
            for h in range(heads):
                rows = grad_ref[pl.ds(row + h * HD, 16), :].astype(F32)
                ref[h, first] = rows[:8].astype(LOW)
                ref[h, second] = rows[8:].astype(LOW)

    return pl.pallas_call(
        kernel,
        out_shape=(whole((heads, 16, 8, D), LOW),) * 2,
        in_specs=[SMEM, VMEM],
        out_specs=(VMEM, VMEM),
        compiler_params=BIG,
    )(place, grad)


def divide_pair(place, key_grad, value_grad, gain_grad):
    def kernel(place_ref, key_ref, value_ref, gain_ref, mine_ref, other_ref):
        gains = gain_ref[...].astype(LOW)
        for side, first, second, row in row_blocks(place_ref):
            ref = other_ref if side else mine_ref
            for part, grad_ref in enumerate((key_ref, value_ref)):
                rows = grad_ref[pl.ds(row, 16), :].astype(F32)
                ref[first, part] = rows[:8].astype(LOW)
                ref[second, part] = rows[8:].astype(LOW)
            ref[first, 2] = gains
            ref[second, 2] = gains

    return pl.pallas_call(
        kernel,
        out_shape=(whole((16, 3, 8, D), LOW),) * 2,
        in_specs=[SMEM, VMEM, VMEM, VMEM],
        out_specs=(VMEM, VMEM),
        compiler_params=BIG,
    )(place, key_grad, value_grad, gain_grad)


def dot_nt(a, b):
    return lax.dot_general(a, b, (((1,), (1,)), ((), ())), preferred_element_type=F32)


def dot_nn(a, b):
    return lax.dot_general(a, b, (((1,), (0,)), ((), ())), preferred_element_type=F32)


def dot_tn(a, b):
    return lax.dot_general(a, b, (((0,), (0,)), ((), ())), preferred_element_type=F32)


def inverse_rms(values):
    return lax.rsqrt(jnp.mean(values * values, axis=-1, keepdims=True) + EPSILON)


def norm_backward(upstream, source, inverse, gain_row):
    weighted = upstream * gain_row
    inner = jnp.mean(weighted * source, axis=-1, keepdims=True)
    source_grad = inverse * weighted - source * (inverse * inverse * inverse) * inner
    gain_grad = jnp.sum(upstream * source * inverse, axis=0)
    return source_grad, gain_grad


def rotary_tables(places):
    frequencies = jnp.exp(
        jnp.arange(HD // 2, dtype=F32) * (-2.0 * math.log(ROPE_BASE) / HD)
    )
    angles = places.astype(F32)[:, None] * frequencies[None, :]
    return jnp.cos(angles), jnp.sin(angles)


def rotate(values, cosine, sine):
    front, back = values[..., : HD // 2], values[..., HD // 2 :]
    return jnp.concatenate(
        [front * cosine - back * sine, back * cosine + front * sine], axis=-1
    )


def in_order(first, mine, other):
    return jnp.where(first, mine, other), jnp.where(first, other, mine)


def on_device(
    hidden_in,
    segments,
    positions,
    out_grad,
    w_query,
    w_key,
    w_value,
    w_out,
    w_gate,
    w_up,
    w_down,
    norm_gains,
    head_gains,
):
    iy = lax.axis_index("y")
    izh = lax.axis_index("zh")
    iz = izh * 2 + lax.axis_index("zl")
    ix = lax.axis_index("x")
    ic = lax.axis_index("core")
    izl = lax.axis_index("zl")
    ring = jnp.arange(4, dtype=jnp.int32)
    z_of = jnp.array([0, 2, 1, 3], jnp.int32)
    place = jnp.concatenate(
        [
            (((ring - iy) % 4)[:, None] * 4 + ((z_of - iz) % 4)[None, :]).reshape(16),
            jnp.stack([ic, 1 - ic]).astype(jnp.int32),
        ]
    )

    def whole_rows(turned):
        count = turned.shape[-2] // 2
        turned = turned.reshape(turned.shape[:-2] + (2, count, HALF))
        axis = turned.ndim - 3
        mine = lax.dynamic_index_in_dim(turned, izh, axis, False)
        other = swap(lax.dynamic_index_in_dim(turned, 1 - izh, axis, False), "zh")
        return jnp.concatenate(in_order(izh == 0, mine, other), axis=-1)

    def shard_rows(rows):
        turned = rows.reshape(rows.shape[:-1] + (2, HALF))
        axis = turned.ndim - 2
        mine = lax.dynamic_index_in_dim(turned, izh, axis, False)
        other = lax.dynamic_index_in_dim(turned, 1 - izh, axis, False).astype(LOW)
        other = swap(other, "zh").astype(F32)
        return jnp.concatenate(in_order(izh == 0, mine, other), axis=-2)

    gain_place = (((izh * 4 + ix) * 4 + iy) * 4 + izl * 2 + ic) * 9
    head_place = (iy * 4 + izl * 2 + ic) * 16
    gains = lax.dynamic_update_slice(jnp.zeros((4, D), LOW), norm_gains, (0, gain_place))
    heads = lax.dynamic_update_slice(jnp.zeros((2, HD), LOW), head_gains, (0, head_place))
    heads = jnp.where((izh == 0) & (ix == 0), heads, jnp.zeros((), LOW)).reshape(1, 2 * HD)
    misc = jnp.concatenate(
        [gains, jnp.pad(heads, ((0, 0), (0, D - 2 * HD))), jnp.zeros((3, D), LOW)], axis=0
    )
    misc = add(*gather_direct(misc, "x")).astype(LOW)
    rows = whole_rows(jnp.stack([w_key.T, w_value.T, w_query.T]))
    pack = jnp.concatenate([rows.reshape(24, D), misc], axis=0)
    pack = jnp.stack(gather_direct(pack, Z))
    pack = jnp.concatenate(gather_ring(pack, "y"), axis=0).reshape(16, 4, 8, D)
    pack = pack.transpose(1, 0, 2, 3)
    pair_part = jnp.stack([pack[0], pack[1], pack[3]])
    key_weight, value_weight, misc = assemble_pair(place, pair_part, swap(pair_part, "core"))
    gain_rows = misc[:4]
    head_gain = misc[4, : 2 * HD].reshape(2, HD)
    query_part = jnp.stack(gather_ring(pack[2], "x"))
    query_weight = assemble_heads(place, query_part, swap(query_part, "core"))

    stream = hidden_in.astype(F32)
    scale_one = inverse_rms(stream)
    normed_one = (stream * scale_one * gain_rows[0]).astype(LOW)
    key_raw = dot_nt(normed_one, key_weight)
    value_low = dot_nt(normed_one, value_weight).astype(LOW)
    token_start = (izh * 4 + ix) * OWN
    own_positions = lax.dynamic_slice_in_dim(positions, token_start, OWN)
    own_segments = lax.dynamic_slice_in_dim(segments, token_start, OWN)
    cosine, sine = rotary_tables(own_positions)
    key_rot, key_back = jax.vjp(
        lambda raw, gain: rotate(raw * inverse_rms(raw) * gain, cosine, sine),
        key_raw,
        head_gain[1],
    )
    pair = jnp.concatenate([key_rot.astype(LOW), value_low], axis=1)
    pair = jnp.stack([pair, swap(pair, "zh")])
    pair = jnp.concatenate(gather_ring(pair, "x"), axis=0)
    pair = pair.reshape(LEN, 2 * HD)
    keys, values = pair[:, :HD], pair[:, HD:]
    key_start = jnp.stack(
        [((izh + b) % 2 * 4 + (ix + a) % 4) * OWN for a in range(4) for b in range(2)]
    )
    key_order = (key_start[:, None] + jnp.arange(OWN, dtype=jnp.int32)[None, :]).reshape(LEN)
    key_segments = jnp.concatenate(
        [lax.dynamic_slice_in_dim(segments, key_start[k], OWN) for k in range(8)]
    )

    query_raw = dot_nt(normed_one, query_weight).reshape(OWN, H, HD)
    query_norm, query_back = jax.vjp(
        lambda raw, gain: rotate(
            raw * inverse_rms(raw) * gain, cosine[:, None, :], sine[:, None, :]
        ),
        query_raw,
        head_gain[0],
    )
    query_rot = query_norm.astype(LOW).transpose(1, 0, 2).reshape(H * OWN, HD)
    query_order = token_start + jnp.arange(OWN, dtype=jnp.int32)
    allowed = (own_segments[:, None] == key_segments[None, :]) & (
        query_order[:, None] >= key_order[None, :]
    )
    scores = (dot_nt(query_rot, keys) * SCALE).reshape(H, OWN, LEN)
    scores = jnp.where(allowed[None], scores, MASKED)
    exponent = jnp.exp(scores - jnp.max(scores, axis=-1, keepdims=True))
    probs = (exponent / jnp.sum(exponent, axis=-1, keepdims=True)).reshape(H * OWN, LEN)
    probs_low = probs.astype(LOW)
    context = dot_nn(probs_low, values).astype(LOW)
    context = context.reshape(H, OWN, HD).transpose(1, 0, 2).reshape(OWN, H * HD)

    across = ("y", "zl", "core", "zh")
    down_rows = jnp.concatenate(
        [w_down.reshape(32, UNITS, 36), w_out.reshape(32, 8, 36)], axis=1
    )
    down_rows = lax.all_to_all(down_rows, across, 0, 0, tiled=True)
    down_rows = (
        down_rows.reshape(16, 2, UNITS + 8, 36).transpose(2, 1, 0, 3).reshape(UNITS + 8, D)
    )

    def pad_units(v):
        return jnp.pad(v, ((0, PADDED - UNITS), (0, 0)))

    rows = whole_rows(jnp.stack([w_gate.T, w_up.T]))
    gate_rows, up_rows = pad_units(rows[0]), pad_units(rows[1])
    out_rows = down_rows[UNITS:]
    down_rows = pad_units(down_rows[:UNITS])
    side_a = jnp.concatenate([gate_rows, down_rows[:DOWN_A], out_rows], axis=0)
    side_b = jnp.concatenate([up_rows, down_rows[DOWN_A:]], axis=0)
    side_a = jnp.stack(gather_ring(jnp.stack(gather_ring(side_a, "y")), Z))
    side_b = jnp.stack(gather_ring(jnp.stack(gather_ring(side_b, Z)), "y"), axis=1)
    units = 16 * PADDED
    gate_weight = side_a[:, :, :PADDED].reshape(units, D)
    up_weight = side_b[:, :, :PADDED].reshape(units, D)
    down_weight = jnp.concatenate(
        [side_a[:, :, PADDED : PADDED + DOWN_A], side_b[:, :, PADDED:]], axis=2
    ).reshape(units, D)
    out_part = side_a[:, :, PADDED + DOWN_A :].transpose(1, 0, 2, 3).reshape(16, 8, D)
    out_part = jnp.stack(gather_ring(out_part, "x"))
    out_weight = assemble_heads(place, out_part, swap(out_part, "core"))

    def spread_tokens(v):
        mine = jnp.concatenate(gather_ring(v, "x"), axis=0)
        return jnp.concatenate([mine, swap(mine, "core")], axis=0)

    def sum_tokens(v):
        v = v.reshape(2, 4, OWN, D)
        mine = add(v[0], swap(v[1], "core")).astype(LOW)
        return scatter_ring([mine[0], mine[1], mine[2], mine[3]], "x")

    attn_raw = dot_nn(context, out_weight)
    scale_two = inverse_rms(attn_raw)
    middle = stream + attn_raw * scale_two * gain_rows[1]
    scale_three = inverse_rms(middle)
    normed_two = (middle * scale_three * gain_rows[2]).astype(LOW)
    wide_two = spread_tokens(normed_two)
    gate_raw = dot_nt(wide_two, gate_weight)
    up_raw = dot_nt(wide_two, up_weight)
    activated, gelu_back = jax.vjp(
        lambda gate, up: jax.nn.gelu(gate, approximate=True) * up, gate_raw, up_raw
    )
    hidden = activated.astype(LOW)
    down_raw = sum_tokens(dot_nn(hidden, down_weight).astype(LOW))
    scale_four = inverse_rms(down_raw)
    result = (middle + down_raw * scale_four * gain_rows[3]).astype(LOW)
    upstream = out_grad.astype(F32)
    down_grad, gain_four = norm_backward(upstream, down_raw, scale_four, gain_rows[3])
    down_wide = spread_tokens(down_grad.astype(LOW))
    hidden_grad = dot_nt(down_wide, down_weight)
    gate_grad, up_grad = gelu_back(hidden_grad)
    gate_low, up_low = gate_grad.astype(LOW), up_grad.astype(LOW)
    normed_two_grad = sum_tokens(
        (dot_nn(gate_low, gate_weight) + dot_nn(up_low, up_weight)).astype(LOW)
    )
    grad_down = dot_tn(hidden, down_wide).astype(LOW).reshape(4, 4, PADDED, D)
    grad_gate = dot_tn(gate_low, wide_two).astype(LOW).reshape(4, 4, PADDED, D)
    grad_up = dot_tn(up_low, wide_two).astype(LOW).reshape(4, 4, PADDED, D)
    side_a = jnp.concatenate([grad_gate, grad_down[:, :, :DOWN_A]], axis=2)
    side_b = jnp.concatenate([grad_up, grad_down[:, :, DOWN_A:]], axis=2)
    side_a = scatter_ring(list(side_a), Z).astype(LOW)
    side_a = scatter_ring(list(side_a), "y")
    side_b = scatter_ring([side_b[:, k] for k in range(4)], "y").astype(LOW)
    side_b = scatter_ring(list(side_b), Z)

    both = shard_rows(jnp.stack([side_a[:UNITS], side_b[:UNITS]]))
    gate_shard, up_shard = both[0].T, both[1].T
    down_rows = jnp.concatenate([side_a[PADDED:], side_b[PADDED:]], axis=0)[:UNITS].astype(LOW)

    middle_part, gain_three = norm_backward(normed_two_grad, middle, scale_three, gain_rows[2])
    middle_grad = upstream + middle_part
    attn_grad, gain_two = norm_backward(middle_grad, attn_raw, scale_two, gain_rows[1])
    attn_low = attn_grad.astype(LOW)
    context_grad = dot_nt(attn_low, out_weight).astype(LOW)
    context_grad = context_grad.reshape(OWN, H, HD).transpose(1, 0, 2).reshape(H * OWN, HD)
    prob_grad = dot_nt(context_grad, values)
    centre = jnp.sum(probs * prob_grad, axis=-1, keepdims=True)
    score_low = (probs * (prob_grad - centre)).astype(LOW)
    key_part = dot_tn(score_low, query_rot) * SCALE
    value_part = dot_tn(probs_low, context_grad)
    pair_grad = jnp.concatenate([key_part, value_part], axis=1).astype(LOW)
    pair_grad = pair_grad.reshape(4, 2, OWN, 2 * HD)
    pair_grad = scatter_ring(list(pair_grad), "x")
    pair_grad = add(pair_grad[0], swap(pair_grad[1].astype(LOW), "zh"))
    query_grad = (dot_nn(score_low, keys) * SCALE).reshape(H, OWN, HD).transpose(1, 0, 2)
    query_raw_grad, query_gain = query_back(query_grad)
    query_low = query_raw_grad.reshape(OWN, H * HD).astype(LOW)
    key_raw_grad, key_gain = key_back(pair_grad[:, :HD])
    key_low = key_raw_grad.astype(LOW)
    value_grad_low = pair_grad[:, HD:].astype(LOW)
    normed_one_grad = (
        dot_nn(query_low, query_weight)
        + dot_nn(key_low, key_weight)
        + dot_nn(value_grad_low, value_weight)
    )
    stream_part, gain_one = norm_backward(normed_one_grad, stream, scale_one, gain_rows[0])
    input_grad = (middle_grad + stream_part).astype(LOW)

    def over_groups(blocks):
        blocks = blocks.reshape((4, 4) + blocks.shape[1:])
        blocks = scatter_ring(list(blocks), "y").astype(LOW)
        return scatter_direct(list(blocks), Z)

    def over_heads(grad):
        mine, other = divide_heads(place, grad.astype(LOW))
        mine = add(mine, swap(other, "core")).astype(LOW)
        return over_groups(scatter_ring(list(mine), "x").astype(LOW))

    out_rows = over_heads(dot_tn(context, attn_low)).astype(LOW)
    down_rows = jnp.concatenate([down_rows, out_rows], axis=0)
    down_rows = down_rows.reshape(UNITS + 8, 2, 16, 36).transpose(2, 1, 0, 3)
    down_rows = lax.all_to_all(
        down_rows.reshape(32, UNITS + 8, 36), across, 0, 0, tiled=True
    ).astype(F32)
    down_shard = down_rows[:, :UNITS].reshape(32 * UNITS, 36)
    out_shard = down_rows[:, UNITS:].reshape(HD, 36)

    query_rows = over_heads(dot_tn(query_low, normed_one))
    gains_grad = jnp.stack([gain_one, gain_two, gain_three, gain_four])
    head_grad = jnp.concatenate([query_gain, key_gain]).reshape(1, 2 * HD)
    misc = jnp.concatenate(
        [gains_grad, jnp.pad(head_grad, ((0, 0), (0, D - 2 * HD))), jnp.zeros((3, D), F32)], axis=0
    )
    mine, other = divide_pair(
        place,
        dot_tn(key_low, normed_one).astype(LOW),
        dot_tn(value_grad_low, normed_one).astype(LOW),
        misc,
    )
    pair_rows = over_groups(add(mine, swap(other, "core")).astype(LOW)).astype(LOW)
    pair_rows = add(*gather_direct(pair_rows, "x"))
    rows = shard_rows(jnp.stack([query_rows, pair_rows[0], pair_rows[1]]))
    query_shard, key_shard, value_shard = rows[0].T, rows[1].T, rows[2].T
    gains_shard = lax.dynamic_slice(pair_rows[2], (0, gain_place), (4, 9))
    head_shard = lax.dynamic_slice(
        pair_rows[2, 4, : 2 * HD].reshape(2, HD), (0, head_place), (2, 16)
    )
    return (
        result,
        input_grad,
        query_shard,
        key_shard,
        value_shard,
        out_shard,
        gate_shard,
        up_shard,
        down_shard,
        gains_shard,
        head_shard,
    )


def solution(mesh):
    split = Mesh(mesh.devices.reshape(4, 2, 2, 2, 4), ("y", "zl", "core", "zh", "x"))
    dp = ("y", "zl", "core")
    weights = (
        P("zh", ("x",) + dp),
        P("zh", dp),
        P("zh", dp),
        P("x", ("zh",) + dp),
        P("zh", ("x",) + dp),
        P("zh", ("x",) + dp),
        P("x", ("zh",) + dp),
        P(None, ("zh", "x") + dp),
        P(None, dp),
    )
    tokens = P(dp + ("zh", "x"), None)
    return jax.shard_map(
        on_device,
        mesh=split,
        in_specs=(tokens, P(dp), P(dp), tokens) + weights,
        out_specs=(tokens, tokens) + weights,
        check_vma=False,
    )
```

```python
import math

import jax
import jax.numpy as jnp
from jax import lax
from jax.experimental import pallas as pl
from jax.experimental.pallas import tpu as pltpu
from jax.sharding import Mesh, PartitionSpec as P

D = 1152
HALF = 576
H = 4
HD = 256
FF = 6912
LEN = 1216
OWN = 152
UNITS = 108
PADDED = 112
EPSILON = 1e-06
ROPE_BASE = 1000000.0
MASKED = -1e30
SCALE = HD ** (-0.5)
LOW = jnp.bfloat16
F32 = jnp.float32


def shift(v, axis, step):
    size = lax.axis_size(axis)
    return lax.ppermute(v, axis, [(i, (i + step) % size) for i in range(size)])


def swap(v, axis):
    return shift(v, axis, 1)


def gather_direct(v, axis):
    return [v, shift(v, axis, -1), shift(v, axis, -2), shift(v, axis, 1)]


def half_of(v):
    if v.ndim > 2:
        return v.shape[0] // 2
    return (v.shape[0] // 2 + 7) // 8 * 8


def gather_ring(v, axis):
    half = half_of(v)
    before = shift(v, axis, 1)
    after = shift(v, axis, -1)
    opposite = jnp.concatenate(
        [shift(before[:half], axis, 1), shift(after[half:], axis, -1)], axis=0
    )
    return [v, after, opposite, before]


def add(*parts):
    total = parts[0].astype(F32)
    for part in parts[1:]:
        total = total + part.astype(F32)
    return total


def scatter_ring(blocks, axis):
    own, after, opposite, before = blocks
    half = half_of(own)
    passed_up = shift(opposite[:half], axis, 1)
    passed_down = shift(opposite[half:], axis, -1)
    up = jnp.concatenate([add(after[:half], passed_up).astype(LOW), after[half:]], axis=0)
    down = jnp.concatenate([before[:half], add(before[half:], passed_down).astype(LOW)], axis=0)
    return add(own, shift(up, axis, 1), shift(down, axis, -1))


def whole(shape, dtype):
    return jax.ShapeDtypeStruct(shape, dtype)


VMEM = pl.BlockSpec(memory_space=pltpu.VMEM)
SMEM = pl.BlockSpec(memory_space=pltpu.SMEM)
BIG = pltpu.CompilerParams(vmem_limit_bytes=32 * 1024 * 1024)


def row_blocks(place_ref):
    for y in range(4):
        for zl in range(2):
            for side in range(2):
                row = y * 64 + zl * 32 + place_ref[8 + side] * 16
                yield side, place_ref[y * 2 + zl], pl.multiple_of(row, 16)


def assemble(place, mine, other, parts):
    heads, summed = mine.shape[0], mine.shape[2] > parts

    def kernel(place_ref, mine_ref, other_ref, *out_refs):
        for side, block, row in row_blocks(place_ref):
            ref = other_ref if side else mine_ref
            for h in range(heads):
                for part in range(parts):
                    out_refs[part][pl.ds(row + h * HD, 16), :] = ref[h, block, part]
        if summed:
            total = mine_ref[0, 0, parts].astype(F32) + other_ref[0, 0, parts].astype(F32)
            for k in range(1, 8):
                total = total + mine_ref[0, k, parts].astype(F32)
                total = total + other_ref[0, k, parts].astype(F32)
            out_refs[parts][...] = total

    shapes = [whole((heads * HD, D), LOW)] * parts + [whole((16, D), F32)] * summed
    return pl.pallas_call(
        kernel,
        out_shape=shapes,
        in_specs=[SMEM, VMEM, VMEM],
        out_specs=[VMEM] * len(shapes),
        compiler_params=BIG,
    )(place, mine, other)


def divide(place, grads, everywhere=None):
    heads, parts = grads[0].shape[0] // HD, len(grads)
    given = list(grads) + ([] if everywhere is None else [everywhere])

    def kernel(place_ref, *refs):
        grad_refs, (mine_ref, other_ref) = refs[: len(given)], refs[len(given) :]
        for side, block, row in row_blocks(place_ref):
            ref = other_ref if side else mine_ref
            for h in range(heads):
                for part in range(parts):
                    ref[h, block, part] = grad_refs[part][pl.ds(row + h * HD, 16), :]
            if everywhere is not None:
                ref[0, block, parts] = grad_refs[parts][...]

    return pl.pallas_call(
        kernel,
        out_shape=(whole((heads, 8, len(given), 16, D), LOW),) * 2,
        in_specs=[SMEM] + [VMEM] * len(given),
        out_specs=(VMEM, VMEM),
        compiler_params=BIG,
    )(place, *given)


def dot_nt(a, b):
    return lax.dot_general(a, b, (((1,), (1,)), ((), ())), preferred_element_type=F32)


def dot_nn(a, b):
    return lax.dot_general(a, b, (((1,), (0,)), ((), ())), preferred_element_type=F32)


def dot_tn(a, b):
    return lax.dot_general(a, b, (((0,), (0,)), ((), ())), preferred_element_type=F32)


def inverse_rms(values):
    return lax.rsqrt(jnp.mean(values * values, axis=-1, keepdims=True) + EPSILON)


def norm_backward(upstream, source, inverse, gain_row):
    weighted = upstream * gain_row
    inner = jnp.mean(weighted * source, axis=-1, keepdims=True)
    source_grad = inverse * weighted - source * (inverse * inverse * inverse) * inner
    gain_grad = jnp.sum(upstream * source * inverse, axis=0)
    return source_grad, gain_grad


def rotary_tables(places):
    frequencies = jnp.exp(
        jnp.arange(HD // 2, dtype=F32) * (-2.0 * math.log(ROPE_BASE) / HD)
    )
    angles = places.astype(F32)[:, None] * frequencies[None, :]
    return jnp.cos(angles), jnp.sin(angles)


def rotate(values, cosine, sine):
    front, back = values[..., : HD // 2], values[..., HD // 2 :]
    return jnp.concatenate(
        [front * cosine - back * sine, back * cosine + front * sine], axis=-1
    )


def in_order(first, mine, other):
    return jnp.where(first, mine, other), jnp.where(first, other, mine)


def on_device(
    hidden_in,
    segments,
    positions,
    out_grad,
    w_query,
    w_key,
    w_value,
    w_out,
    w_gate,
    w_up,
    w_down,
    norm_gains,
    head_gains,
):
    iy = lax.axis_index("y")
    izh = lax.axis_index("zh")
    ix = lax.axis_index("x")
    ic = lax.axis_index("core")
    izl = lax.axis_index("zl")
    ring = jnp.arange(4, dtype=jnp.int32)
    place = jnp.concatenate(
        [
            (((ring - iy) % 4)[:, None] * 2 + ((ring[:2] - izl) % 2)[None, :]).reshape(8),
            jnp.stack([ic, 1 - ic]).astype(jnp.int32),
        ]
    )

    def both_halves(half):
        return jnp.concatenate(in_order(izh == 0, half, swap(half, "zh")), axis=-1)

    def sum_half(rows):
        turned = rows.reshape(rows.shape[:-1] + (2, HALF))
        axis = turned.ndim - 2
        mine = lax.dynamic_index_in_dim(turned, izh, axis, False)
        other = lax.dynamic_index_in_dim(turned, 1 - izh, axis, False)
        return add(mine, swap(other.astype(LOW), "zh"))

    def gather_groups(v):
        pair = jnp.stack([v, swap(v, "zl")])
        return jnp.concatenate(gather_ring(pair, "y"), axis=0)

    def over_groups(blocks):
        blocks = blocks.reshape((4, 2) + blocks.shape[1:])
        pair = scatter_ring(list(blocks), "y").astype(LOW)
        return sum_half(add(pair[0], swap(pair[1], "zl")))

    groups = ("y", "zl", "core")
    out_rows = lax.all_to_all(w_out.reshape(16, 16, 36), groups, 0, 0, tiled=True)
    out_rows = both_halves(out_rows.transpose(1, 0, 2).reshape(16, HALF))
    gain_place = ((ix * 4 + iy) * 4 + izl * 2 + ic) * 9
    head_place = (iy * 4 + izl * 2 + ic) * 16
    gains = lax.dynamic_update_slice(
        jnp.zeros((4, D), LOW), norm_gains, (0, izh * HALF + gain_place)
    )
    heads = lax.dynamic_update_slice(jnp.zeros((2, HD), LOW), head_gains, (0, head_place))
    heads = jnp.where((izh == 0) & (ix == 0), heads, jnp.zeros((), LOW)).reshape(1, 2 * HD)
    misc = jnp.concatenate(
        [gains, jnp.pad(heads, ((0, 0), (0, D - 2 * HD))), jnp.zeros((3, D), LOW)], axis=0
    )
    misc = add(misc, swap(misc, "zh")).astype(LOW)
    misc = add(*gather_direct(misc, "x")).astype(LOW)
    pack = jnp.concatenate(
        [
            both_halves(jnp.concatenate([w_key.T, w_value.T, w_query.T], axis=0)),
            out_rows,
            jnp.pad(misc, ((0, 8), (0, 0))),
        ],
        axis=0,
    )
    pack = gather_groups(pack).reshape(1, 8, 5, 16, D)
    pair_part = jnp.concatenate([pack[:, :, :2], pack[:, :, 4:]], axis=2)
    key_weight, value_weight, misc = assemble(place, pair_part, swap(pair_part, "core"), 2)
    gain_rows = misc[:4]
    head_gain = misc[4, : 2 * HD].reshape(2, HD)
    head_part = jnp.stack(gather_ring(pack[0, :, 2:4], "x"))
    query_weight, out_weight = assemble(place, head_part, swap(head_part, "core"), 2)

    stream = hidden_in.astype(F32)
    scale_one = inverse_rms(stream)
    normed_one = (stream * scale_one * gain_rows[0]).astype(LOW)
    key_raw = dot_nt(normed_one, key_weight)
    value_low = dot_nt(normed_one, value_weight).astype(LOW)
    token_start = (izh * 4 + ix) * OWN
    own_positions = lax.dynamic_slice_in_dim(positions, token_start, OWN)
    own_segments = lax.dynamic_slice_in_dim(segments, token_start, OWN)
    cosine, sine = rotary_tables(own_positions)
    key_rot, key_back = jax.vjp(
        lambda raw, gain: rotate(raw * inverse_rms(raw) * gain, cosine, sine),
        key_raw,
        head_gain[1],
    )
    pair = jnp.concatenate([key_rot.astype(LOW), value_low], axis=1)
    pair = jnp.stack([pair, swap(pair, "zh")])
    pair = jnp.concatenate(gather_ring(pair, "x"), axis=0)
    pair = pair.reshape(LEN, 2 * HD)
    keys, values = pair[:, :HD], pair[:, HD:]
    key_start = jnp.stack(
        [((izh + b) % 2 * 4 + (ix + a) % 4) * OWN for a in range(4) for b in range(2)]
    )
    key_order = (key_start[:, None] + jnp.arange(OWN, dtype=jnp.int32)[None, :]).reshape(LEN)
    key_segments = jnp.concatenate(
        [lax.dynamic_slice_in_dim(segments, key_start[k], OWN) for k in range(8)]
    )

    query_raw = dot_nt(normed_one, query_weight).reshape(OWN, H, HD)
    query_norm, query_back = jax.vjp(
        lambda raw, gain: rotate(
            raw * inverse_rms(raw) * gain, cosine[:, None, :], sine[:, None, :]
        ),
        query_raw,
        head_gain[0],
    )
    query_rot = query_norm.astype(LOW).transpose(1, 0, 2).reshape(H * OWN, HD)
    query_order = token_start + jnp.arange(OWN, dtype=jnp.int32)
    allowed = (own_segments[:, None] == key_segments[None, :]) & (
        query_order[:, None] >= key_order[None, :]
    )
    scores = (dot_nt(query_rot, keys) * SCALE).reshape(H, OWN, LEN)
    scores = jnp.where(allowed[None], scores, MASKED)
    exponent = jnp.exp(scores - jnp.max(scores, axis=-1, keepdims=True))
    probs = (exponent / jnp.sum(exponent, axis=-1, keepdims=True)).reshape(H * OWN, LEN)
    probs_low = probs.astype(LOW)
    context = dot_nn(probs_low, values).astype(LOW)
    context = context.reshape(H, OWN, HD).transpose(1, 0, 2).reshape(OWN, H * HD)

    def pad_units(v):
        return jnp.pad(v, ((0, PADDED - UNITS), (0, 0)))

    down_rows = lax.all_to_all(w_down.reshape(16, UNITS, 36), groups, 0, 0, tiled=True)
    down_rows = down_rows.transpose(1, 0, 2).reshape(UNITS, HALF)
    wide_rows = both_halves(
        jnp.concatenate([pad_units(w_gate.T), pad_units(w_up.T), pad_units(down_rows)], axis=0)
    )
    units = 8 * PADDED
    wide_rows = gather_groups(wide_rows)
    gate_weight, up_weight, down_weight = (
        wide_rows[:, k * PADDED : (k + 1) * PADDED].reshape(units, D) for k in range(3)
    )

    def spread_tokens(v):
        mine = jnp.concatenate(gather_ring(v, "x"), axis=0)
        return jnp.concatenate([mine, swap(mine, "core")], axis=0)

    def sum_tokens(v):
        v = v.reshape(2, 4, OWN, D)
        mine = add(v[0], swap(v[1], "core")).astype(LOW)
        return scatter_ring([mine[0], mine[1], mine[2], mine[3]], "x")

    attn_raw = dot_nn(context, out_weight)
    scale_two = inverse_rms(attn_raw)
    middle = stream + attn_raw * scale_two * gain_rows[1]
    scale_three = inverse_rms(middle)
    normed_two = (middle * scale_three * gain_rows[2]).astype(LOW)
    wide_two = spread_tokens(normed_two)
    gate_raw = dot_nt(wide_two, gate_weight)
    up_raw = dot_nt(wide_two, up_weight)
    activated, gelu_back = jax.vjp(
        lambda gate, up: jax.nn.gelu(gate, approximate=True) * up, gate_raw, up_raw
    )
    hidden = activated.astype(LOW)
    down_raw = sum_tokens(dot_nn(hidden, down_weight).astype(LOW))
    scale_four = inverse_rms(down_raw)
    result = (middle + down_raw * scale_four * gain_rows[3]).astype(LOW)
    upstream = out_grad.astype(F32)
    down_grad, gain_four = norm_backward(upstream, down_raw, scale_four, gain_rows[3])
    down_wide = spread_tokens(down_grad.astype(LOW))
    hidden_grad = dot_nt(down_wide, down_weight)
    gate_grad, up_grad = gelu_back(hidden_grad)
    gate_low, up_low = gate_grad.astype(LOW), up_grad.astype(LOW)
    normed_two_grad = sum_tokens(
        (dot_nn(gate_low, gate_weight) + dot_nn(up_low, up_weight)).astype(LOW)
    )
    grad_wide = jnp.concatenate(
        [
            dot_tn(part, tokens).astype(LOW).reshape(8, PADDED, D)
            for part, tokens in ((gate_low, wide_two), (up_low, wide_two), (hidden, down_wide))
        ],
        axis=1,
    )
    grad_wide, normed_two_grad = lax.optimization_barrier((grad_wide, normed_two_grad))
    wide_rows = over_groups(grad_wide)
    gate_shard, up_shard = wide_rows[:UNITS].T, wide_rows[PADDED : PADDED + UNITS].T
    down_rows = wide_rows[2 * PADDED : 2 * PADDED + UNITS].astype(LOW)

    middle_part, gain_three = norm_backward(normed_two_grad, middle, scale_three, gain_rows[2])
    middle_grad = upstream + middle_part
    attn_grad, gain_two = norm_backward(middle_grad, attn_raw, scale_two, gain_rows[1])
    attn_low = attn_grad.astype(LOW)
    context_grad = dot_nt(attn_low, out_weight).astype(LOW)
    context_grad = context_grad.reshape(OWN, H, HD).transpose(1, 0, 2).reshape(H * OWN, HD)
    prob_grad = dot_nt(context_grad, values)
    centre = jnp.sum(probs * prob_grad, axis=-1, keepdims=True)
    score_low = (probs * (prob_grad - centre)).astype(LOW)
    key_part = dot_tn(score_low, query_rot) * SCALE
    value_part = dot_tn(probs_low, context_grad)
    pair_grad = jnp.concatenate([key_part, value_part], axis=1).astype(LOW)
    pair_grad = pair_grad.reshape(4, 2, OWN, 2 * HD)
    pair_grad = scatter_ring(list(pair_grad), "x")
    pair_grad = add(pair_grad[0], swap(pair_grad[1].astype(LOW), "zh"))
    query_grad = (dot_nn(score_low, keys) * SCALE).reshape(H, OWN, HD).transpose(1, 0, 2)
    query_raw_grad, query_gain = query_back(query_grad)
    query_low = query_raw_grad.reshape(OWN, H * HD).astype(LOW)
    key_raw_grad, key_gain = key_back(pair_grad[:, :HD])
    key_low = key_raw_grad.astype(LOW)
    value_grad_low = pair_grad[:, HD:].astype(LOW)
    normed_one_grad = (
        dot_nn(query_low, query_weight)
        + dot_nn(key_low, key_weight)
        + dot_nn(value_grad_low, value_weight)
    )
    stream_part, gain_one = norm_backward(normed_one_grad, stream, scale_one, gain_rows[0])
    input_grad = (middle_grad + stream_part).astype(LOW)

    mine, other = divide(
        place, [dot_tn(query_low, normed_one).astype(LOW), dot_tn(context, attn_low).astype(LOW)]
    )
    mine = add(mine, swap(other, "core")).astype(LOW)
    head_rows = over_groups(scatter_ring(list(mine), "x").astype(LOW))
    query_shard = head_rows[0].T
    down_rows = jnp.concatenate([down_rows, head_rows[1].astype(LOW)], axis=0)
    down_rows = down_rows.reshape(UNITS + 16, 16, 36).transpose(1, 0, 2)
    down_rows = lax.all_to_all(down_rows, groups, 0, 0, tiled=True).astype(F32)
    down_shard = down_rows[:, :UNITS].reshape(16 * UNITS, 36)
    out_shard = down_rows[:, UNITS:].reshape(HD, 36)

    gains_grad = jnp.stack([gain_one, gain_two, gain_three, gain_four])
    head_grad = jnp.concatenate([query_gain, key_gain]).reshape(1, 2 * HD)
    head_grad = jnp.pad(head_grad, ((0, 0), (0, HALF - 2 * HD)))
    misc = jnp.concatenate(
        [gains_grad, jnp.concatenate([head_grad, head_grad], axis=1), jnp.zeros((11, D), F32)],
        axis=0,
    )
    mine, other = divide(
        place,
        [dot_tn(key_low, normed_one).astype(LOW), dot_tn(value_grad_low, normed_one).astype(LOW)],
        misc.astype(LOW),
    )
    pair_rows = over_groups(add(mine[0], swap(other[0], "core")).astype(LOW)).astype(LOW)
    pair_rows = add(*gather_direct(pair_rows, "x"))
    key_shard, value_shard = pair_rows[0].T, pair_rows[1].T
    gains_shard = lax.dynamic_slice(pair_rows[2], (0, gain_place), (4, 9))
    head_shard = lax.dynamic_slice(
        pair_rows[2, 4, : 2 * HD].reshape(2, HD), (0, head_place), (2, 16)
    )
    return (
        result,
        input_grad,
        query_shard,
        key_shard,
        value_shard,
        out_shard,
        gate_shard,
        up_shard,
        down_shard,
        gains_shard,
        head_shard,
    )


def solution(mesh):
    split = Mesh(mesh.devices.reshape(4, 2, 2, 2, 4), ("y", "zl", "core", "zh", "x"))
    dp = ("y", "zl", "core")
    weights = (
        P("zh", ("x",) + dp),
        P("zh", dp),
        P("zh", dp),
        P("x", ("zh",) + dp),
        P("zh", ("x",) + dp),
        P("zh", ("x",) + dp),
        P("x", ("zh",) + dp),
        P(None, ("zh", "x") + dp),
        P(None, dp),
    )
    tokens = P(dp + ("zh", "x"), None)
    return jax.shard_map(
        on_device,
        mesh=split,
        in_specs=(tokens, P(dp), P(dp), tokens) + weights,
        out_specs=(tokens, tokens) + weights,
        check_vma=False,
    )
```

```python
import math

import jax
import jax.numpy as jnp
from jax import lax
from jax.experimental import pallas as pl
from jax.experimental.layout import Layout, with_layout_constraint
from jax.experimental.pallas import tpu as pltpu
from jax.sharding import Mesh, PartitionSpec as P

D = 1152
HALF = 576
H = 4
HD = 256
FF = 6912
LEN = 1216
OWN = 152
UNITS = 108
PADDED = 112
EPSILON = 1e-06
ROPE_BASE = 1000000.0
MASKED = -1e30
SCALE = HD ** (-0.5)
LOW = jnp.bfloat16
F32 = jnp.float32


def shift(v, axis, step):
    size = lax.axis_size(axis)
    return lax.ppermute(v, axis, [(i, (i + step) % size) for i in range(size)])


def swap(v, axis):
    return shift(v, axis, 1)


def gather_direct(v, axis):
    return [v, shift(v, axis, -1), shift(v, axis, -2), shift(v, axis, 1)]


def half_of(v):
    if v.ndim > 2:
        return v.shape[0] // 2
    return (v.shape[0] // 2 + 7) // 8 * 8


def gather_first(v, axis):
    return shift(v, axis, 1), shift(v, axis, -1)


def gather_second(v, first, axis):
    before, after = first
    half = half_of(v)
    opposite = jnp.concatenate(
        [shift(before[:half], axis, 1), shift(after[half:], axis, -1)], axis=0
    )
    return [v, after, opposite, before]


def gather_ring(v, axis):
    return gather_second(v, gather_first(v, axis), axis)


def add(*parts):
    total = parts[0].astype(F32)
    for part in parts[1:]:
        total = total + part.astype(F32)
    return total


def scatter_first(blocks, axis):
    opposite = blocks[2]
    half = half_of(opposite)
    return shift(opposite[:half], axis, 1), shift(opposite[half:], axis, -1)


def scatter_second(blocks, first, axis):
    own, after, _, before = blocks
    passed_up, passed_down = first
    half = half_of(own)
    up = jnp.concatenate([add(after[:half], passed_up).astype(LOW), after[half:]], axis=0)
    down = jnp.concatenate([before[:half], add(before[half:], passed_down).astype(LOW)], axis=0)
    return add(own, shift(up, axis, 1), shift(down, axis, -1))


def scatter_ring(blocks, axis):
    return scatter_second(blocks, scatter_first(blocks, axis), axis)


def row_major(v):
    return with_layout_constraint(v, Layout(major_to_minor=tuple(range(v.ndim))))


def whole(shape, dtype):
    return jax.ShapeDtypeStruct(shape, dtype)


VMEM = pl.BlockSpec(memory_space=pltpu.VMEM)
SMEM = pl.BlockSpec(memory_space=pltpu.SMEM)
BIG = pltpu.CompilerParams(vmem_limit_bytes=32 * 1024 * 1024)


def row_blocks(place_ref):
    for y in range(4):
        for zl in range(2):
            for side in range(2):
                row = y * 64 + zl * 32 + place_ref[8 + side] * 16
                yield side, place_ref[y * 2 + zl], pl.multiple_of(row, 16)


def assemble(place, mine, other, parts):
    heads, summed = mine.shape[0], mine.shape[2] > parts

    def kernel(place_ref, mine_ref, other_ref, *out_refs):
        for side, block, row in row_blocks(place_ref):
            ref = other_ref if side else mine_ref
            for h in range(heads):
                for part in range(parts):
                    out_refs[part][pl.ds(row + h * HD, 16), :] = ref[h, block, part]
        if summed:
            total = mine_ref[0, 0, parts].astype(F32) + other_ref[0, 0, parts].astype(F32)
            for k in range(1, 8):
                total = total + mine_ref[0, k, parts].astype(F32)
                total = total + other_ref[0, k, parts].astype(F32)
            out_refs[parts][...] = total

    shapes = [whole((heads * HD, D), LOW)] * parts + [whole((16, D), F32)] * summed
    return pl.pallas_call(
        kernel,
        out_shape=shapes,
        in_specs=[SMEM, VMEM, VMEM],
        out_specs=[VMEM] * len(shapes),
        compiler_params=BIG,
    )(place, mine, other)


def divide(place, grads, everywhere=None):
    heads, parts = grads[0].shape[0] // HD, len(grads)
    given = list(grads) + ([] if everywhere is None else [everywhere])

    def kernel(place_ref, *refs):
        grad_refs, (mine_ref, other_ref) = refs[: len(given)], refs[len(given) :]
        for side, block, row in row_blocks(place_ref):
            ref = other_ref if side else mine_ref
            for h in range(heads):
                for part in range(parts):
                    ref[h, block, part] = grad_refs[part][pl.ds(row + h * HD, 16), :]
            if everywhere is not None:
                ref[0, block, parts] = grad_refs[parts][...]

    return pl.pallas_call(
        kernel,
        out_shape=(whole((heads, 8, len(given), 16, D), LOW),) * 2,
        in_specs=[SMEM] + [VMEM] * len(given),
        out_specs=(VMEM, VMEM),
        compiler_params=BIG,
    )(place, *given)


def dot_nt(a, b):
    return lax.dot_general(a, b, (((1,), (1,)), ((), ())), preferred_element_type=F32)


def dot_nn(a, b):
    return lax.dot_general(a, b, (((1,), (0,)), ((), ())), preferred_element_type=F32)


def dot_tn(a, b):
    return lax.dot_general(a, b, (((0,), (0,)), ((), ())), preferred_element_type=F32)


def inverse_rms(values):
    return lax.rsqrt(jnp.mean(values * values, axis=-1, keepdims=True) + EPSILON)


def norm_backward(upstream, source, inverse, gain_row):
    weighted = upstream * gain_row
    inner = jnp.mean(weighted * source, axis=-1, keepdims=True)
    source_grad = inverse * weighted - source * (inverse * inverse * inverse) * inner
    gain_grad = jnp.sum(upstream * source * inverse, axis=0)
    return source_grad, gain_grad


def rotary_tables(places):
    frequencies = jnp.exp(
        jnp.arange(HD // 2, dtype=F32) * (-2.0 * math.log(ROPE_BASE) / HD)
    )
    angles = places.astype(F32)[:, None] * frequencies[None, :]
    return jnp.cos(angles), jnp.sin(angles)


def rotate(values, cosine, sine):
    front, back = values[..., : HD // 2], values[..., HD // 2 :]
    return jnp.concatenate(
        [front * cosine - back * sine, back * cosine + front * sine], axis=-1
    )


def in_order(first, mine, other):
    return jnp.where(first, mine, other), jnp.where(first, other, mine)


def on_device(
    hidden_in,
    segments,
    positions,
    out_grad,
    w_query,
    w_key,
    w_value,
    w_out,
    w_gate,
    w_up,
    w_down,
    norm_gains,
    head_gains,
):
    iy = lax.axis_index("y")
    izh = lax.axis_index("zh")
    ix = lax.axis_index("x")
    ic = lax.axis_index("core")
    izl = lax.axis_index("zl")
    ring = jnp.arange(4, dtype=jnp.int32)
    place = jnp.concatenate(
        [
            (((ring - iy) % 4)[:, None] * 2 + ((ring[:2] - izl) % 2)[None, :]).reshape(8),
            jnp.stack([ic, 1 - ic]).astype(jnp.int32),
        ]
    )

    def both_halves(half):
        return jnp.concatenate(in_order(izh == 0, half, swap(half, "zh")), axis=-1)

    def sum_half(rows):
        turned = rows.reshape(rows.shape[:-1] + (2, HALF))
        axis = turned.ndim - 2
        mine = lax.dynamic_index_in_dim(turned, izh, axis, False)
        other = lax.dynamic_index_in_dim(turned, 1 - izh, axis, False)
        return add(mine, swap(other.astype(LOW), "zh"))

    def over_groups(blocks):
        blocks = blocks.reshape((4, 2) + blocks.shape[1:])
        pair = scatter_ring(list(blocks), "y").astype(LOW)
        return sum_half(add(pair[0], swap(pair[1], "zl")))

    groups = ("y", "zl", "core")
    out_rows = lax.all_to_all(w_out.reshape(16, 16, 36), groups, 0, 0, tiled=True)
    out_rows = both_halves(out_rows.transpose(1, 0, 2).reshape(16, HALF))
    gain_place = ((ix * 4 + iy) * 4 + izl * 2 + ic) * 9
    head_place = (iy * 4 + izl * 2 + ic) * 16
    gains = lax.dynamic_update_slice(
        jnp.zeros((4, D), LOW), norm_gains, (0, izh * HALF + gain_place)
    )
    heads = lax.dynamic_update_slice(jnp.zeros((2, HD), LOW), head_gains, (0, head_place))
    heads = jnp.where((izh == 0) & (ix == 0), heads, jnp.zeros((), LOW)).reshape(1, 2 * HD)
    misc = jnp.concatenate(
        [gains, jnp.pad(heads, ((0, 0), (0, D - 2 * HD))), jnp.zeros((3, D), LOW)], axis=0
    )
    misc = add(misc, swap(misc, "zh")).astype(LOW)
    misc = add(*gather_direct(misc, "x")).astype(LOW)
    pack = jnp.concatenate(
        [
            both_halves(jnp.concatenate([w_key.T, w_value.T, w_query.T], axis=0)),
            out_rows,
            jnp.pad(misc, ((0, 8), (0, 0))),
        ],
        axis=0,
    )
    pack = jnp.stack([pack, swap(pack, "zl")])
    w_gate, w_up, w_down, pack = lax.optimization_barrier((w_gate, w_up, w_down, pack))
    pack = jnp.concatenate(gather_ring(pack, "y"), axis=0).reshape(1, 8, 5, 16, D)
    pair_part = jnp.concatenate([pack[:, :, :2], pack[:, :, 4:]], axis=2)
    key_weight, value_weight, misc = assemble(place, pair_part, swap(pair_part, "core"), 2)
    gain_rows = misc[:4]
    head_gain = misc[4, : 2 * HD].reshape(2, HD)
    head_part = pack[0, :, 2:4]
    head_first = gather_first(head_part, "x")

    stream = hidden_in.astype(F32)
    scale_one = inverse_rms(stream)
    normed_one = (stream * scale_one * gain_rows[0]).astype(LOW)
    key_raw = dot_nt(normed_one, key_weight)
    value_low = dot_nt(normed_one, value_weight).astype(LOW)
    token_start = (izh * 4 + ix) * OWN
    own_positions = lax.dynamic_slice_in_dim(positions, token_start, OWN)
    own_segments = lax.dynamic_slice_in_dim(segments, token_start, OWN)
    cosine, sine = rotary_tables(own_positions)
    key_rot, key_back = jax.vjp(
        lambda raw, gain: rotate(raw * inverse_rms(raw) * gain, cosine, sine),
        key_raw,
        head_gain[1],
    )
    pair = jnp.concatenate([key_rot.astype(LOW), value_low], axis=1)
    pair, head_first = lax.optimization_barrier((pair, head_first))
    pair = jnp.stack([pair, swap(pair, "zh")])
    pair = jnp.concatenate(gather_ring(pair, "x"), axis=0)
    pair = pair.reshape(LEN, 2 * HD)
    keys, values = pair[:, :HD], pair[:, HD:]
    key_start = jnp.stack(
        [((izh + b) % 2 * 4 + (ix + a) % 4) * OWN for a in range(4) for b in range(2)]
    )
    key_order = (key_start[:, None] + jnp.arange(OWN, dtype=jnp.int32)[None, :]).reshape(LEN)
    key_segments = jnp.concatenate(
        [lax.dynamic_slice_in_dim(segments, key_start[k], OWN) for k in range(8)]
    )

    head_part = jnp.stack(gather_second(head_part, head_first, "x"))
    query_weight, out_weight = assemble(place, head_part, swap(head_part, "core"), 2)
    query_raw = dot_nt(normed_one, query_weight).reshape(OWN, H, HD)
    query_norm, query_back = jax.vjp(
        lambda raw, gain: rotate(
            raw * inverse_rms(raw) * gain, cosine[:, None, :], sine[:, None, :]
        ),
        query_raw,
        head_gain[0],
    )
    query_rot = query_norm.astype(LOW).transpose(1, 0, 2).reshape(H * OWN, HD)
    query_order = token_start + jnp.arange(OWN, dtype=jnp.int32)
    allowed = (own_segments[:, None] == key_segments[None, :]) & (
        query_order[:, None] >= key_order[None, :]
    )
    scores = (dot_nt(query_rot, keys) * SCALE).reshape(H, OWN, LEN)
    scores = jnp.where(allowed[None], scores, MASKED)
    exponent = jnp.exp(scores - jnp.max(scores, axis=-1, keepdims=True))
    probs = (exponent / jnp.sum(exponent, axis=-1, keepdims=True)).reshape(H * OWN, LEN)
    probs_low = probs.astype(LOW)
    context = dot_nn(probs_low, values).astype(LOW)
    context = context.reshape(H, OWN, HD).transpose(1, 0, 2).reshape(OWN, H * HD)

    def pad_units(v):
        return jnp.pad(v, ((0, PADDED - UNITS), (0, 0)))

    down_rows = lax.all_to_all(w_down.reshape(16, UNITS, 36), groups, 0, 0, tiled=True)
    down_rows = down_rows.transpose(1, 0, 2).reshape(UNITS, HALF)
    wide_rows = row_major(
        jnp.concatenate([pad_units(w_gate.T), pad_units(w_up.T), pad_units(down_rows)], axis=0)
    )
    wide_rows = row_major(both_halves(wide_rows))
    wide_pair = jnp.stack([wide_rows, row_major(swap(wide_rows, "zl"))])
    wide_rows = [part[k] for part in gather_ring(wide_pair, "y") for k in range(2)]
    gate_weight, up_weight, down_weight = (
        jnp.concatenate([part[k * PADDED : (k + 1) * PADDED] for part in wide_rows], axis=0)
        for k in range(3)
    )

    def spread_tokens(v):
        mine = jnp.concatenate(gather_ring(v, "x"), axis=0)
        return jnp.concatenate([mine, swap(mine, "core")], axis=0)

    def sum_tokens(v):
        v = v.reshape(2, 4, OWN, D)
        mine = add(v[0], swap(v[1], "core")).astype(LOW)
        return scatter_ring([mine[0], mine[1], mine[2], mine[3]], "x")

    attn_raw = dot_nn(context, out_weight)
    scale_two = inverse_rms(attn_raw)
    middle = stream + attn_raw * scale_two * gain_rows[1]
    scale_three = inverse_rms(middle)
    normed_two = (middle * scale_three * gain_rows[2]).astype(LOW)
    wide_two = spread_tokens(normed_two)
    gate_raw = dot_nt(wide_two, gate_weight)
    up_raw = dot_nt(wide_two, up_weight)
    activated, gelu_back = jax.vjp(
        lambda gate, up: jax.nn.gelu(gate, approximate=True) * up, gate_raw, up_raw
    )
    hidden = activated.astype(LOW)
    down_raw = sum_tokens(dot_nn(hidden, down_weight).astype(LOW))
    scale_four = inverse_rms(down_raw)
    result = (middle + down_raw * scale_four * gain_rows[3]).astype(LOW)
    upstream = out_grad.astype(F32)
    down_grad, gain_four = norm_backward(upstream, down_raw, scale_four, gain_rows[3])
    down_wide = spread_tokens(down_grad.astype(LOW))
    hidden_grad = dot_nt(down_wide, down_weight)
    gate_grad, up_grad = gelu_back(hidden_grad)
    gate_low, up_low = gate_grad.astype(LOW), up_grad.astype(LOW)
    normed_two_grad = sum_tokens(
        (dot_nn(gate_low, gate_weight) + dot_nn(up_low, up_weight)).astype(LOW)
    )
    grad_wide = jnp.concatenate(
        [
            dot_tn(part, tokens).astype(LOW).reshape(8, PADDED, D)
            for part, tokens in ((gate_low, wide_two), (up_low, wide_two), (hidden, down_wide))
        ],
        axis=1,
    )
    grad_wide = list(grad_wide.reshape(4, 2, 3 * PADDED, D))
    wide_first = scatter_first(grad_wide, "y")
    wide_first, normed_two_grad = lax.optimization_barrier((wide_first, normed_two_grad))
    wide_pair = scatter_second(grad_wide, wide_first, "y").astype(LOW)

    middle_part, gain_three = norm_backward(normed_two_grad, middle, scale_three, gain_rows[2])
    middle_grad = upstream + middle_part
    attn_grad, gain_two = norm_backward(middle_grad, attn_raw, scale_two, gain_rows[1])
    attn_low = attn_grad.astype(LOW)
    context_grad = dot_nt(attn_low, out_weight).astype(LOW)
    context_grad = context_grad.reshape(OWN, H, HD).transpose(1, 0, 2).reshape(H * OWN, HD)
    prob_grad = dot_nt(context_grad, values)
    centre = jnp.sum(probs * prob_grad, axis=-1, keepdims=True)
    score_low = (probs * (prob_grad - centre)).astype(LOW)
    key_part = dot_tn(score_low, query_rot) * SCALE
    value_part = dot_tn(probs_low, context_grad)
    pair_grad = jnp.concatenate([key_part, value_part], axis=1).astype(LOW)
    pair_grad = pair_grad.reshape(4, 2, OWN, 2 * HD)
    pair_grad = list(pair_grad)
    pair_first = scatter_first(pair_grad, "x")
    query_grad = (dot_nn(score_low, keys) * SCALE).reshape(H, OWN, HD).transpose(1, 0, 2)
    query_raw_grad, query_gain = query_back(query_grad)
    query_low = query_raw_grad.reshape(OWN, H * HD).astype(LOW)
    mine, other = divide(
        place, [dot_tn(query_low, normed_one).astype(LOW), dot_tn(context, attn_low).astype(LOW)]
    )
    mine = add(mine, swap(other, "core")).astype(LOW)
    pair_first, mine = lax.optimization_barrier((pair_first, mine))
    pair_grad = scatter_second(pair_grad, pair_first, "x")
    head_rows = scatter_ring(list(mine), "x").astype(LOW)
    pair_grad = add(pair_grad[0], swap(pair_grad[1].astype(LOW), "zh"))
    pair_grad, wide_pair = lax.optimization_barrier((pair_grad, wide_pair))
    wide_rows = sum_half(add(wide_pair[0], swap(wide_pair[1], "zl")))
    gate_shard, up_shard = wide_rows[:UNITS].T, wide_rows[PADDED : PADDED + UNITS].T
    down_rows = wide_rows[2 * PADDED : 2 * PADDED + UNITS].astype(LOW)
    key_raw_grad, key_gain = key_back(pair_grad[:, :HD])
    key_low = key_raw_grad.astype(LOW)
    value_grad_low = pair_grad[:, HD:].astype(LOW)
    normed_one_grad = (
        dot_nn(query_low, query_weight)
        + dot_nn(key_low, key_weight)
        + dot_nn(value_grad_low, value_weight)
    )
    stream_part, gain_one = norm_backward(normed_one_grad, stream, scale_one, gain_rows[0])
    input_grad = (middle_grad + stream_part).astype(LOW)

    gains_grad = jnp.stack([gain_one, gain_two, gain_three, gain_four])
    head_grad = jnp.concatenate([query_gain, key_gain]).reshape(1, 2 * HD)
    head_grad = jnp.pad(head_grad, ((0, 0), (0, HALF - 2 * HD)))
    misc = jnp.concatenate(
        [gains_grad, jnp.concatenate([head_grad, head_grad], axis=1), jnp.zeros((11, D), F32)],
        axis=0,
    )
    mine, other = divide(
        place,
        [dot_tn(key_low, normed_one).astype(LOW), dot_tn(value_grad_low, normed_one).astype(LOW)],
        misc.astype(LOW),
    )
    mine = add(mine[0], swap(other[0], "core")).astype(LOW)
    rows = over_groups(jnp.concatenate([mine, head_rows], axis=1))
    query_shard = rows[3].T
    down_rows = jnp.concatenate([down_rows, rows[4].astype(LOW)], axis=0)
    down_rows = down_rows.reshape(UNITS + 16, 16, 36).transpose(1, 0, 2)
    down_rows = lax.all_to_all(down_rows, groups, 0, 0, tiled=True).astype(F32)
    down_shard = down_rows[:, :UNITS].reshape(16 * UNITS, 36)
    out_shard = down_rows[:, UNITS:].reshape(HD, 36)
    pair_rows = add(*gather_direct(rows[:3].astype(LOW), "x"))
    key_shard, value_shard = pair_rows[0].T, pair_rows[1].T
    gains_shard = lax.dynamic_slice(pair_rows[2], (0, gain_place), (4, 9))
    head_shard = lax.dynamic_slice(
        pair_rows[2, 4, : 2 * HD].reshape(2, HD), (0, head_place), (2, 16)
    )
    return (
        result,
        input_grad,
        query_shard,
        key_shard,
        value_shard,
        out_shard,
        gate_shard,
        up_shard,
        down_shard,
        gains_shard,
        head_shard,
    )


def solution(mesh):
    split = Mesh(mesh.devices.reshape(4, 2, 2, 2, 4), ("y", "zl", "core", "zh", "x"))
    dp = ("y", "zl", "core")
    weights = (
        P("zh", ("x",) + dp),
        P("zh", dp),
        P("zh", dp),
        P("x", ("zh",) + dp),
        P("zh", ("x",) + dp),
        P("zh", ("x",) + dp),
        P("x", ("zh",) + dp),
        P(None, ("zh", "x") + dp),
        P(None, dp),
    )
    tokens = P(dp + ("zh", "x"), None)
    return jax.shard_map(
        on_device,
        mesh=split,
        in_specs=(tokens, P(dp), P(dp), tokens) + weights,
        out_specs=(tokens, tokens) + weights,
        check_vma=False,
    )
```

```python
import math

import jax
import jax.numpy as jnp
from jax import lax
from jax.experimental import pallas as pl
from jax.experimental.layout import Layout, with_layout_constraint
from jax.experimental.pallas import tpu as pltpu
from jax.sharding import Mesh, PartitionSpec as P

D = 1152
HALF = 576
H = 4
HD = 256
FF = 6912
LEN = 1216
OWN = 152
UNITS = 108
PADDED = 112
EPSILON = 1e-06
ROPE_BASE = 1000000.0
MASKED = -1e30
SCALE = HD ** (-0.5)
LOW = jnp.bfloat16
F32 = jnp.float32


def shift(v, axis, step):
    size = lax.axis_size(axis)
    return lax.ppermute(v, axis, [(i, (i + step) % size) for i in range(size)])


def swap(v, axis):
    return shift(v, axis, 1)


def gather_direct(v, axis):
    return [v, shift(v, axis, -1), shift(v, axis, -2), shift(v, axis, 1)]


def half_of(v):
    if v.ndim > 2:
        return v.shape[0] // 2
    return (v.shape[0] // 2 + 7) // 8 * 8


def gather_first(v, axis):
    return shift(v, axis, 1), shift(v, axis, -1)


def gather_second(v, first, axis):
    before, after = first
    half = half_of(v)
    opposite = jnp.concatenate(
        [shift(before[:half], axis, 1), shift(after[half:], axis, -1)], axis=0
    )
    return [v, after, opposite, before]


def gather_ring(v, axis):
    return gather_second(v, gather_first(v, axis), axis)


def add(*parts):
    total = parts[0].astype(F32)
    for part in parts[1:]:
        total = total + part.astype(F32)
    return total


def scatter_first(blocks, axis):
    opposite = blocks[2]
    half = half_of(opposite)
    return shift(opposite[:half], axis, 1), shift(opposite[half:], axis, -1)


def scatter_parts(blocks, first, axis):
    own, after, _, before = blocks
    passed_up, passed_down = first
    half = half_of(own)
    up = jnp.concatenate([add(after[:half], passed_up).astype(LOW), after[half:]], axis=0)
    down = jnp.concatenate([before[:half], add(before[half:], passed_down).astype(LOW)], axis=0)
    return own, shift(up, axis, 1), shift(down, axis, -1)


def scatter_ring(blocks, axis):
    return add(*scatter_parts(blocks, scatter_first(blocks, axis), axis))


def row_major(v):
    return with_layout_constraint(v, Layout(major_to_minor=tuple(range(v.ndim))))


def whole(shape, dtype):
    return jax.ShapeDtypeStruct(shape, dtype)


VMEM = pl.BlockSpec(memory_space=pltpu.VMEM)
SMEM = pl.BlockSpec(memory_space=pltpu.SMEM)
BIG = pltpu.CompilerParams(vmem_limit_bytes=32 * 1024 * 1024)


def row_blocks(place_ref):
    for y in range(4):
        for zl in range(2):
            for side in range(2):
                row = y * 64 + zl * 32 + place_ref[8 + side] * 16
                yield side, place_ref[y * 2 + zl], pl.multiple_of(row, 16)


def assemble(place, mine, other, parts):
    heads, summed = mine.shape[0], mine.shape[2] > parts

    def kernel(place_ref, mine_ref, other_ref, *out_refs):
        for side, block, row in row_blocks(place_ref):
            ref = other_ref if side else mine_ref
            for h in range(heads):
                for part in range(parts):
                    out_refs[part][pl.ds(row + h * HD, 16), :] = ref[h, block, part]
        if summed:
            total = mine_ref[0, 0, parts].astype(F32) + other_ref[0, 0, parts].astype(F32)
            for k in range(1, 8):
                total = total + mine_ref[0, k, parts].astype(F32)
                total = total + other_ref[0, k, parts].astype(F32)
            out_refs[parts][...] = total

    shapes = [whole((heads * HD, D), LOW)] * parts + [whole((16, D), F32)] * summed
    return pl.pallas_call(
        kernel,
        out_shape=shapes,
        in_specs=[SMEM, VMEM, VMEM],
        out_specs=[VMEM] * len(shapes),
        compiler_params=BIG,
    )(place, mine, other)


def divide(place, grads, everywhere=None):
    heads, parts = grads[0].shape[0] // HD, len(grads)
    given = list(grads) + ([] if everywhere is None else [everywhere])

    def kernel(place_ref, *refs):
        grad_refs, (mine_ref, other_ref) = refs[: len(given)], refs[len(given) :]
        for side, block, row in row_blocks(place_ref):
            ref = other_ref if side else mine_ref
            for h in range(heads):
                for part in range(parts):
                    ref[h, block, part] = grad_refs[part][pl.ds(row + h * HD, 16), :]
            if everywhere is not None:
                ref[0, block, parts] = grad_refs[parts][...]

    return pl.pallas_call(
        kernel,
        out_shape=(whole((heads, 8, len(given), 16, D), LOW),) * 2,
        in_specs=[SMEM] + [VMEM] * len(given),
        out_specs=(VMEM, VMEM),
        compiler_params=BIG,
    )(place, *given)


def dot_nt(a, b):
    return lax.dot_general(a, b, (((1,), (1,)), ((), ())), preferred_element_type=F32)


def dot_nn(a, b):
    return lax.dot_general(a, b, (((1,), (0,)), ((), ())), preferred_element_type=F32)


def dot_tn(a, b):
    return lax.dot_general(a, b, (((0,), (0,)), ((), ())), preferred_element_type=F32)


def inverse_rms(values):
    return lax.rsqrt(jnp.mean(values * values, axis=-1, keepdims=True) + EPSILON)


def norm_backward(upstream, source, inverse, gain_row):
    weighted = upstream * gain_row
    inner = jnp.mean(weighted * source, axis=-1, keepdims=True)
    source_grad = inverse * weighted - source * (inverse * inverse * inverse) * inner
    gain_grad = jnp.sum(upstream * source * inverse, axis=0)
    return source_grad, gain_grad


def rotary_tables(places):
    frequencies = jnp.exp(
        jnp.arange(HD // 2, dtype=F32) * (-2.0 * math.log(ROPE_BASE) / HD)
    )
    angles = places.astype(F32)[:, None] * frequencies[None, :]
    return jnp.cos(angles), jnp.sin(angles)


def rotate(values, cosine, sine):
    front, back = values[..., : HD // 2], values[..., HD // 2 :]
    return jnp.concatenate(
        [front * cosine - back * sine, back * cosine + front * sine], axis=-1
    )


def in_order(first, mine, other):
    return jnp.where(first, mine, other), jnp.where(first, other, mine)


def on_device(
    hidden_in,
    segments,
    positions,
    out_grad,
    w_query,
    w_key,
    w_value,
    w_out,
    w_gate,
    w_up,
    w_down,
    norm_gains,
    head_gains,
):
    iy = lax.axis_index("y")
    izh = lax.axis_index("zh")
    ix = lax.axis_index("x")
    ic = lax.axis_index("core")
    izl = lax.axis_index("zl")
    ring = jnp.arange(4, dtype=jnp.int32)
    place = jnp.concatenate(
        [
            (((ring - iy) % 4)[:, None] * 2 + ((ring[:2] - izl) % 2)[None, :]).reshape(8),
            jnp.stack([ic, 1 - ic]).astype(jnp.int32),
        ]
    )

    def other_both(v):
        return lax.ppermute(v, ("zl", "zh"), [(i, 3 - i) for i in range(4)])

    def spread_z(v):
        near = jnp.concatenate(in_order(izh == 0, v, swap(v, "zh")), axis=1)
        far = jnp.concatenate(in_order(izh == 0, swap(v, "zl"), other_both(v)), axis=1)
        return row_major(jnp.stack([near, far]))

    def sum_z(v):
        near = in_order(izh == 0, v[0, ..., :HALF], v[0, ..., HALF:])
        far = in_order(izh == 0, v[1, ..., :HALF], v[1, ..., HALF:])
        return add(near[0], swap(near[1], "zh"), swap(far[0], "zl"), other_both(far[1]))

    groups = ("y", "zl", "core")
    down_rows = jnp.concatenate(
        [w_down.reshape(16, UNITS, 36), w_out.reshape(16, 16, 36)], axis=1
    )
    down_rows = lax.all_to_all(down_rows, groups, 0, 0, tiled=True)
    down_rows = down_rows.transpose(1, 0, 2).reshape(UNITS + 16, HALF)
    gain_place = ((ix * 4 + iy) * 4 + izl * 2 + ic) * 9
    head_place = (iy * 4 + izl * 2 + ic) * 16
    gains = lax.dynamic_update_slice(
        jnp.zeros((4, D), LOW), norm_gains, (0, izh * HALF + gain_place)
    )
    heads = lax.dynamic_update_slice(jnp.zeros((2, HD), LOW), head_gains, (0, head_place))
    heads = jnp.where((izh == 0) & (ix == 0), heads, jnp.zeros((), LOW)).reshape(1, 2 * HD)
    misc = jnp.concatenate(
        [gains, jnp.pad(heads, ((0, 0), (0, D - 2 * HD))), jnp.zeros((3, D), LOW)], axis=0
    )
    misc = add(*gather_direct(misc, "x")).astype(LOW)
    pack = spread_z(
        jnp.concatenate(
            [w_key.T, w_value.T, w_query.T, down_rows[UNITS:], misc[:, :HALF], misc[:, HALF:]],
            axis=0,
        )
    )
    w_gate, w_up, down_rows, pack = lax.optimization_barrier((w_gate, w_up, down_rows, pack))
    pack = jnp.concatenate(gather_ring(pack, "y"), axis=0).reshape(1, 8, 5, 16, D)
    pair_part = jnp.concatenate([pack[:, :, :2], pack[:, :, 4:]], axis=2)
    key_weight, value_weight, misc = assemble(place, pair_part, swap(pair_part, "core"), 2)
    misc = misc[:, :HALF] + misc[:, HALF:]
    misc = jnp.concatenate([misc[:8], misc[8:]], axis=1)
    gain_rows = misc[:4]
    head_gain = misc[4, : 2 * HD].reshape(2, HD)
    head_part = pack[0, :, 2:4]
    head_first = gather_first(head_part, "x")

    stream = hidden_in.astype(F32)
    scale_one = inverse_rms(stream)
    normed_one = (stream * scale_one * gain_rows[0]).astype(LOW)
    key_raw = dot_nt(normed_one, key_weight)
    value_low = dot_nt(normed_one, value_weight).astype(LOW)
    token_start = (izh * 4 + ix) * OWN
    own_positions = lax.dynamic_slice_in_dim(positions, token_start, OWN)
    own_segments = lax.dynamic_slice_in_dim(segments, token_start, OWN)
    cosine, sine = rotary_tables(own_positions)
    key_rot, key_back = jax.vjp(
        lambda raw, gain: rotate(raw * inverse_rms(raw) * gain, cosine, sine),
        key_raw,
        head_gain[1],
    )
    pair = jnp.concatenate([key_rot.astype(LOW), value_low], axis=1)
    pair_far, head_first = lax.optimization_barrier((swap(pair, "zh"), head_first))
    pair = jnp.stack([pair, pair_far])
    pair = jnp.concatenate(gather_ring(pair, "x"), axis=0)
    pair = pair.reshape(LEN, 2 * HD)
    keys, values = pair[:, :HD], pair[:, HD:]
    key_start = jnp.stack(
        [((izh + b) % 2 * 4 + (ix + a) % 4) * OWN for a in range(4) for b in range(2)]
    )
    key_order = (key_start[:, None] + jnp.arange(OWN, dtype=jnp.int32)[None, :]).reshape(LEN)
    key_segments = jnp.concatenate(
        [lax.dynamic_slice_in_dim(segments, key_start[k], OWN) for k in range(8)]
    )

    head_part = jnp.stack(gather_second(head_part, head_first, "x"))
    query_weight, out_weight = assemble(place, head_part, swap(head_part, "core"), 2)
    query_raw = jnp.concatenate(
        [dot_nt(normed_one, query_weight[h * HD : (h + 1) * HD]) for h in range(H)], axis=0
    )
    cosine_heads, sine_heads = jnp.tile(cosine, (H, 1)), jnp.tile(sine, (H, 1))
    query_norm, query_back = jax.vjp(
        lambda raw, gain: rotate(raw * inverse_rms(raw) * gain, cosine_heads, sine_heads),
        query_raw,
        head_gain[0],
    )
    query_rot = query_norm.astype(LOW)
    query_order = token_start + jnp.arange(OWN, dtype=jnp.int32)
    allowed = (own_segments[:, None] == key_segments[None, :]) & (
        query_order[:, None] >= key_order[None, :]
    )
    scores = (dot_nt(query_rot, keys) * SCALE).reshape(H, OWN, LEN)
    scores = jnp.where(allowed[None], scores, MASKED)
    exponent = jnp.exp(scores - jnp.max(scores, axis=-1, keepdims=True))
    probs = (exponent / jnp.sum(exponent, axis=-1, keepdims=True)).reshape(H * OWN, LEN)
    probs_low = probs.astype(LOW)
    context = dot_nn(probs_low, values).astype(LOW)
    context = jnp.concatenate([context[h * OWN : (h + 1) * OWN] for h in range(H)], axis=1)

    def pad_units(v):
        return jnp.pad(v, ((0, PADDED - UNITS), (0, 0)))

    wide_rows = row_major(
        jnp.concatenate(
            [pad_units(w_gate.T), pad_units(w_up.T), pad_units(down_rows[:UNITS])], axis=0
        )
    )
    wide_pair = spread_z(wide_rows)
    wide_first = gather_first(wide_pair, "y")
    wide_first, context = lax.optimization_barrier((wide_first, context))
    wide_rows = [part[k] for part in gather_second(wide_pair, wide_first, "y") for k in range(2)]
    gate_weight, up_weight, down_weight = (
        jnp.concatenate([part[k * PADDED : (k + 1) * PADDED] for part in wide_rows], axis=0)
        for k in range(3)
    )

    def spread_tokens(v):
        mine = jnp.concatenate(gather_ring(v, "x"), axis=0)
        return jnp.concatenate([mine, swap(mine, "core")], axis=0)

    def sum_tokens(v):
        v = v.reshape(2, 4, OWN, D)
        mine = add(v[0], swap(v[1], "core")).astype(LOW)
        return scatter_ring([mine[0], mine[1], mine[2], mine[3]], "x")

    attn_raw = dot_nn(context, out_weight)
    scale_two = inverse_rms(attn_raw)
    middle = stream + attn_raw * scale_two * gain_rows[1]
    scale_three = inverse_rms(middle)
    normed_two = (middle * scale_three * gain_rows[2]).astype(LOW)
    wide_two = spread_tokens(normed_two)
    gate_raw = dot_nt(wide_two, gate_weight)
    up_raw = dot_nt(wide_two, up_weight)
    activated, gelu_back = jax.vjp(
        lambda gate, up: jax.nn.gelu(gate, approximate=True) * up, gate_raw, up_raw
    )
    hidden = activated.astype(LOW)
    down_raw = sum_tokens(dot_nn(hidden, down_weight).astype(LOW))
    scale_four = inverse_rms(down_raw)
    result = (middle + down_raw * scale_four * gain_rows[3]).astype(LOW)
    upstream = out_grad.astype(F32)
    down_grad, gain_four = norm_backward(upstream, down_raw, scale_four, gain_rows[3])
    down_wide = spread_tokens(down_grad.astype(LOW))
    hidden_grad = dot_nt(down_wide, down_weight)
    gate_grad, up_grad = gelu_back(hidden_grad)
    gate_low, up_low = gate_grad.astype(LOW), up_grad.astype(LOW)
    normed_two_grad = sum_tokens(
        (dot_nn(gate_low, gate_weight) + dot_nn(up_low, up_weight)).astype(LOW)
    )
    grad_wide = jnp.concatenate(
        [
            dot_tn(part, tokens).astype(LOW).reshape(8, PADDED, D)
            for part, tokens in ((gate_low, wide_two), (up_low, wide_two), (hidden, down_wide))
        ],
        axis=1,
    )
    grad_wide = list(grad_wide.reshape(4, 2, 3 * PADDED, D))
    wide_first = scatter_first(grad_wide, "y")

    middle_part, gain_three = norm_backward(normed_two_grad, middle, scale_three, gain_rows[2])
    middle_grad = upstream + middle_part
    attn_grad, gain_two = norm_backward(middle_grad, attn_raw, scale_two, gain_rows[1])
    attn_low = attn_grad.astype(LOW)
    context_grad = dot_nt(attn_low, out_weight).astype(LOW)
    context_grad = jnp.concatenate(
        [context_grad[:, h * HD : (h + 1) * HD] for h in range(H)], axis=0
    )
    prob_grad = dot_nt(context_grad, values)
    centre = jnp.sum(probs * prob_grad, axis=-1, keepdims=True)
    score_low = (probs * (prob_grad - centre)).astype(LOW)
    wide_first, score_low = lax.optimization_barrier((wide_first, score_low))
    wide_parts = scatter_parts(grad_wide, wide_first, "y")
    key_part = dot_tn(score_low, query_rot) * SCALE
    value_part = dot_tn(probs_low, context_grad)
    pair_grad = jnp.concatenate([key_part, value_part], axis=1).astype(LOW)
    pair_grad = pair_grad.reshape(4, 2, OWN, 2 * HD)
    pair_grad = list(pair_grad)
    pair_first = scatter_first(pair_grad, "x")
    query_grad = dot_nn(score_low, keys) * SCALE
    query_raw_grad, query_gain = query_back(query_grad)
    query_low = query_raw_grad.astype(LOW)
    query_low = jnp.concatenate([query_low[h * OWN : (h + 1) * OWN] for h in range(H)], axis=1)
    mine, other = divide(
        place, [dot_tn(query_low, normed_one).astype(LOW), dot_tn(context, attn_low).astype(LOW)]
    )
    mine = add(mine, swap(other, "core")).astype(LOW)
    pair_first, mine = lax.optimization_barrier((pair_first, mine))
    pair_grad = add(*scatter_parts(pair_grad, pair_first, "x"))
    head_rows = scatter_ring(list(mine), "x").astype(LOW)
    pair_grad = add(pair_grad[0], swap(pair_grad[1].astype(LOW), "zh"))
    pair_grad, wide_parts = lax.optimization_barrier((pair_grad, wide_parts))
    wide_rows = sum_z(add(*wide_parts).astype(LOW))
    gate_shard, up_shard = wide_rows[:UNITS].T, wide_rows[PADDED : PADDED + UNITS].T
    down_rows = wide_rows[2 * PADDED : 2 * PADDED + UNITS].astype(LOW)
    key_raw_grad, key_gain = key_back(pair_grad[:, :HD])
    key_low = key_raw_grad.astype(LOW)
    value_grad_low = pair_grad[:, HD:].astype(LOW)
    normed_one_grad = (
        dot_nn(query_low, query_weight)
        + dot_nn(key_low, key_weight)
        + dot_nn(value_grad_low, value_weight)
    )
    stream_part, gain_one = norm_backward(normed_one_grad, stream, scale_one, gain_rows[0])
    input_grad = (middle_grad + stream_part).astype(LOW)

    gains_grad = jnp.stack([gain_one, gain_two, gain_three, gain_four])
    head_grad = jnp.concatenate([query_gain, key_gain]).reshape(1, 2 * HD)
    head_grad = jnp.pad(head_grad, ((0, 0), (0, HALF - 2 * HD)))
    misc = jnp.concatenate(
        [gains_grad, jnp.concatenate([head_grad, head_grad], axis=1), jnp.zeros((11, D), F32)],
        axis=0,
    )
    mine, other = divide(
        place,
        [dot_tn(key_low, normed_one).astype(LOW), dot_tn(value_grad_low, normed_one).astype(LOW)],
        misc.astype(LOW),
    )
    mine = add(mine[0], swap(other[0], "core")).astype(LOW)
    rows = jnp.concatenate([mine, head_rows], axis=1).reshape(4, 2, 5, 16, D)
    rows = sum_z(scatter_ring(list(rows), "y").astype(LOW))
    query_shard = rows[3].T
    down_rows = jnp.concatenate([down_rows, rows[4].astype(LOW)], axis=0)
    down_rows = down_rows.reshape(UNITS + 16, 16, 36).transpose(1, 0, 2)
    down_rows = lax.all_to_all(down_rows, groups, 0, 0, tiled=True).astype(F32)
    down_shard = down_rows[:, :UNITS].reshape(16 * UNITS, 36)
    out_shard = down_rows[:, UNITS:].reshape(HD, 36)
    pair_rows = add(*gather_direct(rows[:3].astype(LOW), "x"))
    key_shard, value_shard = pair_rows[0].T, pair_rows[1].T
    gains_shard = lax.dynamic_slice(pair_rows[2], (0, gain_place), (4, 9))
    head_shard = lax.dynamic_slice(
        pair_rows[2, 4, : 2 * HD].reshape(2, HD), (0, head_place), (2, 16)
    )
    return (
        result,
        input_grad,
        query_shard,
        key_shard,
        value_shard,
        out_shard,
        gate_shard,
        up_shard,
        down_shard,
        gains_shard,
        head_shard,
    )


def solution(mesh):
    split = Mesh(mesh.devices.reshape(4, 2, 2, 2, 4), ("y", "zl", "core", "zh", "x"))
    dp = ("y", "zl", "core")
    weights = (
        P("zh", ("x",) + dp),
        P("zh", dp),
        P("zh", dp),
        P("x", ("zh",) + dp),
        P("zh", ("x",) + dp),
        P("zh", ("x",) + dp),
        P("x", ("zh",) + dp),
        P(None, ("zh", "x") + dp),
        P(None, dp),
    )
    tokens = P(dp + ("zh", "x"), None)
    return jax.shard_map(
        on_device,
        mesh=split,
        in_specs=(tokens, P(dp), P(dp), tokens) + weights,
        out_specs=(tokens, tokens) + weights,
        check_vma=False,
    )
```

```python
import math

import jax
import jax.numpy as jnp
from jax import lax
from jax.experimental import pallas as pl
from jax.experimental.layout import Layout, with_layout_constraint
from jax.experimental.pallas import tpu as pltpu
from jax.sharding import Mesh, PartitionSpec as P

D = 1152
HALF = 576
H = 4
HD = 256
FF = 6912
LEN = 1216
OWN = 152
UNITS = 108
PADDED = 112
EPSILON = 1e-06
ROPE_BASE = 1000000.0
MASKED = -1e30
SCALE = HD ** (-0.5)
LOW = jnp.bfloat16
F32 = jnp.float32


def shift(v, axis, step):
    size = lax.axis_size(axis)
    return lax.ppermute(v, axis, [(i, (i + step) % size) for i in range(size)])


def swap(v, axis):
    return shift(v, axis, 1)


def gather_direct(v, axis):
    return [v, shift(v, axis, -1), shift(v, axis, -2), shift(v, axis, 1)]


def shift_z(v, step):
    own = [(z % 2) * 2 + z // 2 for z in range(4)]
    return lax.ppermute(v, ("zl", "zh"), [(own[z], own[(z + step) % 4]) for z in range(4)])


def half_of(v):
    if v.ndim > 2:
        return v.shape[0] // 2
    return (v.shape[0] // 2 + 7) // 8 * 8


def gather_first(v, axis):
    return shift(v, axis, 1), shift(v, axis, -1)


def gather_second(v, first, axis):
    before, after = first
    half = half_of(v)
    opposite = jnp.concatenate(
        [shift(before[:half], axis, 1), shift(after[half:], axis, -1)], axis=0
    )
    return [v, after, opposite, before]


def gather_ring(v, axis):
    return gather_second(v, gather_first(v, axis), axis)


def add(*parts):
    total = parts[0].astype(F32)
    for part in parts[1:]:
        total = total + part.astype(F32)
    return total


def scatter_first(blocks, axis):
    opposite = blocks[2]
    half = half_of(opposite)
    return shift(opposite[:half], axis, 1), shift(opposite[half:], axis, -1)


def scatter_parts(blocks, first, axis):
    own, after, _, before = blocks
    passed_up, passed_down = first
    half = half_of(own)
    up = jnp.concatenate([add(after[:half], passed_up).astype(LOW), after[half:]], axis=0)
    down = jnp.concatenate([before[:half], add(before[half:], passed_down).astype(LOW)], axis=0)
    return own, shift(up, axis, 1), shift(down, axis, -1)


def scatter_ring(blocks, axis):
    return add(*scatter_parts(blocks, scatter_first(blocks, axis), axis))


def row_major(v):
    return with_layout_constraint(v, Layout(major_to_minor=tuple(range(v.ndim))))


def whole(shape, dtype):
    return jax.ShapeDtypeStruct(shape, dtype)


VMEM = pl.BlockSpec(memory_space=pltpu.VMEM)
SMEM = pl.BlockSpec(memory_space=pltpu.SMEM)
BIG = pltpu.CompilerParams(vmem_limit_bytes=32 * 1024 * 1024)


def row_blocks(place_ref):
    for y in range(4):
        for zl in range(2):
            for side in range(2):
                row = y * 64 + zl * 32 + place_ref[8 + side] * 16
                yield side, place_ref[y * 2 + zl], pl.multiple_of(row, 16)


def assemble(place, mine, other, parts):
    heads, summed = mine.shape[0], mine.shape[2] > parts

    def kernel(place_ref, mine_ref, other_ref, *out_refs):
        for side, block, row in row_blocks(place_ref):
            ref = other_ref if side else mine_ref
            for h in range(heads):
                for part in range(parts):
                    out_refs[part][pl.ds(row + h * HD, 16), :] = ref[h, block, part]
        if summed:
            total = mine_ref[0, 0, parts].astype(F32) + other_ref[0, 0, parts].astype(F32)
            for k in range(1, 8):
                total = total + mine_ref[0, k, parts].astype(F32)
                total = total + other_ref[0, k, parts].astype(F32)
            out_refs[parts][...] = total

    shapes = [whole((heads * HD, D), LOW)] * parts + [whole((16, D), F32)] * summed
    return pl.pallas_call(
        kernel,
        out_shape=shapes,
        in_specs=[SMEM, VMEM, VMEM],
        out_specs=[VMEM] * len(shapes),
        compiler_params=BIG,
    )(place, mine, other)


def divide(place, grads, everywhere=None):
    heads, parts = grads[0].shape[0] // HD, len(grads)
    given = list(grads) + ([] if everywhere is None else [everywhere])

    def kernel(place_ref, *refs):
        grad_refs, (mine_ref, other_ref) = refs[: len(given)], refs[len(given) :]
        for side, block, row in row_blocks(place_ref):
            ref = other_ref if side else mine_ref
            for h in range(heads):
                for part in range(parts):
                    ref[h, block, part] = grad_refs[part][pl.ds(row + h * HD, 16), :]
            if everywhere is not None:
                ref[0, block, parts] = grad_refs[parts][...]

    return pl.pallas_call(
        kernel,
        out_shape=(whole((heads, 8, len(given), 16, D), LOW),) * 2,
        in_specs=[SMEM] + [VMEM] * len(given),
        out_specs=(VMEM, VMEM),
        compiler_params=BIG,
    )(place, *given)


def dot_nt(a, b):
    return lax.dot_general(a, b, (((1,), (1,)), ((), ())), preferred_element_type=F32)


def dot_nn(a, b):
    return lax.dot_general(a, b, (((1,), (0,)), ((), ())), preferred_element_type=F32)


def dot_tn(a, b):
    return lax.dot_general(a, b, (((0,), (0,)), ((), ())), preferred_element_type=F32)


def inverse_rms(values):
    return lax.rsqrt(jnp.mean(values * values, axis=-1, keepdims=True) + EPSILON)


def norm_backward(upstream, source, inverse, gain_row):
    weighted = upstream * gain_row
    inner = jnp.mean(weighted * source, axis=-1, keepdims=True)
    source_grad = inverse * weighted - source * (inverse * inverse * inverse) * inner
    gain_grad = jnp.sum(upstream * source * inverse, axis=0)
    return source_grad, gain_grad


def rotary_tables(places):
    frequencies = jnp.exp(
        jnp.arange(HD // 2, dtype=F32) * (-2.0 * math.log(ROPE_BASE) / HD)
    )
    angles = places.astype(F32)[:, None] * frequencies[None, :]
    return jnp.cos(angles), jnp.sin(angles)


def rotate(values, cosine, sine):
    front, back = values[..., : HD // 2], values[..., HD // 2 :]
    return jnp.concatenate(
        [front * cosine - back * sine, back * cosine + front * sine], axis=-1
    )


def in_order(first, mine, other):
    return jnp.where(first, mine, other), jnp.where(first, other, mine)


def on_device(
    hidden_in,
    segments,
    positions,
    out_grad,
    w_query,
    w_key,
    w_value,
    w_out,
    w_gate,
    w_up,
    w_down,
    norm_gains,
    head_gains,
):
    iy = lax.axis_index("y")
    izh = lax.axis_index("zh")
    ix = lax.axis_index("x")
    ic = lax.axis_index("core")
    izl = lax.axis_index("zl")
    ring = jnp.arange(4, dtype=jnp.int32)
    place = jnp.concatenate(
        [
            (((ring - iy) % 4)[:, None] * 2 + ((ring[:2] - izl) % 2)[None, :]).reshape(8),
            jnp.stack([ic, 1 - ic]).astype(jnp.int32),
        ]
    )

    def other_both(v):
        return lax.ppermute(v, ("zl", "zh"), [(i, 3 - i) for i in range(4)])

    def spread_z(v):
        near = jnp.concatenate(in_order(izh == 0, v, swap(v, "zh")), axis=1)
        far = jnp.concatenate(in_order(izh == 0, swap(v, "zl"), other_both(v)), axis=1)
        return row_major(jnp.stack([near, far]))

    def ring_z_first(v):
        return shift_z(v, 1), shift_z(v, -1)

    def ring_z_second(first):
        before, after = first
        half = half_of(before)
        return shift_z(before[:half], 1), shift_z(after[half:], -1)

    def ring_z_last(v, first, second):
        before, after = first
        opposite = jnp.concatenate(second, axis=0)
        even = izl == 0
        near_z, far_z = jnp.where(even, after, before), jnp.where(even, before, after)
        near = jnp.concatenate(in_order(izh == 0, v, opposite), axis=1)
        far = jnp.concatenate(in_order(izh == 0, near_z, far_z), axis=1)
        return row_major(jnp.stack([near, far]))

    def sum_z(v):
        near = in_order(izh == 0, v[0, ..., :HALF], v[0, ..., HALF:])
        far = in_order(izh == 0, v[1, ..., :HALF], v[1, ..., HALF:])
        return add(near[0], swap(near[1], "zh"), swap(far[0], "zl"), other_both(far[1]))

    groups = ("y", "zl", "core")
    down_rows = jnp.concatenate(
        [w_down.reshape(16, UNITS, 36), w_out.reshape(16, 16, 36)], axis=1
    )
    down_rows, norm_gains = lax.optimization_barrier((down_rows, norm_gains))
    down_rows = lax.all_to_all(down_rows, groups, 0, 0, tiled=True)
    down_rows = down_rows.transpose(1, 0, 2).reshape(UNITS + 16, HALF)
    gain_place = ((ix * 4 + iy) * 4 + izl * 2 + ic) * 9
    head_place = (iy * 4 + izl * 2 + ic) * 16
    gains = lax.dynamic_update_slice(
        jnp.zeros((4, D), LOW), norm_gains, (0, izh * HALF + gain_place)
    )
    heads = lax.dynamic_update_slice(jnp.zeros((2, HD), LOW), head_gains, (0, head_place))
    heads = jnp.where((izh == 0) & (ix == 0), heads, jnp.zeros((), LOW)).reshape(1, 2 * HD)
    misc = jnp.concatenate(
        [gains, jnp.pad(heads, ((0, 0), (0, D - 2 * HD))), jnp.zeros((3, D), LOW)], axis=0
    )
    misc = add(*gather_direct(misc, "x")).astype(LOW)
    pack = spread_z(
        jnp.concatenate(
            [w_key.T, w_value.T, w_query.T, down_rows[UNITS:], misc[:, :HALF], misc[:, HALF:]],
            axis=0,
        )
    )
    w_gate, w_up, down_rows, pack = lax.optimization_barrier((w_gate, w_up, down_rows, pack))
    def pad_units(v):
        return jnp.pad(v, ((0, PADDED - UNITS), (0, 0)))

    wide_rows = row_major(
        jnp.concatenate(
            [pad_units(w_gate.T), pad_units(w_up.T), pad_units(down_rows[:UNITS])], axis=0
        )
    )
    wide_z = ring_z_first(wide_rows)
    pack_first = gather_first(pack, "y")
    pack_first, wide_z = lax.optimization_barrier((pack_first, wide_z))
    wide_second = ring_z_second(wide_z)
    pack = jnp.concatenate(gather_second(pack, pack_first, "y"), axis=0).reshape(1, 8, 5, 16, D)
    pair_part = jnp.concatenate([pack[:, :, :2], pack[:, :, 4:]], axis=2)
    key_weight, value_weight, misc = assemble(place, pair_part, swap(pair_part, "core"), 2)
    misc = misc[:, :HALF] + misc[:, HALF:]
    misc = jnp.concatenate([misc[:8], misc[8:]], axis=1)
    gain_rows = misc[:4]
    head_gain = misc[4, : 2 * HD].reshape(2, HD)
    head_part = pack[0, :, 2:4]
    head_first = gather_first(head_part, "x")

    stream = hidden_in.astype(F32)
    scale_one = inverse_rms(stream)
    normed_one = (stream * scale_one * gain_rows[0]).astype(LOW)
    key_raw = dot_nt(normed_one, key_weight)
    value_low = dot_nt(normed_one, value_weight).astype(LOW)
    token_start = (izh * 4 + ix) * OWN
    own_positions = lax.dynamic_slice_in_dim(positions, token_start, OWN)
    own_segments = lax.dynamic_slice_in_dim(segments, token_start, OWN)
    cosine, sine = rotary_tables(own_positions)
    key_rot, key_back = jax.vjp(
        lambda raw, gain: rotate(raw * inverse_rms(raw) * gain, cosine, sine),
        key_raw,
        head_gain[1],
    )
    pair = jnp.concatenate([key_rot.astype(LOW), value_low], axis=1)
    pair_far, head_first, wide_second = lax.optimization_barrier(
        (swap(pair, "zh"), head_first, wide_second)
    )
    wide_pair = ring_z_last(wide_rows, wide_z, wide_second)
    pair = jnp.stack([pair, pair_far])
    pair_first = gather_first(pair, "x")
    head_part = jnp.stack(gather_second(head_part, head_first, "x"))
    pair_first, head_part = lax.optimization_barrier((pair_first, head_part))
    pair = jnp.concatenate(gather_second(pair, pair_first, "x"), axis=0)
    pair = pair.reshape(LEN, 2 * HD)
    keys, values = pair[:, :HD], pair[:, HD:]
    key_start = jnp.stack(
        [((izh + b) % 2 * 4 + (ix + a) % 4) * OWN for a in range(4) for b in range(2)]
    )
    key_order = (key_start[:, None] + jnp.arange(OWN, dtype=jnp.int32)[None, :]).reshape(LEN)
    key_segments = jnp.concatenate(
        [lax.dynamic_slice_in_dim(segments, key_start[k], OWN) for k in range(8)]
    )

    query_weight, out_weight = assemble(place, head_part, swap(head_part, "core"), 2)
    query_raw = jnp.concatenate(
        [dot_nt(normed_one, query_weight[h * HD : (h + 1) * HD]) for h in range(H)], axis=0
    )
    cosine_heads, sine_heads = jnp.tile(cosine, (H, 1)), jnp.tile(sine, (H, 1))
    query_norm, query_back = jax.vjp(
        lambda raw, gain: rotate(raw * inverse_rms(raw) * gain, cosine_heads, sine_heads),
        query_raw,
        head_gain[0],
    )
    query_rot = query_norm.astype(LOW)
    query_order = token_start + jnp.arange(OWN, dtype=jnp.int32)
    allowed = (own_segments[:, None] == key_segments[None, :]) & (
        query_order[:, None] >= key_order[None, :]
    )
    scores = (dot_nt(query_rot, keys) * SCALE).reshape(H, OWN, LEN)
    scores = jnp.where(allowed[None], scores, MASKED)
    exponent = jnp.exp(scores - jnp.max(scores, axis=-1, keepdims=True))
    probs = (exponent / jnp.sum(exponent, axis=-1, keepdims=True)).reshape(H * OWN, LEN)
    probs_low = probs.astype(LOW)
    context = dot_nn(probs_low, values).astype(LOW)
    context = jnp.concatenate([context[h * OWN : (h + 1) * OWN] for h in range(H)], axis=1)

    units = 8 * PADDED
    wide_first = gather_first(wide_pair, "y")
    wide_first, context = lax.optimization_barrier((wide_first, context))
    wide_rows = [part[k] for part in gather_second(wide_pair, wide_first, "y") for k in range(2)]
    gate_weight, up_weight, down_weight = (
        jnp.concatenate([part[k * PADDED : (k + 1) * PADDED] for part in wide_rows], axis=0)
        for k in range(3)
    )

    def spread_tokens(v):
        mine = jnp.concatenate(gather_ring(v, "x"), axis=0)
        return jnp.concatenate([mine, swap(mine, "core")], axis=0)

    def sum_first(v):
        v = v.reshape(2, 4, OWN, D)
        mine = list(add(v[0], swap(v[1], "core")).astype(LOW))
        return mine, scatter_first(mine, "x")

    def sum_second(mine, first):
        return add(*scatter_parts(mine, first, "x"))

    attn_raw = dot_nn(context, out_weight)
    scale_two = inverse_rms(attn_raw)
    middle = stream + attn_raw * scale_two * gain_rows[1]
    scale_three = inverse_rms(middle)
    normed_two = (middle * scale_three * gain_rows[2]).astype(LOW)
    wide_two = spread_tokens(normed_two)
    gate_raw = dot_nt(wide_two, gate_weight)
    up_raw = dot_nt(wide_two, up_weight)
    activated, gelu_back = jax.vjp(
        lambda gate, up: jax.nn.gelu(gate, approximate=True) * up, gate_raw, up_raw
    )
    hidden = activated.astype(LOW)
    down_raw = sum_second(*sum_first(dot_nn(hidden, down_weight).astype(LOW)))
    scale_four = inverse_rms(down_raw)
    result = (middle + down_raw * scale_four * gain_rows[3]).astype(LOW)
    upstream = out_grad.astype(F32)
    down_grad, gain_four = norm_backward(upstream, down_raw, scale_four, gain_rows[3])
    down_wide = spread_tokens(down_grad.astype(LOW))
    hidden_grad = dot_nt(down_wide, down_weight)
    gate_grad, up_grad = gelu_back(hidden_grad)
    gate_low, up_low = gate_grad.astype(LOW), up_grad.astype(LOW)
    mine, first = sum_first(
        (dot_nn(gate_low, gate_weight) + dot_nn(up_low, up_weight)).astype(LOW)
    )
    first, gate_low, up_low, hidden = lax.optimization_barrier((first, gate_low, up_low, hidden))
    normed_two_grad = sum_second(mine, first)
    grad_wide = jnp.concatenate(
        [
            dot_tn(part, tokens).astype(LOW).reshape(8, PADDED, D)
            for part, tokens in ((gate_low, wide_two), (up_low, wide_two), (hidden, down_wide))
        ],
        axis=1,
    )
    grad_wide = list(grad_wide.reshape(4, 2, 3 * PADDED, D))
    wide_first = scatter_first(grad_wide, "y")

    middle_part, gain_three = norm_backward(normed_two_grad, middle, scale_three, gain_rows[2])
    middle_grad = upstream + middle_part
    attn_grad, gain_two = norm_backward(middle_grad, attn_raw, scale_two, gain_rows[1])
    attn_low = attn_grad.astype(LOW)
    context_grad = dot_nt(attn_low, out_weight).astype(LOW)
    context_grad = jnp.concatenate(
        [context_grad[:, h * HD : (h + 1) * HD] for h in range(H)], axis=0
    )
    prob_grad = dot_nt(context_grad, values)
    centre = jnp.sum(probs * prob_grad, axis=-1, keepdims=True)
    score_low = (probs * (prob_grad - centre)).astype(LOW)
    wide_first, score_low = lax.optimization_barrier((wide_first, score_low))
    wide_parts = scatter_parts(grad_wide, wide_first, "y")
    key_part = dot_tn(score_low, query_rot) * SCALE
    value_part = dot_tn(probs_low, context_grad)
    pair_grad = jnp.concatenate([key_part, value_part], axis=1).astype(LOW)
    pair_grad = pair_grad.reshape(4, 2, OWN, 2 * HD)
    pair_grad = list(pair_grad)
    pair_first = scatter_first(pair_grad, "x")
    query_grad = dot_nn(score_low, keys) * SCALE
    query_raw_grad, query_gain = query_back(query_grad)
    query_low = query_raw_grad.astype(LOW)
    query_low = jnp.concatenate([query_low[h * OWN : (h + 1) * OWN] for h in range(H)], axis=1)
    mine, other = divide(
        place, [dot_tn(query_low, normed_one).astype(LOW), dot_tn(context, attn_low).astype(LOW)]
    )
    mine = add(mine, swap(other, "core")).astype(LOW)
    pair_first, mine = lax.optimization_barrier((pair_first, mine))
    pair_grad = add(*scatter_parts(pair_grad, pair_first, "x"))
    head_rows = scatter_ring(list(mine), "x").astype(LOW)
    pair_grad = add(pair_grad[0], swap(pair_grad[1].astype(LOW), "zh"))
    key_raw_grad, key_gain = key_back(pair_grad[:, :HD])
    key_low = key_raw_grad.astype(LOW)
    value_grad_low = pair_grad[:, HD:].astype(LOW)
    normed_one_grad = (
        dot_nn(query_low, query_weight)
        + dot_nn(key_low, key_weight)
        + dot_nn(value_grad_low, value_weight)
    )
    stream_part, gain_one = norm_backward(normed_one_grad, stream, scale_one, gain_rows[0])
    input_grad = (middle_grad + stream_part).astype(LOW)

    gains_grad = jnp.stack([gain_one, gain_two, gain_three, gain_four])
    head_grad = jnp.concatenate([query_gain, key_gain]).reshape(1, 2 * HD)
    head_grad = jnp.pad(head_grad, ((0, 0), (0, HALF - 2 * HD)))
    misc = jnp.concatenate(
        [gains_grad, jnp.concatenate([head_grad, head_grad], axis=1), jnp.zeros((11, D), F32)],
        axis=0,
    )
    mine, other = divide(
        place,
        [dot_tn(key_low, normed_one).astype(LOW), dot_tn(value_grad_low, normed_one).astype(LOW)],
        misc.astype(LOW),
    )
    mine = add(mine[0], swap(other[0], "core")).astype(LOW)
    rows = list(jnp.concatenate([mine, head_rows], axis=1).reshape(4, 2, 5, 16, D))
    first = scatter_first(rows, "y")
    first, wide_parts = lax.optimization_barrier((first, wide_parts))
    rows = sum_z(add(*scatter_parts(rows, first, "y")).astype(LOW))
    wide_rows = sum_z(add(*wide_parts).astype(LOW))
    gate_shard, up_shard = wide_rows[:UNITS].T, wide_rows[PADDED : PADDED + UNITS].T
    down_rows = wide_rows[2 * PADDED : 2 * PADDED + UNITS].astype(LOW)
    query_shard = rows[3].T
    down_rows = jnp.concatenate([down_rows, rows[4].astype(LOW)], axis=0)
    down_rows = down_rows.reshape(UNITS + 16, 16, 36).transpose(1, 0, 2)
    down_rows = lax.all_to_all(down_rows, groups, 0, 0, tiled=True).astype(F32)
    down_shard = down_rows[:, :UNITS].reshape(16 * UNITS, 36)
    out_shard = down_rows[:, UNITS:].reshape(HD, 36)
    pair_rows = add(*gather_direct(rows[:3].astype(LOW), "x"))
    key_shard, value_shard = pair_rows[0].T, pair_rows[1].T
    gains_shard = lax.dynamic_slice(pair_rows[2], (0, gain_place), (4, 9))
    head_shard = lax.dynamic_slice(
        pair_rows[2, 4, : 2 * HD].reshape(2, HD), (0, head_place), (2, 16)
    )
    return (
        result,
        input_grad,
        query_shard,
        key_shard,
        value_shard,
        out_shard,
        gate_shard,
        up_shard,
        down_shard,
        gains_shard,
        head_shard,
    )


def solution(mesh):
    split = Mesh(mesh.devices.reshape(4, 2, 2, 2, 4), ("y", "zl", "core", "zh", "x"))
    dp = ("y", "zl", "core")
    weights = (
        P("zh", ("x",) + dp),
        P("zh", dp),
        P("zh", dp),
        P("x", ("zh",) + dp),
        P("zh", ("x",) + dp),
        P("zh", ("x",) + dp),
        P("x", ("zh",) + dp),
        P(None, ("zh", "x") + dp),
        P(None, dp),
    )
    tokens = P(dp + ("zh", "x"), None)
    return jax.shard_map(
        on_device,
        mesh=split,
        in_specs=(tokens, P(dp), P(dp), tokens) + weights,
        out_specs=(tokens, tokens) + weights,
        check_vma=False,
    )
```

```python
import math

import jax
import jax.numpy as jnp
from jax import lax
from jax.experimental import pallas as pl
from jax.experimental.layout import Layout, with_layout_constraint
from jax.experimental.pallas import tpu as pltpu
from jax.sharding import Mesh, PartitionSpec as P

D = 1152
HALF = 576
H = 4
HD = 256
FF = 6912
LEN = 1216
OWN = 152
UNITS = 108
PADDED = 112
EPSILON = 1e-06
ROPE_BASE = 1000000.0
MASKED = -1e30
SCALE = HD ** (-0.5)
LOW = jnp.bfloat16
F32 = jnp.float32


def shift(v, axis, step):
    size = lax.axis_size(axis)
    return lax.ppermute(v, axis, [(i, (i + step) % size) for i in range(size)])


def swap(v, axis):
    return shift(v, axis, 1)


def gather_direct(v, axis):
    return [v, shift(v, axis, -1), shift(v, axis, -2), shift(v, axis, 1)]


def shift_z(v, step):
    own = [(z % 2) * 2 + z // 2 for z in range(4)]
    return lax.ppermute(v, ("zl", "zh"), [(own[z], own[(z + step) % 4]) for z in range(4)])


def half_of(v):
    if v.ndim > 2:
        return v.shape[0] // 2
    return (v.shape[0] // 2 + 7) // 8 * 8


def gather_first(v, axis):
    return shift(v, axis, 1), shift(v, axis, -1)


def gather_second(v, first, axis):
    before, after = first
    half = half_of(v)
    opposite = jnp.concatenate(
        [shift(before[:half], axis, 1), shift(after[half:], axis, -1)], axis=0
    )
    return [v, after, opposite, before]


def gather_ring(v, axis):
    return gather_second(v, gather_first(v, axis), axis)


def add(*parts):
    total = parts[0].astype(F32)
    for part in parts[1:]:
        total = total + part.astype(F32)
    return total


def scatter_first(blocks, axis):
    opposite = blocks[2]
    half = half_of(opposite)
    return shift(opposite[:half], axis, 1), shift(opposite[half:], axis, -1)


def scatter_parts(blocks, first, axis):
    own, after, _, before = blocks
    passed_up, passed_down = first
    half = half_of(own)
    up = jnp.concatenate([add(after[:half], passed_up).astype(LOW), after[half:]], axis=0)
    down = jnp.concatenate([before[:half], add(before[half:], passed_down).astype(LOW)], axis=0)
    return own, shift(up, axis, 1), shift(down, axis, -1)


def scatter_ring(blocks, axis):
    return add(*scatter_parts(blocks, scatter_first(blocks, axis), axis))


def row_major(v):
    return with_layout_constraint(v, Layout(major_to_minor=tuple(range(v.ndim))))


def whole(shape, dtype):
    return jax.ShapeDtypeStruct(shape, dtype)


VMEM = pl.BlockSpec(memory_space=pltpu.VMEM)
SMEM = pl.BlockSpec(memory_space=pltpu.SMEM)
BIG = pltpu.CompilerParams(vmem_limit_bytes=32 * 1024 * 1024)


def row_blocks(place_ref):
    for y in range(4):
        for zl in range(2):
            for side in range(2):
                row = y * 64 + zl * 32 + place_ref[8 + side] * 16
                yield side, place_ref[y * 2 + zl], pl.multiple_of(row, 16)


def assemble(place, mine, other, parts):
    heads, summed = mine.shape[0], mine.shape[2] > parts

    def kernel(place_ref, mine_ref, other_ref, *out_refs):
        for side, block, row in row_blocks(place_ref):
            ref = other_ref if side else mine_ref
            for h in range(heads):
                for part in range(parts):
                    out_refs[part][pl.ds(row + h * HD, 16), :] = ref[h, block, part]
        if summed:
            total = mine_ref[0, 0, parts].astype(F32) + other_ref[0, 0, parts].astype(F32)
            for k in range(1, 8):
                total = total + mine_ref[0, k, parts].astype(F32)
                total = total + other_ref[0, k, parts].astype(F32)
            out_refs[parts][...] = total

    shapes = [whole((heads * HD, D), LOW)] * parts + [whole((16, D), F32)] * summed
    return pl.pallas_call(
        kernel,
        out_shape=shapes,
        in_specs=[SMEM, VMEM, VMEM],
        out_specs=[VMEM] * len(shapes),
        compiler_params=BIG,
    )(place, mine, other)


def divide(place, grads, everywhere=None):
    heads, parts = grads[0].shape[0] // HD, len(grads)
    given = list(grads) + ([] if everywhere is None else [everywhere])

    def kernel(place_ref, *refs):
        grad_refs, (mine_ref, other_ref) = refs[: len(given)], refs[len(given) :]
        for side, block, row in row_blocks(place_ref):
            ref = other_ref if side else mine_ref
            for h in range(heads):
                for part in range(parts):
                    ref[h, block, part] = grad_refs[part][pl.ds(row + h * HD, 16), :]
            if everywhere is not None:
                ref[0, block, parts] = grad_refs[parts][...]

    return pl.pallas_call(
        kernel,
        out_shape=(whole((heads, 8, len(given), 16, D), LOW),) * 2,
        in_specs=[SMEM] + [VMEM] * len(given),
        out_specs=(VMEM, VMEM),
        compiler_params=BIG,
    )(place, *given)


def dot_nt(a, b):
    return lax.dot_general(a, b, (((1,), (1,)), ((), ())), preferred_element_type=F32)


def dot_nn(a, b):
    return lax.dot_general(a, b, (((1,), (0,)), ((), ())), preferred_element_type=F32)


def dot_tn(a, b):
    return lax.dot_general(a, b, (((0,), (0,)), ((), ())), preferred_element_type=F32)


def inverse_rms(values):
    return lax.rsqrt(jnp.mean(values * values, axis=-1, keepdims=True) + EPSILON)


def norm_backward(upstream, source, inverse, gain_row):
    weighted = upstream * gain_row
    inner = jnp.mean(weighted * source, axis=-1, keepdims=True)
    source_grad = inverse * weighted - source * (inverse * inverse * inverse) * inner
    gain_grad = jnp.sum(upstream * source * inverse, axis=0)
    return source_grad, gain_grad


def rotary_tables(places):
    frequencies = jnp.exp(
        jnp.arange(HD // 2, dtype=F32) * (-2.0 * math.log(ROPE_BASE) / HD)
    )
    angles = places.astype(F32)[:, None] * frequencies[None, :]
    return jnp.cos(angles), jnp.sin(angles)


def rotate(values, cosine, sine):
    front, back = values[..., : HD // 2], values[..., HD // 2 :]
    return jnp.concatenate(
        [front * cosine - back * sine, back * cosine + front * sine], axis=-1
    )


def in_order(first, mine, other):
    return jnp.where(first, mine, other), jnp.where(first, other, mine)


def on_device(
    hidden_in,
    segments,
    positions,
    out_grad,
    w_query,
    w_key,
    w_value,
    w_out,
    w_gate,
    w_up,
    w_down,
    norm_gains,
    head_gains,
):
    iy = lax.axis_index("y")
    izh = lax.axis_index("zh")
    ix = lax.axis_index("x")
    ic = lax.axis_index("core")
    izl = lax.axis_index("zl")
    ring = jnp.arange(4, dtype=jnp.int32)
    place = jnp.concatenate(
        [
            (((ring - iy) % 4)[:, None] * 2 + ((ring[:2] - izl) % 2)[None, :]).reshape(8),
            jnp.stack([ic, 1 - ic]).astype(jnp.int32),
        ]
    )

    def other_both(v):
        return lax.ppermute(v, ("zl", "zh"), [(i, 3 - i) for i in range(4)])

    def spread_z(v):
        near = jnp.concatenate(in_order(izh == 0, v, swap(v, "zh")), axis=1)
        far = jnp.concatenate(in_order(izh == 0, swap(v, "zl"), other_both(v)), axis=1)
        return row_major(jnp.stack([near, far]))

    def ring_z_first(v):
        return shift_z(v, 1), shift_z(v, -1)

    def ring_z_second(first):
        before, after = first
        half = half_of(before)
        return shift_z(before[:half], 1), shift_z(after[half:], -1)

    def ring_z_last(v, first, second):
        before, after = first
        opposite = jnp.concatenate(second, axis=0)
        even = izl == 0
        near_z, far_z = jnp.where(even, after, before), jnp.where(even, before, after)
        near = jnp.concatenate(in_order(izh == 0, v, opposite), axis=1)
        far = jnp.concatenate(in_order(izh == 0, near_z, far_z), axis=1)
        return row_major(jnp.stack([near, far]))

    def sum_z(v):
        near = in_order(izh == 0, v[0, ..., :HALF], v[0, ..., HALF:])
        far = in_order(izh == 0, v[1, ..., :HALF], v[1, ..., HALF:])
        return add(near[0], swap(near[1], "zh"), swap(far[0], "zl"), other_both(far[1]))

    groups = ("y", "zl", "core")
    down_rows = jnp.concatenate(
        [w_down.reshape(16, UNITS, 36), w_out.reshape(16, 16, 36)], axis=1
    )
    down_rows, norm_gains = lax.optimization_barrier((down_rows, norm_gains))
    down_rows = lax.all_to_all(down_rows, groups, 0, 0, tiled=True)
    hidden_pair = jnp.stack([hidden_in, swap(hidden_in, "zh")])
    hidden_first = gather_first(hidden_pair, "x")
    down_rows = down_rows.transpose(1, 0, 2).reshape(UNITS + 16, HALF)
    gain_place = ((ix * 4 + iy) * 4 + izl * 2 + ic) * 9
    head_place = (iy * 4 + izl * 2 + ic) * 16
    gains = lax.dynamic_update_slice(
        jnp.zeros((4, D), LOW), norm_gains, (0, izh * HALF + gain_place)
    )
    heads = lax.dynamic_update_slice(jnp.zeros((2, HD), LOW), head_gains, (0, head_place))
    heads = jnp.where((izh == 0) & (ix == 0), heads, jnp.zeros((), LOW)).reshape(1, 2 * HD)
    misc = jnp.concatenate(
        [gains, jnp.pad(heads, ((0, 0), (0, D - 2 * HD))), jnp.zeros((3, D), LOW)], axis=0
    )
    misc = add(*gather_direct(misc, "x")).astype(LOW)
    pack = spread_z(
        jnp.concatenate(
            [w_key.T, w_value.T, w_query.T, down_rows[UNITS:], misc[:, :HALF], misc[:, HALF:]],
            axis=0,
        )
    )
    w_gate, w_up, down_rows, pack, hidden_first = lax.optimization_barrier(
        (w_gate, w_up, down_rows, pack, hidden_first)
    )
    def pad_units(v):
        return jnp.pad(v, ((0, PADDED - UNITS), (0, 0)))

    wide_rows = row_major(
        jnp.concatenate(
            [pad_units(w_gate.T), pad_units(w_up.T), pad_units(down_rows[:UNITS])], axis=0
        )
    )
    wide_z = ring_z_first(wide_rows)
    pack_first = gather_first(pack, "y")
    pack_first, wide_z = lax.optimization_barrier((pack_first, wide_z))
    hidden_wide = jnp.concatenate(gather_second(hidden_pair, hidden_first, "x"), axis=0)
    hidden_wide = hidden_wide.reshape(LEN, D)
    wide_second = ring_z_second(wide_z)
    pack = jnp.concatenate(gather_second(pack, pack_first, "y"), axis=0).reshape(1, 8, 5, 16, D)
    pair_part = jnp.concatenate([pack[:, :, :2], pack[:, :, 4:]], axis=2)
    key_weight, value_weight, misc = assemble(place, pair_part, swap(pair_part, "core"), 2)
    misc = misc[:, :HALF] + misc[:, HALF:]
    misc = jnp.concatenate([misc[:8], misc[8:]], axis=1)
    gain_rows = misc[:4]
    head_gain = misc[4, : 2 * HD].reshape(2, HD)
    head_part = pack[0, :, 2:4]
    head_first = gather_first(head_part, "x")

    key_start = jnp.stack(
        [((izh + b) % 2 * 4 + (ix + a) % 4) * OWN for a in range(4) for b in range(2)]
    )
    key_order = (key_start[:, None] + jnp.arange(OWN, dtype=jnp.int32)[None, :]).reshape(LEN)
    key_segments, key_positions = (
        jnp.concatenate([lax.dynamic_slice_in_dim(v, key_start[k], OWN) for k in range(8)])
        for v in (segments, positions)
    )
    token_start = (izh * 4 + ix) * OWN
    own_segments = key_segments[:OWN]
    cosine_wide, sine_wide = rotary_tables(key_positions)
    cosine, sine = cosine_wide[:OWN], sine_wide[:OWN]
    stream_wide = hidden_wide.astype(F32)
    scale_wide = inverse_rms(stream_wide)
    normed_wide = (stream_wide * scale_wide * gain_rows[0]).astype(LOW)
    stream, scale_one, normed_one = stream_wide[:OWN], scale_wide[:OWN], normed_wide[:OWN]
    keys_raw = dot_nt(normed_wide, key_weight)
    values = dot_nt(normed_wide, value_weight).astype(LOW)
    keys = rotate(
        keys_raw * inverse_rms(keys_raw) * head_gain[1], cosine_wide, sine_wide
    ).astype(LOW)
    _, key_back = jax.vjp(
        lambda raw, gain: rotate(raw * inverse_rms(raw) * gain, cosine, sine),
        keys_raw[:OWN],
        head_gain[1],
    )
    wide_second, head_first = lax.optimization_barrier((wide_second, head_first))
    wide_pair = ring_z_last(wide_rows, wide_z, wide_second)
    head_part = jnp.stack(gather_second(head_part, head_first, "x"))
    query_weight, out_weight = assemble(place, head_part, swap(head_part, "core"), 2)
    query_raw = jnp.concatenate(
        [dot_nt(normed_one, query_weight[h * HD : (h + 1) * HD]) for h in range(H)], axis=0
    )
    cosine_heads, sine_heads = jnp.tile(cosine, (H, 1)), jnp.tile(sine, (H, 1))
    query_norm, query_back = jax.vjp(
        lambda raw, gain: rotate(raw * inverse_rms(raw) * gain, cosine_heads, sine_heads),
        query_raw,
        head_gain[0],
    )
    query_rot = query_norm.astype(LOW)
    query_order = token_start + jnp.arange(OWN, dtype=jnp.int32)
    allowed = (own_segments[:, None] == key_segments[None, :]) & (
        query_order[:, None] >= key_order[None, :]
    )
    scores = (dot_nt(query_rot, keys) * SCALE).reshape(H, OWN, LEN)
    scores = jnp.where(allowed[None], scores, MASKED)
    exponent = jnp.exp(scores - jnp.max(scores, axis=-1, keepdims=True))
    probs = (exponent / jnp.sum(exponent, axis=-1, keepdims=True)).reshape(H * OWN, LEN)
    probs_low = probs.astype(LOW)
    context = dot_nn(probs_low, values).astype(LOW)
    context = jnp.concatenate([context[h * OWN : (h + 1) * OWN] for h in range(H)], axis=1)

    units = 8 * PADDED
    wide_first = gather_first(wide_pair, "y")
    wide_first, context = lax.optimization_barrier((wide_first, context))
    wide_rows = [part[k] for part in gather_second(wide_pair, wide_first, "y") for k in range(2)]
    gate_weight, up_weight, down_weight = (
        jnp.concatenate([part[k * PADDED : (k + 1) * PADDED] for part in wide_rows], axis=0)
        for k in range(3)
    )

    def spread_tokens(v):
        mine = jnp.concatenate(gather_ring(v, "x"), axis=0)
        return jnp.concatenate([mine, swap(mine, "core")], axis=0)

    def sum_first(v):
        v = v.reshape(2, 4, OWN, D)
        mine = list(add(v[0], swap(v[1], "core")).astype(LOW))
        return mine, scatter_first(mine, "x")

    def sum_second(mine, first):
        return add(*scatter_parts(mine, first, "x"))

    attn_raw = dot_nn(context, out_weight)
    scale_two = inverse_rms(attn_raw)
    middle = stream + attn_raw * scale_two * gain_rows[1]
    scale_three = inverse_rms(middle)
    normed_two = (middle * scale_three * gain_rows[2]).astype(LOW)
    wide_two = spread_tokens(normed_two)
    gate_raw = dot_nt(wide_two, gate_weight)
    up_raw = dot_nt(wide_two, up_weight)
    activated, gelu_back = jax.vjp(
        lambda gate, up: jax.nn.gelu(gate, approximate=True) * up, gate_raw, up_raw
    )
    hidden = activated.astype(LOW)
    down_raw = sum_second(*sum_first(dot_nn(hidden, down_weight).astype(LOW)))
    scale_four = inverse_rms(down_raw)
    result = (middle + down_raw * scale_four * gain_rows[3]).astype(LOW)
    upstream = out_grad.astype(F32)
    down_grad, gain_four = norm_backward(upstream, down_raw, scale_four, gain_rows[3])
    down_wide = spread_tokens(down_grad.astype(LOW))
    hidden_grad = dot_nt(down_wide, down_weight)
    gate_grad, up_grad = gelu_back(hidden_grad)
    gate_low, up_low = gate_grad.astype(LOW), up_grad.astype(LOW)
    mine, first = sum_first(
        (dot_nn(gate_low, gate_weight) + dot_nn(up_low, up_weight)).astype(LOW)
    )
    normed_two_grad = sum_second(mine, first)
    grad_wide = jnp.concatenate(
        [
            dot_tn(part, tokens).astype(LOW).reshape(8, PADDED, D)
            for part, tokens in ((gate_low, wide_two), (up_low, wide_two), (hidden, down_wide))
        ],
        axis=1,
    )
    grad_wide = list(grad_wide.reshape(4, 2, 3 * PADDED, D))
    wide_first = scatter_first(grad_wide, "y")

    middle_part, gain_three = norm_backward(normed_two_grad, middle, scale_three, gain_rows[2])
    middle_grad = upstream + middle_part
    attn_grad, gain_two = norm_backward(middle_grad, attn_raw, scale_two, gain_rows[1])
    attn_low = attn_grad.astype(LOW)
    context_grad = dot_nt(attn_low, out_weight).astype(LOW)
    context_grad = jnp.concatenate(
        [context_grad[:, h * HD : (h + 1) * HD] for h in range(H)], axis=0
    )
    prob_grad = dot_nt(context_grad, values)
    centre = jnp.sum(probs * prob_grad, axis=-1, keepdims=True)
    score_low = (probs * (prob_grad - centre)).astype(LOW)
    wide_first, score_low = lax.optimization_barrier((wide_first, score_low))
    wide_parts = scatter_parts(grad_wide, wide_first, "y")
    key_part = dot_tn(score_low, query_rot) * SCALE
    value_part = dot_tn(probs_low, context_grad)
    pair_grad = jnp.concatenate([key_part, value_part], axis=1).astype(LOW)
    pair_grad = pair_grad.reshape(4, 2, OWN, 2 * HD)
    pair_grad = list(pair_grad)
    pair_first = scatter_first(pair_grad, "x")
    query_grad = dot_nn(score_low, keys) * SCALE
    query_raw_grad, query_gain = query_back(query_grad)
    query_low = query_raw_grad.astype(LOW)
    query_low = jnp.concatenate([query_low[h * OWN : (h + 1) * OWN] for h in range(H)], axis=1)
    mine, other = divide(
        place, [dot_tn(query_low, normed_one).astype(LOW), dot_tn(context, attn_low).astype(LOW)]
    )
    mine = add(mine, swap(other, "core")).astype(LOW)
    pair_first, mine = lax.optimization_barrier((pair_first, mine))
    pair_grad = add(*scatter_parts(pair_grad, pair_first, "x"))
    head_rows = scatter_ring(list(mine), "x").astype(LOW)
    pair_grad = add(pair_grad[0], swap(pair_grad[1].astype(LOW), "zh"))
    key_raw_grad, key_gain = key_back(pair_grad[:, :HD])
    key_low = key_raw_grad.astype(LOW)
    value_grad_low = pair_grad[:, HD:].astype(LOW)
    normed_one_grad = (
        dot_nn(query_low, query_weight)
        + dot_nn(key_low, key_weight)
        + dot_nn(value_grad_low, value_weight)
    )
    stream_part, gain_one = norm_backward(normed_one_grad, stream, scale_one, gain_rows[0])
    input_grad = (middle_grad + stream_part).astype(LOW)

    gains_grad = jnp.stack([gain_one, gain_two, gain_three, gain_four])
    head_grad = jnp.concatenate([query_gain, key_gain]).reshape(1, 2 * HD)
    head_grad = jnp.pad(head_grad, ((0, 0), (0, HALF - 2 * HD)))
    misc = jnp.concatenate(
        [gains_grad, jnp.concatenate([head_grad, head_grad], axis=1), jnp.zeros((11, D), F32)],
        axis=0,
    )
    mine, other = divide(
        place,
        [dot_tn(key_low, normed_one).astype(LOW), dot_tn(value_grad_low, normed_one).astype(LOW)],
        misc.astype(LOW),
    )
    mine = add(mine[0], swap(other[0], "core")).astype(LOW)
    mine, wide_parts = lax.optimization_barrier((mine, wide_parts))
    rows = list(jnp.concatenate([mine, head_rows], axis=1).reshape(4, 2, 5, 16, D))
    first = scatter_first(rows, "y")
    wide_pair = add(*wide_parts).astype(LOW)
    first, wide_pair = lax.optimization_barrier((first, wide_pair))
    rows = sum_z(add(*scatter_parts(rows, first, "y")).astype(LOW))
    wide_rows = sum_z(wide_pair)
    gate_shard, up_shard = wide_rows[:UNITS].T, wide_rows[PADDED : PADDED + UNITS].T
    down_rows = wide_rows[2 * PADDED : 2 * PADDED + UNITS].astype(LOW)
    query_shard = rows[3].T
    down_rows = jnp.concatenate([down_rows, rows[4].astype(LOW)], axis=0)
    down_rows = down_rows.reshape(UNITS + 16, 16, 36).transpose(1, 0, 2)
    down_rows = lax.all_to_all(down_rows, groups, 0, 0, tiled=True).astype(F32)
    down_shard = down_rows[:, :UNITS].reshape(16 * UNITS, 36)
    out_shard = down_rows[:, UNITS:].reshape(HD, 36)
    pair_rows = add(*gather_direct(rows[:3].astype(LOW), "x"))
    key_shard, value_shard = pair_rows[0].T, pair_rows[1].T
    gains_shard = lax.dynamic_slice(pair_rows[2], (0, gain_place), (4, 9))
    head_shard = lax.dynamic_slice(
        pair_rows[2, 4, : 2 * HD].reshape(2, HD), (0, head_place), (2, 16)
    )
    return (
        result,
        input_grad,
        query_shard,
        key_shard,
        value_shard,
        out_shard,
        gate_shard,
        up_shard,
        down_shard,
        gains_shard,
        head_shard,
    )


def solution(mesh):
    split = Mesh(mesh.devices.reshape(4, 2, 2, 2, 4), ("y", "zl", "core", "zh", "x"))
    dp = ("y", "zl", "core")
    weights = (
        P("zh", ("x",) + dp),
        P("zh", dp),
        P("zh", dp),
        P("x", ("zh",) + dp),
        P("zh", ("x",) + dp),
        P("zh", ("x",) + dp),
        P("x", ("zh",) + dp),
        P(None, ("zh", "x") + dp),
        P(None, dp),
    )
    tokens = P(dp + ("zh", "x"), None)
    return jax.shard_map(
        on_device,
        mesh=split,
        in_specs=(tokens, P(dp), P(dp), tokens) + weights,
        out_specs=(tokens, tokens) + weights,
        check_vma=False,
    )
```

```python
import math

import jax
import jax.numpy as jnp
from jax import lax
from jax.experimental import pallas as pl
from jax.experimental.layout import Layout, with_layout_constraint
from jax.experimental.pallas import tpu as pltpu
from jax.sharding import Mesh, PartitionSpec as P

D = 1152
HALF = 576
H = 4
HD = 256
FF = 6912
LEN = 1216
OWN = 152
UNITS = 108
PADDED = 112
EPSILON = 1e-06
ROPE_BASE = 1000000.0
MASKED = -1e30
SCALE = HD ** (-0.5)
LOW = jnp.bfloat16
F32 = jnp.float32


def shift(v, axis, step):
    size = lax.axis_size(axis)
    return lax.ppermute(v, axis, [(i, (i + step) % size) for i in range(size)])


def swap(v, axis):
    return shift(v, axis, 1)


def gather_direct(v, axis):
    return [v, shift(v, axis, -1), shift(v, axis, -2), shift(v, axis, 1)]


def half_of(v):
    if v.ndim > 2:
        return v.shape[0] // 2
    return (v.shape[0] // 2 + 7) // 8 * 8


def gather_first(v, axis):
    return shift(v, axis, 1), shift(v, axis, -1)


def gather_second(v, first, axis):
    before, after = first
    half = half_of(v)
    opposite = jnp.concatenate(
        [shift(before[:half], axis, 1), shift(after[half:], axis, -1)], axis=0
    )
    return [v, after, opposite, before]


def gather_ring(v, axis):
    return gather_second(v, gather_first(v, axis), axis)


def add(*parts):
    total = parts[0].astype(F32)
    for part in parts[1:]:
        total = total + part.astype(F32)
    return total


def scatter_first(blocks, axis):
    opposite = blocks[2]
    half = half_of(opposite)
    return shift(opposite[:half], axis, 1), shift(opposite[half:], axis, -1)


def scatter_parts(blocks, first, axis):
    own, after, _, before = blocks
    passed_up, passed_down = first
    half = half_of(own)
    up = jnp.concatenate([add(after[:half], passed_up).astype(LOW), after[half:]], axis=0)
    down = jnp.concatenate([before[:half], add(before[half:], passed_down).astype(LOW)], axis=0)
    return own, shift(up, axis, 1), shift(down, axis, -1)


def scatter_ring(blocks, axis):
    return add(*scatter_parts(blocks, scatter_first(blocks, axis), axis))


def row_major(v):
    return with_layout_constraint(v, Layout(major_to_minor=tuple(range(v.ndim))))


def whole(shape, dtype):
    return jax.ShapeDtypeStruct(shape, dtype)


VMEM = pl.BlockSpec(memory_space=pltpu.VMEM)
SMEM = pl.BlockSpec(memory_space=pltpu.SMEM)
BIG = pltpu.CompilerParams(vmem_limit_bytes=32 * 1024 * 1024)


def row_blocks(place_ref):
    for y in range(4):
        for zl in range(2):
            for side in range(2):
                row = y * 64 + zl * 32 + place_ref[8 + side] * 16
                yield side, place_ref[y * 2 + zl], pl.multiple_of(row, 16)


def assemble(place, mine, other, parts):
    heads, summed = mine.shape[0], mine.shape[2] > parts

    def kernel(place_ref, mine_ref, other_ref, *out_refs):
        for side, block, row in row_blocks(place_ref):
            ref = other_ref if side else mine_ref
            for h in range(heads):
                for part in range(parts):
                    out_refs[part][pl.ds(row + h * HD, 16), :] = ref[h, block, part]
        if summed:
            total = mine_ref[0, 0, parts].astype(F32) + other_ref[0, 0, parts].astype(F32)
            for k in range(1, 8):
                total = total + mine_ref[0, k, parts].astype(F32)
                total = total + other_ref[0, k, parts].astype(F32)
            out_refs[parts][...] = total

    shapes = [whole((heads * HD, D), LOW)] * parts + [whole((16, D), F32)] * summed
    return pl.pallas_call(
        kernel,
        out_shape=shapes,
        in_specs=[SMEM, VMEM, VMEM],
        out_specs=[VMEM] * len(shapes),
        compiler_params=BIG,
    )(place, mine, other)


def divide(place, grads, everywhere=None):
    heads, parts = grads[0].shape[0] // HD, len(grads)
    given = list(grads) + ([] if everywhere is None else [everywhere])

    def kernel(place_ref, *refs):
        grad_refs, (mine_ref, other_ref) = refs[: len(given)], refs[len(given) :]
        for side, block, row in row_blocks(place_ref):
            ref = other_ref if side else mine_ref
            for h in range(heads):
                for part in range(parts):
                    ref[h, block, part] = grad_refs[part][pl.ds(row + h * HD, 16), :]
            if everywhere is not None:
                ref[0, block, parts] = grad_refs[parts][...]

    return pl.pallas_call(
        kernel,
        out_shape=(whole((heads, 8, len(given), 16, D), LOW),) * 2,
        in_specs=[SMEM] + [VMEM] * len(given),
        out_specs=(VMEM, VMEM),
        compiler_params=BIG,
    )(place, *given)


def dot_nt(a, b):
    return lax.dot_general(a, b, (((1,), (1,)), ((), ())), preferred_element_type=F32)


def dot_nn(a, b):
    return lax.dot_general(a, b, (((1,), (0,)), ((), ())), preferred_element_type=F32)


def dot_tn(a, b):
    return lax.dot_general(a, b, (((0,), (0,)), ((), ())), preferred_element_type=F32)


def inverse_rms(values):
    return lax.rsqrt(jnp.mean(values * values, axis=-1, keepdims=True) + EPSILON)


def norm_backward(upstream, source, inverse, gain_row):
    weighted = upstream * gain_row
    inner = jnp.mean(weighted * source, axis=-1, keepdims=True)
    source_grad = inverse * weighted - source * (inverse * inverse * inverse) * inner
    gain_grad = jnp.sum(upstream * source * inverse, axis=0, keepdims=True)
    return source_grad, gain_grad


def rotary_tables(places):
    frequencies = jnp.exp(
        jnp.arange(HD // 2, dtype=F32) * (-2.0 * math.log(ROPE_BASE) / HD)
    )
    angles = places.astype(F32)[:, None] * frequencies[None, :]
    return jnp.cos(angles), jnp.sin(angles)


def rotate(values, cosine, sine):
    front, back = values[..., : HD // 2], values[..., HD // 2 :]
    return jnp.concatenate(
        [front * cosine - back * sine, back * cosine + front * sine], axis=-1
    )


def in_order(first, mine, other):
    return jnp.where(first, mine, other), jnp.where(first, other, mine)


def on_device(
    hidden_in,
    segments,
    positions,
    out_grad,
    w_query,
    w_key,
    w_value,
    w_out,
    w_gate,
    w_up,
    w_down,
    norm_gains,
    head_gains,
):
    iy = lax.axis_index("y")
    izh = lax.axis_index("zh")
    ix = lax.axis_index("x")
    ic = lax.axis_index("core")
    izl = lax.axis_index("zl")
    ring = jnp.arange(4, dtype=jnp.int32)
    place = jnp.concatenate(
        [
            (((ring - iy) % 4)[:, None] * 2 + ((ring[:2] - izl) % 2)[None, :]).reshape(8),
            jnp.stack([ic, 1 - ic]).astype(jnp.int32),
        ]
    )

    def other_both(v):
        return lax.ppermute(v, ("zl", "zh"), [(i, 3 - i) for i in range(4)])

    def spread_z(v):
        near = jnp.concatenate(in_order(izh == 0, v, swap(v, "zh")), axis=1)
        far = jnp.concatenate(in_order(izh == 0, swap(v, "zl"), other_both(v)), axis=1)
        return row_major(jnp.stack([near, far]))

    def sum_z(v):
        near = in_order(izh == 0, v[0, ..., :HALF], v[0, ..., HALF:])
        far = in_order(izh == 0, v[1, ..., :HALF], v[1, ..., HALF:])
        return add(near[0], swap(near[1], "zh"), swap(far[0], "zl"), other_both(far[1]))

    groups = ("y", "zl", "core")
    down_rows = jnp.concatenate(
        [w_down.reshape(16, UNITS, 36), w_out.reshape(16, 16, 36)], axis=1
    )
    down_rows = lax.all_to_all(down_rows, groups, 0, 0, tiled=True)
    down_rows = down_rows.transpose(1, 0, 2).reshape(UNITS + 16, HALF)
    gain_place = ((ix * 4 + iy) * 4 + izl * 2 + ic) * 9
    head_place = (iy * 4 + izl * 2 + ic) * 16
    gains = lax.dynamic_update_slice(
        jnp.zeros((4, D), LOW), norm_gains, (0, izh * HALF + gain_place)
    )
    heads = lax.dynamic_update_slice(jnp.zeros((2, HD), LOW), head_gains, (0, head_place))
    heads = jnp.where((izh == 0) & (ix == 0), heads, jnp.zeros((), LOW)).reshape(1, 2 * HD)
    misc = jnp.concatenate(
        [gains, jnp.pad(heads, ((0, 0), (0, D - 2 * HD))), jnp.zeros((3, D), LOW)], axis=0
    )
    misc = add(*gather_direct(misc, "x")).astype(LOW)
    pack = spread_z(
        jnp.concatenate(
            [w_key.T, w_value.T, w_query.T, down_rows[UNITS:], misc[:, :HALF], misc[:, HALF:]],
            axis=0,
        )
    )
    w_gate, w_up, down_rows, pack = lax.optimization_barrier((w_gate, w_up, down_rows, pack))
    pack = jnp.concatenate(gather_ring(pack, "y"), axis=0).reshape(1, 8, 5, 16, D)
    pair_part = jnp.concatenate([pack[:, :, :2], pack[:, :, 4:]], axis=2)
    key_weight, value_weight, misc = assemble(place, pair_part, swap(pair_part, "core"), 2)
    misc = misc[:, :HALF] + misc[:, HALF:]
    misc = jnp.concatenate([misc[:8], misc[8:]], axis=1)
    gain_rows = misc[:4]
    head_gain = misc[4, : 2 * HD].reshape(2, HD)
    head_part = pack[0, :, 2:4]
    head_first = gather_first(head_part, "x")

    stream = hidden_in.astype(F32)
    scale_one = inverse_rms(stream)
    normed_one = (stream * scale_one * gain_rows[0]).astype(LOW)
    key_raw = dot_nt(normed_one, key_weight)
    value_low = dot_nt(normed_one, value_weight).astype(LOW)
    token_start = (izh * 4 + ix) * OWN
    own_positions = lax.dynamic_slice_in_dim(positions, token_start, OWN)
    own_segments = lax.dynamic_slice_in_dim(segments, token_start, OWN)
    cosine, sine = rotary_tables(own_positions)
    key_rot, key_back = jax.vjp(
        lambda raw, gain: rotate(raw * inverse_rms(raw) * gain, cosine, sine),
        key_raw,
        head_gain[1],
    )
    pair = jnp.concatenate([key_rot.astype(LOW), value_low], axis=1)
    pair_far, head_first = lax.optimization_barrier((swap(pair, "zh"), head_first))
    pair = jnp.stack([pair, pair_far])
    pair = jnp.concatenate(gather_ring(pair, "x"), axis=0)
    pair = pair.reshape(LEN, 2 * HD)
    keys, values = pair[:, :HD], pair[:, HD:]
    key_start = jnp.stack(
        [((izh + b) % 2 * 4 + (ix + a) % 4) * OWN for a in range(4) for b in range(2)]
    )
    key_order = (key_start[:, None] + jnp.arange(OWN, dtype=jnp.int32)[None, :]).reshape(LEN)
    key_segments = jnp.concatenate(
        [lax.dynamic_slice_in_dim(segments, key_start[k], OWN) for k in range(8)]
    )

    head_part = jnp.stack(gather_second(head_part, head_first, "x"))
    query_weight, out_weight = assemble(place, head_part, swap(head_part, "core"), 2)
    query_raw = jnp.concatenate(
        [dot_nt(normed_one, query_weight[h * HD : (h + 1) * HD]) for h in range(H)], axis=0
    )
    cosine_heads, sine_heads = jnp.tile(cosine, (H, 1)), jnp.tile(sine, (H, 1))
    query_norm, query_back = jax.vjp(
        lambda raw, gain: rotate(raw * inverse_rms(raw) * gain, cosine_heads, sine_heads),
        query_raw,
        head_gain[0],
    )
    query_rot = query_norm.astype(LOW)
    query_order = token_start + jnp.arange(OWN, dtype=jnp.int32)
    allowed = (own_segments[:, None] == key_segments[None, :]) & (
        query_order[:, None] >= key_order[None, :]
    )
    scores = (dot_nt(query_rot, keys) * SCALE).reshape(H, OWN, LEN)
    scores = jnp.where(allowed[None], scores, MASKED)
    exponent = jnp.exp(scores - jnp.max(scores, axis=-1, keepdims=True))
    probs = (exponent / jnp.sum(exponent, axis=-1, keepdims=True)).reshape(H * OWN, LEN)
    probs_low = probs.astype(LOW)
    context = dot_nn(probs_low, values).astype(LOW)
    context = jnp.concatenate([context[h * OWN : (h + 1) * OWN] for h in range(H)], axis=1)

    def pad_units(v):
        return jnp.pad(v, ((0, PADDED - UNITS), (0, 0)))

    wide_rows = row_major(
        jnp.concatenate(
            [pad_units(w_gate.T), pad_units(w_up.T), pad_units(down_rows[:UNITS])], axis=0
        )
    )
    wide_pair = spread_z(wide_rows)
    wide_first = gather_first(wide_pair, "y")
    wide_first, context = lax.optimization_barrier((wide_first, context))
    wide_rows = [part[k] for part in gather_second(wide_pair, wide_first, "y") for k in range(2)]
    gate_weight, up_weight, down_weight = (
        jnp.concatenate([part[k * PADDED : (k + 1) * PADDED] for part in wide_rows], axis=0)
        for k in range(3)
    )

    def spread_tokens(v):
        mine = jnp.concatenate(gather_ring(v, "x"), axis=0)
        return mine, swap(mine, "core")

    def sum_tokens(own, other):
        own, other = own.reshape(4, OWN, D), other.reshape(4, OWN, D)
        mine = add(own, swap(other, "core")).astype(LOW)
        return scatter_ring([mine[0], mine[1], mine[2], mine[3]], "x")

    def gated(gate, up):
        return jax.nn.gelu(gate.astype(F32), approximate=True) * up.astype(F32)

    attn_raw = dot_nn(context, out_weight)
    scale_two = inverse_rms(attn_raw)
    middle = stream + attn_raw * scale_two * gain_rows[1]
    scale_three = inverse_rms(middle)
    normed_two = (middle * scale_three * gain_rows[2]).astype(LOW)
    wide_two = spread_tokens(normed_two)
    gates = [dot_nt(tokens, gate_weight).astype(LOW) for tokens in wide_two]
    ups = [dot_nt(tokens, up_weight).astype(LOW) for tokens in wide_two]
    hidden = [gated(*pair).astype(LOW) for pair in zip(gates, ups)]
    down_raw = sum_tokens(*(dot_nn(part, down_weight).astype(LOW) for part in hidden))
    scale_four = inverse_rms(down_raw)
    result = (middle + down_raw * scale_four * gain_rows[3]).astype(LOW)
    upstream = out_grad.astype(F32)
    down_grad, gain_four = norm_backward(upstream, down_raw, scale_four, gain_rows[3])
    down_wide = spread_tokens(down_grad.astype(LOW))
    gate_low, up_low = [], []
    for tokens, gate, up in zip(down_wide, gates, ups):
        _, gated_back = jax.vjp(gated, gate.astype(F32), up.astype(F32))
        gate_grad, up_grad = gated_back(dot_nt(tokens, down_weight))
        gate_low.append(gate_grad.astype(LOW))
        up_low.append(up_grad.astype(LOW))
    normed_two_grad = sum_tokens(
        *(
            (dot_nn(gate, gate_weight) + dot_nn(up, up_weight)).astype(LOW)
            for gate, up in zip(gate_low, up_low)
        )
    )
    gate_low, up_low, hidden, wide_two, down_wide = (
        jnp.concatenate(halves, axis=0) for halves in (gate_low, up_low, hidden, wide_two, down_wide)
    )
    grad_wide = jnp.concatenate(
        [
            dot_tn(part, tokens).astype(LOW).reshape(8, PADDED, D)
            for part, tokens in ((gate_low, wide_two), (up_low, wide_two), (hidden, down_wide))
        ],
        axis=1,
    )
    grad_wide = list(grad_wide.reshape(4, 2, 3 * PADDED, D))
    wide_first = scatter_first(grad_wide, "y")

    middle_part, gain_three = norm_backward(normed_two_grad, middle, scale_three, gain_rows[2])
    middle_grad = upstream + middle_part
    attn_grad, gain_two = norm_backward(middle_grad, attn_raw, scale_two, gain_rows[1])
    attn_low = attn_grad.astype(LOW)
    context_grad = dot_nt(attn_low, out_weight).astype(LOW)
    context_grad = jnp.concatenate(
        [context_grad[:, h * HD : (h + 1) * HD] for h in range(H)], axis=0
    )
    prob_grad = dot_nt(context_grad, values)
    probs = probs_low.astype(F32)
    centre = jnp.sum(probs * prob_grad, axis=-1, keepdims=True)
    score_low = (probs * (prob_grad - centre)).astype(LOW)
    wide_first, score_low = lax.optimization_barrier((wide_first, score_low))
    wide_parts = scatter_parts(grad_wide, wide_first, "y")
    key_part = dot_tn(score_low, query_rot) * SCALE
    value_part = dot_tn(probs_low, context_grad)
    pair_grad = jnp.concatenate([key_part, value_part], axis=1).astype(LOW)
    pair_grad = pair_grad.reshape(4, 2, OWN, 2 * HD)
    pair_grad = list(pair_grad)
    pair_first = scatter_first(pair_grad, "x")
    query_grad = dot_nn(score_low, keys) * SCALE
    query_raw_grad, query_gain = query_back(query_grad)
    query_low = query_raw_grad.astype(LOW)
    query_low = jnp.concatenate([query_low[h * OWN : (h + 1) * OWN] for h in range(H)], axis=1)
    mine, other = divide(
        place, [dot_tn(query_low, normed_one).astype(LOW), dot_tn(context, attn_low).astype(LOW)]
    )
    mine = add(mine, swap(other, "core")).astype(LOW)
    pair_first, mine = lax.optimization_barrier((pair_first, mine))
    pair_grad = add(*scatter_parts(pair_grad, pair_first, "x"))
    head_rows = scatter_ring(list(mine), "x").astype(LOW)
    pair_grad = add(pair_grad[0], swap(pair_grad[1].astype(LOW), "zh"))
    pair_grad, wide_parts = lax.optimization_barrier((pair_grad, wide_parts))
    wide_rows = sum_z(add(*wide_parts).astype(LOW))
    gate_shard, up_shard = wide_rows[:UNITS].T, wide_rows[PADDED : PADDED + UNITS].T
    down_rows = wide_rows[2 * PADDED : 2 * PADDED + UNITS].astype(LOW)
    key_raw_grad, key_gain = key_back(pair_grad[:, :HD])
    key_low = key_raw_grad.astype(LOW)
    value_grad_low = pair_grad[:, HD:].astype(LOW)
    normed_one_grad = (
        dot_nn(query_low, query_weight)
        + dot_nn(key_low, key_weight)
        + dot_nn(value_grad_low, value_weight)
    )
    stream_part, gain_one = norm_backward(normed_one_grad, stream, scale_one, gain_rows[0])
    input_grad = (middle_grad + stream_part).astype(LOW)

    gains_grad = jnp.concatenate([gain_one, gain_two, gain_three, gain_four], axis=0)
    head_grad = jnp.concatenate([query_gain, key_gain]).reshape(1, 2 * HD)
    head_grad = jnp.pad(head_grad, ((0, 0), (0, HALF - 2 * HD)))
    misc = jnp.concatenate(
        [gains_grad, jnp.concatenate([head_grad, head_grad], axis=1), jnp.zeros((11, D), F32)],
        axis=0,
    )
    mine, other = divide(
        place,
        [dot_tn(key_low, normed_one).astype(LOW), dot_tn(value_grad_low, normed_one).astype(LOW)],
        misc.astype(LOW),
    )
    mine = add(mine[0], swap(other[0], "core")).astype(LOW)
    rows = jnp.concatenate([mine, head_rows], axis=1).reshape(4, 2, 5, 16, D)
    rows = sum_z(scatter_ring(list(rows), "y").astype(LOW))
    query_shard = rows[3].T
    down_rows = jnp.concatenate([down_rows, rows[4].astype(LOW)], axis=0)
    down_rows = down_rows.reshape(UNITS + 16, 16, 36).transpose(1, 0, 2)
    down_rows = lax.all_to_all(down_rows, groups, 0, 0, tiled=True).astype(F32)
    down_shard = down_rows[:, :UNITS].reshape(16 * UNITS, 36)
    out_shard = down_rows[:, UNITS:].reshape(HD, 36)
    pair_rows = add(*gather_direct(rows[:3].astype(LOW), "x"))
    key_shard, value_shard = pair_rows[0].T, pair_rows[1].T
    gains_shard = lax.dynamic_slice(pair_rows[2], (0, gain_place), (4, 9))
    head_shard = lax.dynamic_slice(
        pair_rows[2, 4, : 2 * HD].reshape(2, HD), (0, head_place), (2, 16)
    )
    return (
        result,
        input_grad,
        query_shard,
        key_shard,
        value_shard,
        out_shard,
        gate_shard,
        up_shard,
        down_shard,
        gains_shard,
        head_shard,
    )


def solution(mesh):
    split = Mesh(mesh.devices.reshape(4, 2, 2, 2, 4), ("y", "zl", "core", "zh", "x"))
    dp = ("y", "zl", "core")
    weights = (
        P("zh", ("x",) + dp),
        P("zh", dp),
        P("zh", dp),
        P("x", ("zh",) + dp),
        P("zh", ("x",) + dp),
        P("zh", ("x",) + dp),
        P("x", ("zh",) + dp),
        P(None, ("zh", "x") + dp),
        P(None, dp),
    )
    tokens = P(dp + ("zh", "x"), None)
    return jax.shard_map(
        on_device,
        mesh=split,
        in_specs=(tokens, P(dp), P(dp), tokens) + weights,
        out_specs=(tokens, tokens) + weights,
        check_vma=False,
    )
```

```python
import math

import jax
import jax.numpy as jnp
from jax import lax
from jax.experimental import pallas as pl
from jax.experimental.layout import Layout, with_layout_constraint
from jax.experimental.pallas import tpu as pltpu
from jax.sharding import Mesh, PartitionSpec as P

D = 1152
HALF = 576
H = 4
HD = 256
FF = 6912
LEN = 1216
OWN = 152
UNITS = 108
PADDED = 112
EPSILON = 1e-06
ROPE_BASE = 1000000.0
MASKED = -1e30
SCALE = HD ** (-0.5)
LOW = jnp.bfloat16
F32 = jnp.float32


def shift(v, axis, step):
    size = lax.axis_size(axis)
    return lax.ppermute(v, axis, [(i, (i + step) % size) for i in range(size)])


def swap(v, axis):
    return shift(v, axis, 1)


def gather_direct(v, axis):
    return [v, shift(v, axis, -1), shift(v, axis, -2), shift(v, axis, 1)]


def half_of(v):
    if v.ndim > 2:
        return v.shape[0] // 2
    return (v.shape[0] // 2 + 7) // 8 * 8


def gather_first(v, axis):
    return shift(v, axis, 1), shift(v, axis, -1)


def gather_second(v, first, axis):
    before, after = first
    half = half_of(v)
    opposite = jnp.concatenate(
        [shift(before[:half], axis, 1), shift(after[half:], axis, -1)], axis=0
    )
    return [v, after, opposite, before]


def gather_ring(v, axis):
    return gather_second(v, gather_first(v, axis), axis)


def add(*parts):
    total = parts[0].astype(F32)
    for part in parts[1:]:
        total = total + part.astype(F32)
    return total


def scatter_first(blocks, axis):
    _, after, opposite, before = blocks
    half = half_of(opposite)
    up = jnp.concatenate([opposite[:half], after[half:]], axis=0)
    down = jnp.concatenate([opposite[half:], before[:half]], axis=0)
    return shift(up, axis, 1), shift(down, axis, -1)


def scatter_second(blocks, first, axis):
    own, after, _, before = blocks
    up, down = first
    half, rest = half_of(own), own.shape[0] - half_of(own)
    from_before = shift(add(after[:half], up[:half]).astype(LOW), axis, 1)
    from_after = shift(add(before[half:], down[:rest]).astype(LOW), axis, -1)
    return add(
        own,
        jnp.concatenate([from_before, up[half:]], axis=0),
        jnp.concatenate([down[rest:], from_after], axis=0),
    )


def scatter_ring(blocks, axis):
    return scatter_second(blocks, scatter_first(blocks, axis), axis)


def row_major(v):
    return with_layout_constraint(v, Layout(major_to_minor=tuple(range(v.ndim))))


def whole(shape, dtype):
    return jax.ShapeDtypeStruct(shape, dtype)


VMEM = pl.BlockSpec(memory_space=pltpu.VMEM)
SMEM = pl.BlockSpec(memory_space=pltpu.SMEM)
BIG = pltpu.CompilerParams(vmem_limit_bytes=32 * 1024 * 1024)


def row_blocks(place_ref):
    for y in range(4):
        for zl in range(2):
            for side in range(2):
                row = y * 64 + zl * 32 + place_ref[8 + side] * 16
                yield side, place_ref[y * 2 + zl], pl.multiple_of(row, 16)


def assemble(place, mine, other, parts):
    heads, summed = mine.shape[0], mine.shape[2] > parts

    def kernel(place_ref, mine_ref, other_ref, *out_refs):
        for side, block, row in row_blocks(place_ref):
            ref = other_ref if side else mine_ref
            for h in range(heads):
                for part in range(parts):
                    out_refs[part][pl.ds(row + h * HD, 16), :] = ref[h, block, part]
        if summed:
            total = mine_ref[0, 0, parts].astype(F32) + other_ref[0, 0, parts].astype(F32)
            for k in range(1, 8):
                total = total + mine_ref[0, k, parts].astype(F32)
                total = total + other_ref[0, k, parts].astype(F32)
            out_refs[parts][...] = total

    shapes = [whole((heads * HD, D), LOW)] * parts + [whole((16, D), F32)] * summed
    return pl.pallas_call(
        kernel,
        out_shape=shapes,
        in_specs=[SMEM, VMEM, VMEM],
        out_specs=[VMEM] * len(shapes),
        compiler_params=BIG,
    )(place, mine, other)


def divide(place, grads, everywhere=None):
    heads, parts = grads[0].shape[0] // HD, len(grads)
    given = list(grads) + ([] if everywhere is None else [everywhere])

    def kernel(place_ref, *refs):
        grad_refs, (mine_ref, other_ref) = refs[: len(given)], refs[len(given) :]
        for side, block, row in row_blocks(place_ref):
            ref = other_ref if side else mine_ref
            for h in range(heads):
                for part in range(parts):
                    ref[h, block, part] = grad_refs[part][pl.ds(row + h * HD, 16), :]
            if everywhere is not None:
                ref[0, block, parts] = grad_refs[parts][...]

    return pl.pallas_call(
        kernel,
        out_shape=(whole((heads, 8, len(given), 16, D), LOW),) * 2,
        in_specs=[SMEM] + [VMEM] * len(given),
        out_specs=(VMEM, VMEM),
        compiler_params=BIG,
    )(place, *given)


def dot_nt(a, b):
    return lax.dot_general(a, b, (((1,), (1,)), ((), ())), preferred_element_type=F32)


def dot_nn(a, b):
    return lax.dot_general(a, b, (((1,), (0,)), ((), ())), preferred_element_type=F32)


def dot_tn(a, b):
    return lax.dot_general(a, b, (((0,), (0,)), ((), ())), preferred_element_type=F32)


def inverse_rms(values):
    return lax.rsqrt(jnp.mean(values * values, axis=-1, keepdims=True) + EPSILON)


def norm_backward(upstream, source, inverse, gain_row):
    weighted = upstream * gain_row
    inner = jnp.mean(weighted * source, axis=-1, keepdims=True)
    source_grad = inverse * weighted - source * (inverse * inverse * inverse) * inner
    gain_grad = jnp.sum(upstream * source * inverse, axis=0, keepdims=True)
    return source_grad, gain_grad


def rotary_tables(places):
    frequencies = jnp.exp(
        jnp.arange(HD // 2, dtype=F32) * (-2.0 * math.log(ROPE_BASE) / HD)
    )
    angles = places.astype(F32)[:, None] * frequencies[None, :]
    return jnp.cos(angles), jnp.sin(angles)


def rotate(values, cosine, sine):
    front, back = values[..., : HD // 2], values[..., HD // 2 :]
    return jnp.concatenate(
        [front * cosine - back * sine, back * cosine + front * sine], axis=-1
    )


def in_order(first, mine, other):
    return jnp.where(first, mine, other), jnp.where(first, other, mine)


def on_device(
    hidden_in,
    segments,
    positions,
    out_grad,
    w_query,
    w_key,
    w_value,
    w_out,
    w_gate,
    w_up,
    w_down,
    norm_gains,
    head_gains,
):
    iy = lax.axis_index("y")
    izh = lax.axis_index("zh")
    ix = lax.axis_index("x")
    ic = lax.axis_index("core")
    izl = lax.axis_index("zl")
    ring = jnp.arange(4, dtype=jnp.int32)
    place = jnp.concatenate(
        [
            (((ring - iy) % 4)[:, None] * 2 + ((ring[:2] - izl) % 2)[None, :]).reshape(8),
            jnp.stack([ic, 1 - ic]).astype(jnp.int32),
        ]
    )

    def other_both(v):
        return lax.ppermute(v, ("zl", "zh"), [(i, 3 - i) for i in range(4)])

    def z_parts(v):
        return swap(v, "zh"), swap(v, "zl"), other_both(v)

    def join_z(v, parts):
        near = jnp.concatenate(in_order(izh == 0, v, parts[0]), axis=1)
        far = jnp.concatenate(in_order(izh == 0, parts[1], parts[2]), axis=1)
        return row_major(jnp.stack([near, far]))

    def spread_z(v):
        return join_z(v, z_parts(v))

    def sum_z(v):
        near = in_order(izh == 0, v[0, ..., :HALF], v[0, ..., HALF:])
        far = in_order(izh == 0, v[1, ..., :HALF], v[1, ..., HALF:])
        return add(near[0], swap(near[1], "zh"), swap(far[0], "zl"), other_both(far[1]))

    groups = ("y", "zl", "core")
    down_rows = jnp.concatenate(
        [w_down.reshape(16, UNITS, 36), w_out.reshape(16, 16, 36)], axis=1
    )
    down_rows = lax.all_to_all(down_rows, groups, 0, 0, tiled=True)
    down_rows = down_rows.transpose(1, 0, 2).reshape(UNITS + 16, HALF)
    gain_place = ((ix * 4 + iy) * 4 + izl * 2 + ic) * 9
    head_place = (iy * 4 + izl * 2 + ic) * 16
    gains = lax.dynamic_update_slice(
        jnp.zeros((4, D), LOW), norm_gains, (0, izh * HALF + gain_place)
    )
    heads = lax.dynamic_update_slice(jnp.zeros((2, HD), LOW), head_gains, (0, head_place))
    heads = jnp.where((izh == 0) & (ix == 0), heads, jnp.zeros((), LOW)).reshape(1, 2 * HD)
    misc = jnp.concatenate(
        [gains, jnp.pad(heads, ((0, 0), (0, D - 2 * HD))), jnp.zeros((3, D), LOW)], axis=0
    )
    misc = add(*gather_direct(misc, "x")).astype(LOW)
    pack = spread_z(
        jnp.concatenate(
            [w_key.T, w_value.T, w_query.T, down_rows[UNITS:], misc[:, :HALF], misc[:, HALF:]],
            axis=0,
        )
    )
    w_gate, w_up, down_rows, pack = lax.optimization_barrier((w_gate, w_up, down_rows, pack))
    pack = jnp.concatenate(gather_ring(pack, "y"), axis=0).reshape(1, 8, 5, 16, D)
    pair_part = jnp.concatenate([pack[:, :, :2], pack[:, :, 4:]], axis=2)
    key_weight, value_weight, misc = assemble(place, pair_part, swap(pair_part, "core"), 2)
    misc = misc[:, :HALF] + misc[:, HALF:]
    misc = jnp.concatenate([misc[:8], misc[8:]], axis=1)
    gain_rows = misc[:4]
    head_gain = misc[4, : 2 * HD].reshape(2, HD)
    head_part = pack[0, :, 2:4]
    head_first = gather_first(head_part, "x")

    stream = hidden_in.astype(F32)
    scale_one = inverse_rms(stream)
    normed_one = (stream * scale_one * gain_rows[0]).astype(LOW)
    key_raw = dot_nt(normed_one, key_weight)
    value_low = dot_nt(normed_one, value_weight).astype(LOW)
    token_start = (izh * 4 + ix) * OWN
    own_positions = lax.dynamic_slice_in_dim(positions, token_start, OWN)
    own_segments = lax.dynamic_slice_in_dim(segments, token_start, OWN)
    cosine, sine = rotary_tables(own_positions)
    key_rot, key_back = jax.vjp(
        lambda raw, gain: rotate(raw * inverse_rms(raw) * gain, cosine, sine),
        key_raw,
        head_gain[1],
    )
    pair = jnp.concatenate([key_rot.astype(LOW), value_low], axis=1)
    def pad_units(v):
        return jnp.pad(v, ((0, PADDED - UNITS), (0, 0)))

    wide_rows = row_major(
        jnp.concatenate(
            [pad_units(w_gate.T), pad_units(w_up.T), pad_units(down_rows[:UNITS])], axis=0
        )
    )
    wide_z = z_parts(wide_rows)
    pair_far, head_first, wide_z = lax.optimization_barrier((swap(pair, "zh"), head_first, wide_z))
    wide_pair = join_z(wide_rows, wide_z)
    pair = jnp.stack([pair, pair_far])
    head_part = jnp.stack(gather_second(head_part, head_first, "x"))
    pair_first, head_part = lax.optimization_barrier((gather_first(pair, "x"), head_part))
    pair = jnp.concatenate(gather_second(pair, pair_first, "x"), axis=0)
    pair, wide_first = lax.optimization_barrier((pair, gather_first(wide_pair, "y")))
    pair = pair.reshape(LEN, 2 * HD)
    keys, values = pair[:, :HD], pair[:, HD:]
    key_start = jnp.stack(
        [((izh + b) % 2 * 4 + (ix + a) % 4) * OWN for a in range(4) for b in range(2)]
    )
    key_order = (key_start[:, None] + jnp.arange(OWN, dtype=jnp.int32)[None, :]).reshape(LEN)
    key_segments = jnp.concatenate(
        [lax.dynamic_slice_in_dim(segments, key_start[k], OWN) for k in range(8)]
    )

    query_weight, out_weight = assemble(place, head_part, swap(head_part, "core"), 2)
    query_raw = jnp.concatenate(
        [dot_nt(normed_one, query_weight[h * HD : (h + 1) * HD]) for h in range(H)], axis=0
    )
    cosine_heads, sine_heads = jnp.tile(cosine, (H, 1)), jnp.tile(sine, (H, 1))
    query_norm, query_back = jax.vjp(
        lambda raw, gain: rotate(raw * inverse_rms(raw) * gain, cosine_heads, sine_heads),
        query_raw,
        head_gain[0],
    )
    query_rot = query_norm.astype(LOW)
    query_order = token_start + jnp.arange(OWN, dtype=jnp.int32)
    allowed = (own_segments[:, None] == key_segments[None, :]) & (
        query_order[:, None] >= key_order[None, :]
    )
    scores = (dot_nt(query_rot, keys) * SCALE).reshape(H, OWN, LEN)
    scores = jnp.where(allowed[None], scores, MASKED)
    exponent = jnp.exp(scores - jnp.max(scores, axis=-1, keepdims=True))
    probs = (exponent / jnp.sum(exponent, axis=-1, keepdims=True)).reshape(H * OWN, LEN)
    probs_low = probs.astype(LOW)
    context = dot_nn(probs_low, values).astype(LOW)
    context = jnp.concatenate([context[h * OWN : (h + 1) * OWN] for h in range(H)], axis=1)

    wide_rows = [part[k] for part in gather_second(wide_pair, wide_first, "y") for k in range(2)]
    gate_weight, up_weight, down_weight = (
        jnp.concatenate([part[k * PADDED : (k + 1) * PADDED] for part in wide_rows], axis=0)
        for k in range(3)
    )

    def spread_tokens(v):
        mine = jnp.concatenate(gather_ring(v, "x"), axis=0)
        return mine, swap(mine, "core")

    def sum_tokens(own, other):
        own, other = own.reshape(4, OWN, D), other.reshape(4, OWN, D)
        mine = add(own, swap(other, "core")).astype(LOW)
        return scatter_ring([mine[0], mine[1], mine[2], mine[3]], "x")

    def gated(gate, up):
        return jax.nn.gelu(gate.astype(F32), approximate=True) * up.astype(F32)

    attn_raw = dot_nn(context, out_weight)
    scale_two = inverse_rms(attn_raw)
    middle = stream + attn_raw * scale_two * gain_rows[1]
    scale_three = inverse_rms(middle)
    normed_two = (middle * scale_three * gain_rows[2]).astype(LOW)
    wide_two = spread_tokens(normed_two)
    gates = [dot_nt(tokens, gate_weight).astype(LOW) for tokens in wide_two]
    ups = [dot_nt(tokens, up_weight).astype(LOW) for tokens in wide_two]
    hidden = [gated(*pair).astype(LOW) for pair in zip(gates, ups)]
    down_raw = sum_tokens(*(dot_nn(part, down_weight).astype(LOW) for part in hidden))
    scale_four = inverse_rms(down_raw)
    result = (middle + down_raw * scale_four * gain_rows[3]).astype(LOW)
    upstream = out_grad.astype(F32)
    down_grad, gain_four = norm_backward(upstream, down_raw, scale_four, gain_rows[3])
    down_wide = spread_tokens(down_grad.astype(LOW))
    gate_low, up_low = [], []
    for tokens, gate, up in zip(down_wide, gates, ups):
        _, gated_back = jax.vjp(gated, gate.astype(F32), up.astype(F32))
        gate_grad, up_grad = gated_back(dot_nt(tokens, down_weight))
        gate_low.append(gate_grad.astype(LOW))
        up_low.append(up_grad.astype(LOW))
    normed_two_grad = sum_tokens(
        *(
            (dot_nn(gate, gate_weight) + dot_nn(up, up_weight)).astype(LOW)
            for gate, up in zip(gate_low, up_low)
        )
    )
    gate_low, up_low, hidden, wide_two, down_wide = (
        jnp.concatenate(halves, axis=0) for halves in (gate_low, up_low, hidden, wide_two, down_wide)
    )
    grad_wide = jnp.concatenate(
        [
            dot_tn(part, tokens).astype(LOW).reshape(8, PADDED, D)
            for part, tokens in ((gate_low, wide_two), (up_low, wide_two), (hidden, down_wide))
        ],
        axis=1,
    )
    grad_wide = list(grad_wide.reshape(4, 2, 3 * PADDED, D))
    own_wide, after_wide, opposite_wide, before_wide = grad_wide
    wide_first = shift(opposite_wide[:1], "y", 1), shift(opposite_wide[1:], "y", -1)
    wide_ends = shift(before_wide[:1], "y", -1), shift(after_wide[1:], "y", 1)

    middle_part, gain_three = norm_backward(normed_two_grad, middle, scale_three, gain_rows[2])
    middle_grad = upstream + middle_part
    attn_grad, gain_two = norm_backward(middle_grad, attn_raw, scale_two, gain_rows[1])
    attn_low = attn_grad.astype(LOW)
    context_grad = dot_nt(attn_low, out_weight).astype(LOW)
    context_grad = jnp.concatenate(
        [context_grad[:, h * HD : (h + 1) * HD] for h in range(H)], axis=0
    )
    prob_grad = dot_nt(context_grad, values)
    probs = probs_low.astype(F32)
    centre = jnp.sum(probs * prob_grad, axis=-1, keepdims=True)
    score_low = (probs * (prob_grad - centre)).astype(LOW)
    wide_first, score_low = lax.optimization_barrier((wide_first, score_low))
    wide_parts = (
        shift(add(after_wide[:1], wide_first[0]).astype(LOW), "y", 1),
        shift(add(before_wide[1:], wide_first[1]).astype(LOW), "y", -1),
    )
    key_part = dot_tn(score_low, query_rot) * SCALE
    value_part = dot_tn(probs_low, context_grad)
    pair_grad = jnp.concatenate([key_part, value_part], axis=1).astype(LOW)
    pair_grad = pair_grad.reshape(4, 2, OWN, 2 * HD)
    pair_grad = list(pair_grad)
    pair_first = scatter_first(pair_grad, "x")
    query_grad = dot_nn(score_low, keys) * SCALE
    query_raw_grad, query_gain = query_back(query_grad)
    query_low = query_raw_grad.astype(LOW)
    query_low = jnp.concatenate([query_low[h * OWN : (h + 1) * OWN] for h in range(H)], axis=1)
    mine, other = divide(
        place, [dot_tn(query_low, normed_one).astype(LOW), dot_tn(context, attn_low).astype(LOW)]
    )
    mine = add(mine, swap(other, "core")).astype(LOW)
    pair_first, mine, wide_ends = lax.optimization_barrier((pair_first, mine, wide_ends))
    pair_grad = scatter_second(pair_grad, pair_first, "x")
    head_rows = scatter_ring(list(mine), "x").astype(LOW)
    pair_grad = add(pair_grad[0], swap(pair_grad[1].astype(LOW), "zh"))
    pair_grad, wide_parts = lax.optimization_barrier((pair_grad, wide_parts))
    wide_pair = [
        add(own_wide[k], wide_parts[k][0], wide_ends[k][0]).astype(LOW) for k in range(2)
    ]
    wide_rows = sum_z(jnp.stack(wide_pair))
    gate_shard, up_shard = wide_rows[:UNITS].T, wide_rows[PADDED : PADDED + UNITS].T
    down_rows = wide_rows[2 * PADDED : 2 * PADDED + UNITS].astype(LOW)
    key_raw_grad, key_gain = key_back(pair_grad[:, :HD])
    key_low = key_raw_grad.astype(LOW)
    value_grad_low = pair_grad[:, HD:].astype(LOW)
    normed_one_grad = (
        dot_nn(query_low, query_weight)
        + dot_nn(key_low, key_weight)
        + dot_nn(value_grad_low, value_weight)
    )
    stream_part, gain_one = norm_backward(normed_one_grad, stream, scale_one, gain_rows[0])
    input_grad = (middle_grad + stream_part).astype(LOW)

    gains_grad = jnp.concatenate([gain_one, gain_two, gain_three, gain_four], axis=0)
    head_grad = jnp.concatenate([query_gain, key_gain]).reshape(1, 2 * HD)
    head_grad = jnp.pad(head_grad, ((0, 0), (0, HALF - 2 * HD)))
    misc = jnp.concatenate(
        [gains_grad, jnp.concatenate([head_grad, head_grad], axis=1), jnp.zeros((11, D), F32)],
        axis=0,
    )
    mine, other = divide(
        place,
        [dot_tn(key_low, normed_one).astype(LOW), dot_tn(value_grad_low, normed_one).astype(LOW)],
        misc.astype(LOW),
    )
    mine = add(mine[0], swap(other[0], "core")).astype(LOW)
    rows = jnp.concatenate([mine, head_rows], axis=1).reshape(4, 2, 5, 16, D)
    rows = sum_z(scatter_ring(list(rows), "y").astype(LOW))
    query_shard = rows[3].T
    down_rows = jnp.concatenate([down_rows, rows[4].astype(LOW)], axis=0)
    down_rows = down_rows.reshape(UNITS + 16, 16, 36).transpose(1, 0, 2)
    down_rows = lax.all_to_all(down_rows, groups, 0, 0, tiled=True).astype(F32)
    down_shard = down_rows[:, :UNITS].reshape(16 * UNITS, 36)
    out_shard = down_rows[:, UNITS:].reshape(HD, 36)
    pair_rows = add(*gather_direct(rows[:3].astype(LOW), "x"))
    key_shard, value_shard = pair_rows[0].T, pair_rows[1].T
    gains_shard = lax.dynamic_slice(pair_rows[2], (0, gain_place), (4, 9))
    head_shard = lax.dynamic_slice(
        pair_rows[2, 4, : 2 * HD].reshape(2, HD), (0, head_place), (2, 16)
    )
    return (
        result,
        input_grad,
        query_shard,
        key_shard,
        value_shard,
        out_shard,
        gate_shard,
        up_shard,
        down_shard,
        gains_shard,
        head_shard,
    )


def solution(mesh):
    split = Mesh(mesh.devices.reshape(4, 2, 2, 2, 4), ("y", "zl", "core", "zh", "x"))
    dp = ("y", "zl", "core")
    weights = (
        P("zh", ("x",) + dp),
        P("zh", dp),
        P("zh", dp),
        P("x", ("zh",) + dp),
        P("zh", ("x",) + dp),
        P("zh", ("x",) + dp),
        P("x", ("zh",) + dp),
        P(None, ("zh", "x") + dp),
        P(None, dp),
    )
    tokens = P(dp + ("zh", "x"), None)
    return jax.shard_map(
        on_device,
        mesh=split,
        in_specs=(tokens, P(dp), P(dp), tokens) + weights,
        out_specs=(tokens, tokens) + weights,
        check_vma=False,
    )
```

```python
import math

import jax
import jax.numpy as jnp
from jax import lax
from jax.experimental import pallas as pl
from jax.experimental.layout import Layout, with_layout_constraint
from jax.experimental.pallas import tpu as pltpu
from jax.sharding import Mesh, PartitionSpec as P

D = 1152
HALF = 576
H = 4
HD = 256
FF = 6912
LEN = 1216
OWN = 152
UNITS = 108
PADDED = 112
EPSILON = 1e-06
ROPE_BASE = 1000000.0
MASKED = -1e30
SCALE = HD ** (-0.5)
LOW = jnp.bfloat16
F32 = jnp.float32


def shift(v, axis, step):
    size = lax.axis_size(axis)
    return lax.ppermute(v, axis, [(i, (i + step) % size) for i in range(size)])


def swap(v, axis):
    return shift(v, axis, 1)


def gather_direct(v, axis):
    return [v, shift(v, axis, -1), shift(v, axis, -2), shift(v, axis, 1)]


def half_of(v):
    if v.ndim > 2:
        return v.shape[0] // 2
    return (v.shape[0] // 2 + 7) // 8 * 8


def gather_first(v, axis):
    return shift(v, axis, 1), shift(v, axis, -1)


def gather_second(v, first, axis):
    before, after = first
    half = half_of(v)
    opposite = jnp.concatenate(
        [shift(before[:half], axis, 1), shift(after[half:], axis, -1)], axis=0
    )
    return [v, after, opposite, before]


def gather_ring(v, axis):
    return gather_second(v, gather_first(v, axis), axis)


def add(*parts):
    total = parts[0].astype(F32)
    for part in parts[1:]:
        total = total + part.astype(F32)
    return total


def scatter_first(blocks, axis):
    _, after, opposite, before = blocks
    half = half_of(opposite)
    up = jnp.concatenate([opposite[:half], after[half:]], axis=0)
    down = jnp.concatenate([opposite[half:], before[:half]], axis=0)
    return shift(up, axis, 1), shift(down, axis, -1)


def scatter_second(blocks, first, axis):
    own, after, _, before = blocks
    up, down = first
    half, rest = half_of(own), own.shape[0] - half_of(own)
    from_before = shift(add(after[:half], up[:half]).astype(LOW), axis, 1)
    from_after = shift(add(before[half:], down[:rest]).astype(LOW), axis, -1)
    return add(
        own,
        jnp.concatenate([from_before, up[half:]], axis=0),
        jnp.concatenate([down[rest:], from_after], axis=0),
    )


def scatter_ring(blocks, axis):
    return scatter_second(blocks, scatter_first(blocks, axis), axis)


def row_major(v):
    return with_layout_constraint(v, Layout(major_to_minor=tuple(range(v.ndim))))


def whole(shape, dtype):
    return jax.ShapeDtypeStruct(shape, dtype)


VMEM = pl.BlockSpec(memory_space=pltpu.VMEM)
SMEM = pl.BlockSpec(memory_space=pltpu.SMEM)
BIG = pltpu.CompilerParams(vmem_limit_bytes=32 * 1024 * 1024)


def row_blocks(place_ref):
    for y in range(4):
        for zl in range(2):
            for side in range(2):
                row = y * 64 + zl * 32 + place_ref[8 + side] * 16
                yield side, place_ref[y * 2 + zl], pl.multiple_of(row, 16)


def assemble(place, mine, other, parts):
    heads, summed = mine.shape[0], mine.shape[2] > parts

    def kernel(place_ref, mine_ref, other_ref, *out_refs):
        for side, block, row in row_blocks(place_ref):
            ref = other_ref if side else mine_ref
            for h in range(heads):
                for part in range(parts):
                    out_refs[part][pl.ds(row + h * HD, 16), :] = ref[h, block, part]
        if summed:
            total = mine_ref[0, 0, parts].astype(F32) + other_ref[0, 0, parts].astype(F32)
            for k in range(1, 8):
                total = total + mine_ref[0, k, parts].astype(F32)
                total = total + other_ref[0, k, parts].astype(F32)
            out_refs[parts][...] = total

    shapes = [whole((heads * HD, D), LOW)] * parts + [whole((16, D), F32)] * summed
    return pl.pallas_call(
        kernel,
        out_shape=shapes,
        in_specs=[SMEM, VMEM, VMEM],
        out_specs=[VMEM] * len(shapes),
        compiler_params=BIG,
    )(place, mine, other)


def divide(place, grads, everywhere=None):
    heads, parts = grads[0].shape[0] // HD, len(grads)
    given = list(grads) + ([] if everywhere is None else [everywhere])

    def kernel(place_ref, *refs):
        grad_refs, (mine_ref, other_ref) = refs[: len(given)], refs[len(given) :]
        for side, block, row in row_blocks(place_ref):
            ref = other_ref if side else mine_ref
            for h in range(heads):
                for part in range(parts):
                    ref[h, block, part] = grad_refs[part][pl.ds(row + h * HD, 16), :]
            if everywhere is not None:
                ref[0, block, parts] = grad_refs[parts][...]

    return pl.pallas_call(
        kernel,
        out_shape=(whole((heads, 8, len(given), 16, D), LOW),) * 2,
        in_specs=[SMEM] + [VMEM] * len(given),
        out_specs=(VMEM, VMEM),
        compiler_params=BIG,
    )(place, *given)


def dot_nt(a, b):
    return lax.dot_general(a, b, (((1,), (1,)), ((), ())), preferred_element_type=F32)


def dot_nn(a, b):
    return lax.dot_general(a, b, (((1,), (0,)), ((), ())), preferred_element_type=F32)


def dot_tn(a, b):
    return lax.dot_general(a, b, (((0,), (0,)), ((), ())), preferred_element_type=F32)


def inverse_rms(values):
    return lax.rsqrt(jnp.mean(values * values, axis=-1, keepdims=True) + EPSILON)


def norm_backward(upstream, source, inverse, gain_row):
    weighted = upstream * gain_row
    inner = jnp.mean(weighted * source, axis=-1, keepdims=True)
    source_grad = inverse * weighted - source * (inverse * inverse * inverse) * inner
    gain_grad = jnp.sum(upstream * source * inverse, axis=0, keepdims=True)
    return source_grad, gain_grad


def rotary_tables(places):
    frequencies = jnp.exp(
        jnp.arange(HD // 2, dtype=F32) * (-2.0 * math.log(ROPE_BASE) / HD)
    )
    angles = places.astype(F32)[:, None] * frequencies[None, :]
    return jnp.cos(angles), jnp.sin(angles)


def rotate(values, cosine, sine):
    front, back = values[..., : HD // 2], values[..., HD // 2 :]
    return jnp.concatenate(
        [front * cosine - back * sine, back * cosine + front * sine], axis=-1
    )


def in_order(first, mine, other):
    return jnp.where(first, mine, other), jnp.where(first, other, mine)


def on_device(
    hidden_in,
    segments,
    positions,
    out_grad,
    w_query,
    w_key,
    w_value,
    w_out,
    w_gate,
    w_up,
    w_down,
    norm_gains,
    head_gains,
):
    iy = lax.axis_index("y")
    izh = lax.axis_index("zh")
    ix = lax.axis_index("x")
    ic = lax.axis_index("core")
    izl = lax.axis_index("zl")
    ring = jnp.arange(4, dtype=jnp.int32)
    place = jnp.concatenate(
        [
            (((ring - iy) % 4)[:, None] * 2 + ((ring[:2] - izl) % 2)[None, :]).reshape(8),
            jnp.stack([ic, 1 - ic]).astype(jnp.int32),
        ]
    )

    def other_both(v):
        return lax.ppermute(v, ("zl", "zh"), [(i, 3 - i) for i in range(4)])

    def spread_z(v):
        near = jnp.concatenate(in_order(izh == 0, v, swap(v, "zh")), axis=1)
        far = jnp.concatenate(in_order(izh == 0, swap(v, "zl"), other_both(v)), axis=1)
        return row_major(jnp.stack([near, far]))

    def sum_z(v):
        near = in_order(izh == 0, v[0, ..., :HALF], v[0, ..., HALF:])
        far = in_order(izh == 0, v[1, ..., :HALF], v[1, ..., HALF:])
        return add(near[0], swap(near[1], "zh"), swap(far[0], "zl"), other_both(far[1]))

    groups = ("y", "zl", "core")
    down_rows = jnp.concatenate(
        [w_down.reshape(16, UNITS, 36), w_out.reshape(16, 16, 36)], axis=1
    )
    down_rows = lax.all_to_all(down_rows, groups, 0, 0, tiled=True)
    down_rows = down_rows.transpose(1, 0, 2).reshape(UNITS + 16, HALF)
    gain_place = ((ix * 4 + iy) * 4 + izl * 2 + ic) * 9
    head_place = (iy * 4 + izl * 2 + ic) * 16
    gains = lax.dynamic_update_slice(
        jnp.zeros((4, D), LOW), norm_gains, (0, izh * HALF + gain_place)
    )
    heads = lax.dynamic_update_slice(jnp.zeros((2, HD), LOW), head_gains, (0, head_place))
    heads = jnp.where((izh == 0) & (ix == 0), heads, jnp.zeros((), LOW)).reshape(1, 2 * HD)
    misc = jnp.concatenate(
        [gains, jnp.pad(heads, ((0, 0), (0, D - 2 * HD))), jnp.zeros((3, D), LOW)], axis=0
    )
    misc = add(*gather_direct(misc, "x")).astype(LOW)
    pack = spread_z(
        jnp.concatenate(
            [w_key.T, w_value.T, w_query.T, down_rows[UNITS:], misc[:, :HALF], misc[:, HALF:]],
            axis=0,
        )
    )
    w_gate, w_up, down_rows, pack = lax.optimization_barrier((w_gate, w_up, down_rows, pack))
    pack = jnp.concatenate(gather_ring(pack, "y"), axis=0).reshape(1, 8, 5, 16, D)
    pair_part = jnp.concatenate([pack[:, :, :2], pack[:, :, 4:]], axis=2)
    key_weight, value_weight, misc = assemble(place, pair_part, swap(pair_part, "core"), 2)
    misc = misc[:, :HALF] + misc[:, HALF:]
    misc = jnp.concatenate([misc[:8], misc[8:]], axis=1)
    gain_rows = misc[:4]
    head_gain = misc[4, : 2 * HD].reshape(2, HD)
    head_part = pack[0, :, 2:4]
    head_first = gather_first(head_part, "x")

    stream = hidden_in.astype(F32)
    scale_one = inverse_rms(stream)
    normed_one = (stream * scale_one * gain_rows[0]).astype(LOW)
    key_raw = dot_nt(normed_one, key_weight)
    value_low = dot_nt(normed_one, value_weight).astype(LOW)
    token_start = (izh * 4 + ix) * OWN
    own_positions = lax.dynamic_slice_in_dim(positions, token_start, OWN)
    own_segments = lax.dynamic_slice_in_dim(segments, token_start, OWN)
    cosine, sine = rotary_tables(own_positions)
    key_rot, key_back = jax.vjp(
        lambda raw, gain: rotate(raw * inverse_rms(raw) * gain, cosine, sine),
        key_raw,
        head_gain[1],
    )
    pair = jnp.concatenate([key_rot.astype(LOW), value_low], axis=1)
    pair_far, head_first = lax.optimization_barrier((swap(pair, "zh"), head_first))
    pair = jnp.stack([pair, pair_far])
    pair = jnp.concatenate(gather_ring(pair, "x"), axis=0)
    pair = pair.reshape(LEN, 2 * HD)
    keys, values = pair[:, :HD], pair[:, HD:]
    key_start = jnp.stack(
        [((izh + b) % 2 * 4 + (ix + a) % 4) * OWN for a in range(4) for b in range(2)]
    )
    key_order = (key_start[:, None] + jnp.arange(OWN, dtype=jnp.int32)[None, :]).reshape(LEN)
    key_segments = jnp.concatenate(
        [lax.dynamic_slice_in_dim(segments, key_start[k], OWN) for k in range(8)]
    )

    head_part = jnp.stack(gather_second(head_part, head_first, "x"))
    query_weight, out_weight = assemble(place, head_part, swap(head_part, "core"), 2)
    query_raw = jnp.concatenate(
        [dot_nt(normed_one, query_weight[h * HD : (h + 1) * HD]) for h in range(H)], axis=0
    )
    cosine_heads, sine_heads = jnp.tile(cosine, (H, 1)), jnp.tile(sine, (H, 1))
    query_norm, query_back = jax.vjp(
        lambda raw, gain: rotate(raw * inverse_rms(raw) * gain, cosine_heads, sine_heads),
        query_raw,
        head_gain[0],
    )
    query_rot = query_norm.astype(LOW)
    query_order = token_start + jnp.arange(OWN, dtype=jnp.int32)
    allowed = (own_segments[:, None] == key_segments[None, :]) & (
        query_order[:, None] >= key_order[None, :]
    )
    scores = (dot_nt(query_rot, keys) * SCALE).reshape(H, OWN, LEN)
    scores = jnp.where(allowed[None], scores, MASKED)
    exponent = jnp.exp(scores - jnp.max(scores, axis=-1, keepdims=True))
    probs = (exponent / jnp.sum(exponent, axis=-1, keepdims=True)).reshape(H * OWN, LEN)
    probs_low = probs.astype(LOW)
    context = dot_nn(probs_low, values).astype(LOW)
    context = jnp.concatenate([context[h * OWN : (h + 1) * OWN] for h in range(H)], axis=1)

    def pad_units(v):
        return jnp.pad(v, ((0, PADDED - UNITS), (0, 0)))

    wide_rows = row_major(
        jnp.concatenate(
            [pad_units(w_gate.T), pad_units(w_up.T), pad_units(down_rows[:UNITS])], axis=0
        )
    )
    wide_pair = spread_z(wide_rows)
    wide_first = gather_first(wide_pair, "y")
    wide_first, context = lax.optimization_barrier((wide_first, context))
    wide_rows = [part[k] for part in gather_second(wide_pair, wide_first, "y") for k in range(2)]
    gate_weight, up_weight, down_weight = (
        jnp.concatenate([part[k * PADDED : (k + 1) * PADDED] for part in wide_rows], axis=0)
        for k in range(3)
    )

    def spread_tokens(v):
        mine = jnp.concatenate(gather_ring(v, "x"), axis=0)
        return mine, swap(mine, "core")

    def sum_tokens(own, other):
        own, other = own.reshape(4, OWN, D), other.reshape(4, OWN, D)
        mine = add(own, swap(other, "core")).astype(LOW)
        return scatter_ring([mine[0], mine[1], mine[2], mine[3]], "x")

    def gated(gate, up):
        return jax.nn.gelu(gate.astype(F32), approximate=True) * up.astype(F32)

    attn_raw = dot_nn(context, out_weight)
    scale_two = inverse_rms(attn_raw)
    middle = stream + attn_raw * scale_two * gain_rows[1]
    scale_three = inverse_rms(middle)
    normed_two = (middle * scale_three * gain_rows[2]).astype(LOW)
    wide_two = spread_tokens(normed_two)
    gates = [dot_nt(tokens, gate_weight).astype(LOW) for tokens in wide_two]
    ups = [dot_nt(tokens, up_weight).astype(LOW) for tokens in wide_two]
    hidden = [gated(*pair).astype(LOW) for pair in zip(gates, ups)]
    down_raw = sum_tokens(*(dot_nn(part, down_weight).astype(LOW) for part in hidden))
    scale_four = inverse_rms(down_raw)
    result = (middle + down_raw * scale_four * gain_rows[3]).astype(LOW)
    upstream = out_grad.astype(F32)
    down_grad, gain_four = norm_backward(upstream, down_raw, scale_four, gain_rows[3])
    down_wide = spread_tokens(down_grad.astype(LOW))
    gate_low, up_low = [], []
    for tokens, gate, up in zip(down_wide, gates, ups):
        _, gated_back = jax.vjp(gated, gate.astype(F32), up.astype(F32))
        gate_grad, up_grad = gated_back(dot_nt(tokens, down_weight))
        gate_low.append(gate_grad.astype(LOW))
        up_low.append(up_grad.astype(LOW))
    normed_two_grad = sum_tokens(
        *(
            (dot_nn(gate, gate_weight) + dot_nn(up, up_weight)).astype(LOW)
            for gate, up in zip(gate_low, up_low)
        )
    )
    gate_low, up_low, hidden, wide_two, down_wide = (
        jnp.concatenate(halves, axis=0) for halves in (gate_low, up_low, hidden, wide_two, down_wide)
    )
    grad_wide = jnp.concatenate(
        [
            dot_tn(part, tokens).astype(LOW).reshape(8, PADDED, D)
            for part, tokens in ((gate_low, wide_two), (up_low, wide_two), (hidden, down_wide))
        ],
        axis=1,
    )
    grad_wide = list(grad_wide.reshape(4, 2, 3 * PADDED, D))
    own_wide, after_wide, opposite_wide, before_wide = grad_wide
    wide_first = shift(opposite_wide[:1], "y", 1), shift(opposite_wide[1:], "y", -1)
    wide_ends = shift(before_wide[:1], "y", -1), shift(after_wide[1:], "y", 1)

    middle_part, gain_three = norm_backward(normed_two_grad, middle, scale_three, gain_rows[2])
    middle_grad = upstream + middle_part
    attn_grad, gain_two = norm_backward(middle_grad, attn_raw, scale_two, gain_rows[1])
    attn_low = attn_grad.astype(LOW)
    context_grad = dot_nt(attn_low, out_weight).astype(LOW)
    context_grad = jnp.concatenate(
        [context_grad[:, h * HD : (h + 1) * HD] for h in range(H)], axis=0
    )
    prob_grad = dot_nt(context_grad, values)
    probs = probs_low.astype(F32)
    centre = jnp.sum(probs * prob_grad, axis=-1, keepdims=True)
    score_low = (probs * (prob_grad - centre)).astype(LOW)
    wide_first, score_low = lax.optimization_barrier((wide_first, score_low))
    wide_parts = (
        shift(add(after_wide[:1], wide_first[0]).astype(LOW), "y", 1),
        shift(add(before_wide[1:], wide_first[1]).astype(LOW), "y", -1),
    )
    key_part = dot_tn(score_low, query_rot) * SCALE
    value_part = dot_tn(probs_low, context_grad)
    pair_grad = jnp.concatenate([key_part, value_part], axis=1).astype(LOW)
    pair_grad = pair_grad.reshape(4, 2, OWN, 2 * HD)
    pair_grad = list(pair_grad)
    pair_first = scatter_first(pair_grad, "x")
    query_grad = dot_nn(score_low, keys) * SCALE
    query_raw_grad, query_gain = query_back(query_grad)
    query_low = query_raw_grad.astype(LOW)
    query_low = jnp.concatenate([query_low[h * OWN : (h + 1) * OWN] for h in range(H)], axis=1)
    mine, other = divide(
        place, [dot_tn(query_low, normed_one).astype(LOW), dot_tn(context, attn_low).astype(LOW)]
    )
    mine = add(mine, swap(other, "core")).astype(LOW)
    pair_first, mine, wide_ends = lax.optimization_barrier((pair_first, mine, wide_ends))
    pair_grad = scatter_second(pair_grad, pair_first, "x")
    head_rows = scatter_ring(list(mine), "x").astype(LOW)
    pair_far = swap(pair_grad[1].astype(LOW), "zh")
    pair_far, head_rows = lax.optimization_barrier((pair_far, head_rows))
    pair_grad = add(pair_grad[0], pair_far)
    pair_grad, wide_parts = lax.optimization_barrier((pair_grad, wide_parts))
    wide_pair = [
        add(own_wide[k], wide_parts[k][0], wide_ends[k][0]).astype(LOW) for k in range(2)
    ]
    wide_rows = sum_z(jnp.stack(wide_pair))
    gate_shard, up_shard = wide_rows[:UNITS].T, wide_rows[PADDED : PADDED + UNITS].T
    down_rows = wide_rows[2 * PADDED : 2 * PADDED + UNITS].astype(LOW)
    key_raw_grad, key_gain = key_back(pair_grad[:, :HD])
    key_low = key_raw_grad.astype(LOW)
    value_grad_low = pair_grad[:, HD:].astype(LOW)
    normed_one_grad = (
        dot_nn(query_low, query_weight)
        + dot_nn(key_low, key_weight)
        + dot_nn(value_grad_low, value_weight)
    )
    stream_part, gain_one = norm_backward(normed_one_grad, stream, scale_one, gain_rows[0])
    input_grad = (middle_grad + stream_part).astype(LOW)

    gains_grad = jnp.concatenate([gain_one, gain_two, gain_three, gain_four], axis=0)
    head_grad = jnp.concatenate([query_gain, key_gain]).reshape(1, 2 * HD)
    head_grad = jnp.pad(head_grad, ((0, 0), (0, HALF - 2 * HD)))
    misc = jnp.concatenate(
        [gains_grad, jnp.concatenate([head_grad, head_grad], axis=1), jnp.zeros((11, D), F32)],
        axis=0,
    )
    mine, other = divide(
        place,
        [dot_tn(key_low, normed_one).astype(LOW), dot_tn(value_grad_low, normed_one).astype(LOW)],
        misc.astype(LOW),
    )
    mine = add(mine[0], swap(other[0], "core")).astype(LOW)
    rows = jnp.concatenate([mine, head_rows], axis=1).reshape(4, 2, 5, 16, D)
    rows = sum_z(scatter_ring(list(rows), "y").astype(LOW))
    query_shard = rows[3].T
    down_rows = jnp.concatenate([down_rows, rows[4].astype(LOW)], axis=0)
    down_rows = down_rows.reshape(UNITS + 16, 16, 36).transpose(1, 0, 2)
    down_rows = lax.all_to_all(down_rows, groups, 0, 0, tiled=True).astype(F32)
    down_shard = down_rows[:, :UNITS].reshape(16 * UNITS, 36)
    out_shard = down_rows[:, UNITS:].reshape(HD, 36)
    pair_rows = add(*gather_direct(rows[:3].astype(LOW), "x"))
    key_shard, value_shard = pair_rows[0].T, pair_rows[1].T
    gains_shard = lax.dynamic_slice(pair_rows[2], (0, gain_place), (4, 9))
    head_shard = lax.dynamic_slice(
        pair_rows[2, 4, : 2 * HD].reshape(2, HD), (0, head_place), (2, 16)
    )
    return (
        result,
        input_grad,
        query_shard,
        key_shard,
        value_shard,
        out_shard,
        gate_shard,
        up_shard,
        down_shard,
        gains_shard,
        head_shard,
    )


def solution(mesh):
    split = Mesh(mesh.devices.reshape(4, 2, 2, 2, 4), ("y", "zl", "core", "zh", "x"))
    dp = ("y", "zl", "core")
    weights = (
        P("zh", ("x",) + dp),
        P("zh", dp),
        P("zh", dp),
        P("x", ("zh",) + dp),
        P("zh", ("x",) + dp),
        P("zh", ("x",) + dp),
        P("x", ("zh",) + dp),
        P(None, ("zh", "x") + dp),
        P(None, dp),
    )
    tokens = P(dp + ("zh", "x"), None)
    return jax.shard_map(
        on_device,
        mesh=split,
        in_specs=(tokens, P(dp), P(dp), tokens) + weights,
        out_specs=(tokens, tokens) + weights,
        check_vma=False,
    )
```

```python
import math

import jax
import jax.numpy as jnp
from jax import lax
from jax.experimental import pallas as pl
from jax.experimental.layout import Layout, with_layout_constraint
from jax.experimental.pallas import tpu as pltpu
from jax.sharding import Mesh, PartitionSpec as P

D = 1152
HALF = 576
H = 4
HD = 256
FF = 6912
LEN = 1216
OWN = 152
UNITS = 108
PADDED = 112
EPSILON = 1e-06
ROPE_BASE = 1000000.0
MASKED = -1e30
SCALE = HD ** (-0.5)
LOW = jnp.bfloat16
F32 = jnp.float32


def shift(v, axis, step):
    size = lax.axis_size(axis)
    return lax.ppermute(v, axis, [(i, (i + step) % size) for i in range(size)])


def swap(v, axis):
    return shift(v, axis, 1)


def gather_direct(v, axis):
    return [v, shift(v, axis, -1), shift(v, axis, -2), shift(v, axis, 1)]


def shift_z(v, step):
    own = [(z % 2) * 2 + z // 2 for z in range(4)]
    return lax.ppermute(v, ("zl", "zh"), [(own[z], own[(z + step) % 4]) for z in range(4)])


def half_of(v):
    if v.ndim > 2:
        return v.shape[0] // 2
    return (v.shape[0] // 2 + 7) // 8 * 8


def gather_first(v, axis):
    return shift(v, axis, 1), shift(v, axis, -1)


def gather_second(v, first, axis):
    before, after = first
    half = half_of(v)
    opposite = jnp.concatenate(
        [shift(before[:half], axis, 1), shift(after[half:], axis, -1)], axis=0
    )
    return [v, after, opposite, before]


def gather_ring(v, axis):
    return gather_second(v, gather_first(v, axis), axis)


def add(*parts):
    total = parts[0].astype(F32)
    for part in parts[1:]:
        total = total + part.astype(F32)
    return total


def scatter_first(blocks, axis):
    opposite = blocks[2]
    half = half_of(opposite)
    return shift(opposite[:half], axis, 1), shift(opposite[half:], axis, -1)


def scatter_parts(blocks, first, axis):
    own, after, _, before = blocks
    passed_up, passed_down = first
    half = half_of(own)
    up = jnp.concatenate([add(after[:half], passed_up).astype(LOW), after[half:]], axis=0)
    down = jnp.concatenate([before[:half], add(before[half:], passed_down).astype(LOW)], axis=0)
    return own, shift(up, axis, 1), shift(down, axis, -1)


def scatter_ring(blocks, axis):
    return add(*scatter_parts(blocks, scatter_first(blocks, axis), axis))


def scatter_both(blocks, axis):
    own, after, opposite, before = blocks
    half, rest = half_of(own), own.shape[0] - half_of(own)
    up = shift(jnp.concatenate([opposite[:half], after[half:]], axis=0), axis, 1)
    down = shift(jnp.concatenate([opposite[half:], before[:half]], axis=0), axis, -1)
    from_before = shift(add(after[:half], up[:half]).astype(LOW), axis, 1)
    from_after = shift(add(before[half:], down[:rest]).astype(LOW), axis, -1)
    return add(
        own,
        jnp.concatenate([from_before, up[half:]], axis=0),
        jnp.concatenate([down[rest:], from_after], axis=0),
    )


def row_major(v):
    return with_layout_constraint(v, Layout(major_to_minor=tuple(range(v.ndim))))


def whole(shape, dtype):
    return jax.ShapeDtypeStruct(shape, dtype)


VMEM = pl.BlockSpec(memory_space=pltpu.VMEM)
SMEM = pl.BlockSpec(memory_space=pltpu.SMEM)
BIG = pltpu.CompilerParams(vmem_limit_bytes=32 * 1024 * 1024)


def row_blocks(place_ref):
    for y in range(4):
        for zl in range(2):
            for side in range(2):
                row = y * 64 + zl * 32 + place_ref[8 + side] * 16
                yield side, place_ref[y * 2 + zl], pl.multiple_of(row, 16)


def assemble(place, mine, other, parts):
    heads, summed = mine.shape[0], mine.shape[2] > parts

    def kernel(place_ref, mine_ref, other_ref, *out_refs):
        for side, block, row in row_blocks(place_ref):
            ref = other_ref if side else mine_ref
            for h in range(heads):
                for part in range(parts):
                    out_refs[part][pl.ds(row + h * HD, 16), :] = ref[h, block, part]
        if summed:
            total = mine_ref[0, 0, parts].astype(F32) + other_ref[0, 0, parts].astype(F32)
            for k in range(1, 8):
                total = total + mine_ref[0, k, parts].astype(F32)
                total = total + other_ref[0, k, parts].astype(F32)
            out_refs[parts][...] = total

    shapes = [whole((heads * HD, D), LOW)] * parts + [whole((16, D), F32)] * summed
    return pl.pallas_call(
        kernel,
        out_shape=shapes,
        in_specs=[SMEM, VMEM, VMEM],
        out_specs=[VMEM] * len(shapes),
        compiler_params=BIG,
    )(place, mine, other)


def divide(place, grads, everywhere=None):
    heads, parts = grads[0].shape[0] // HD, len(grads)
    given = list(grads) + ([] if everywhere is None else [everywhere])

    def kernel(place_ref, *refs):
        grad_refs, (mine_ref, other_ref) = refs[: len(given)], refs[len(given) :]
        for side, block, row in row_blocks(place_ref):
            ref = other_ref if side else mine_ref
            for h in range(heads):
                for part in range(parts):
                    ref[h, block, part] = grad_refs[part][pl.ds(row + h * HD, 16), :]
            if everywhere is not None:
                ref[0, block, parts] = grad_refs[parts][...]

    return pl.pallas_call(
        kernel,
        out_shape=(whole((heads, 8, len(given), 16, D), LOW),) * 2,
        in_specs=[SMEM] + [VMEM] * len(given),
        out_specs=(VMEM, VMEM),
        compiler_params=BIG,
    )(place, *given)


def dot_nt(a, b):
    return lax.dot_general(a, b, (((1,), (1,)), ((), ())), preferred_element_type=F32)


def dot_nn(a, b):
    return lax.dot_general(a, b, (((1,), (0,)), ((), ())), preferred_element_type=F32)


def dot_tn(a, b):
    return lax.dot_general(a, b, (((0,), (0,)), ((), ())), preferred_element_type=F32)


def inverse_rms(values):
    return lax.rsqrt(jnp.mean(values * values, axis=-1, keepdims=True) + EPSILON)


def norm_backward(upstream, source, inverse, gain_row):
    weighted = upstream * gain_row
    inner = jnp.mean(weighted * source, axis=-1, keepdims=True)
    source_grad = inverse * weighted - source * (inverse * inverse * inverse) * inner
    gain_grad = jnp.sum(upstream * source * inverse, axis=0, keepdims=True)
    return source_grad, gain_grad


def rotary_tables(places):
    frequencies = jnp.exp(
        jnp.arange(HD // 2, dtype=F32) * (-2.0 * math.log(ROPE_BASE) / HD)
    )
    angles = places.astype(F32)[:, None] * frequencies[None, :]
    return jnp.cos(angles), jnp.sin(angles)


def rotate(values, cosine, sine):
    front, back = values[..., : HD // 2], values[..., HD // 2 :]
    return jnp.concatenate(
        [front * cosine - back * sine, back * cosine + front * sine], axis=-1
    )


def in_order(first, mine, other):
    return jnp.where(first, mine, other), jnp.where(first, other, mine)


def on_device(
    hidden_in,
    segments,
    positions,
    out_grad,
    w_query,
    w_key,
    w_value,
    w_out,
    w_gate,
    w_up,
    w_down,
    norm_gains,
    head_gains,
):
    iy = lax.axis_index("y")
    izh = lax.axis_index("zh")
    ix = lax.axis_index("x")
    ic = lax.axis_index("core")
    izl = lax.axis_index("zl")
    ring = jnp.arange(4, dtype=jnp.int32)
    place = jnp.concatenate(
        [
            (((ring - iy) % 4)[:, None] * 2 + ((ring[:2] - izl) % 2)[None, :]).reshape(8),
            jnp.stack([ic, 1 - ic]).astype(jnp.int32),
        ]
    )

    def other_both(v):
        return lax.ppermute(v, ("zl", "zh"), [(i, 3 - i) for i in range(4)])

    def spread_z(v):
        near = jnp.concatenate(in_order(izh == 0, v, swap(v, "zh")), axis=1)
        far = jnp.concatenate(in_order(izh == 0, swap(v, "zl"), other_both(v)), axis=1)
        return row_major(jnp.stack([near, far]))

    def ring_z_second(first):
        before, after = first
        half = half_of(before)
        return shift_z(before[:half], 1), shift_z(after[half:], -1)

    def ring_z_last(v, first, second):
        before, after = first
        opposite = jnp.concatenate(second, axis=0)
        even = izl == 0
        near_z, far_z = jnp.where(even, after, before), jnp.where(even, before, after)
        near = jnp.concatenate(in_order(izh == 0, v, opposite), axis=1)
        far = jnp.concatenate(in_order(izh == 0, near_z, far_z), axis=1)
        return row_major(near[None]), row_major(far[None])

    def sum_z(v):
        near = in_order(izh == 0, v[0, ..., :HALF], v[0, ..., HALF:])
        far = in_order(izh == 0, v[1, ..., :HALF], v[1, ..., HALF:])
        return add(near[0], swap(near[1], "zh"), swap(far[0], "zl"), other_both(far[1]))

    groups = ("y", "zl", "core")
    down_rows = jnp.concatenate(
        [w_down.reshape(16, UNITS, 36), w_out.reshape(16, 16, 36)], axis=1
    )
    down_rows = lax.all_to_all(down_rows, groups, 0, 0, tiled=True)
    down_rows = down_rows.transpose(1, 0, 2).reshape(UNITS + 16, HALF)
    gain_place = ((ix * 4 + iy) * 4 + izl * 2 + ic) * 9
    head_place = (iy * 4 + izl * 2 + ic) * 16
    gains = lax.dynamic_update_slice(
        jnp.zeros((4, D), LOW), norm_gains, (0, izh * HALF + gain_place)
    )
    heads = lax.dynamic_update_slice(jnp.zeros((2, HD), LOW), head_gains, (0, head_place))
    heads = jnp.where((izh == 0) & (ix == 0), heads, jnp.zeros((), LOW)).reshape(1, 2 * HD)
    misc = jnp.concatenate(
        [gains, jnp.pad(heads, ((0, 0), (0, D - 2 * HD))), jnp.zeros((3, D), LOW)], axis=0
    )
    misc = add(*gather_direct(misc, "x")).astype(LOW)
    pack = spread_z(
        jnp.concatenate(
            [w_key.T, w_value.T, w_query.T, down_rows[UNITS:], misc[:, :HALF], misc[:, HALF:]],
            axis=0,
        )
    )
    w_gate, w_up, down_rows, pack = lax.optimization_barrier((w_gate, w_up, down_rows, pack))
    def pad_units(v):
        return jnp.pad(v, ((0, PADDED - UNITS), (0, 0)))

    wide_rows = row_major(
        jnp.concatenate(
            [pad_units(w_gate.T), pad_units(w_up.T), pad_units(down_rows[:UNITS])], axis=0
        )
    )
    wide_z = shift_z(wide_rows, 1), shift_z(wide_rows, -1)
    pack_first = gather_first(pack, "y")
    pack_first, wide_z = lax.optimization_barrier((pack_first, wide_z))
    wide_second = ring_z_second(wide_z)
    pack = jnp.concatenate(gather_second(pack, pack_first, "y"), axis=0).reshape(1, 8, 5, 16, D)
    pair_part = jnp.concatenate([pack[:, :, :2], pack[:, :, 4:]], axis=2)
    key_weight, value_weight, misc = assemble(place, pair_part, swap(pair_part, "core"), 2)
    misc = misc[:, :HALF] + misc[:, HALF:]
    misc = jnp.concatenate([misc[:8], misc[8:]], axis=1)
    gain_rows = misc[:4]
    head_gain = misc[4, : 2 * HD].reshape(2, HD)
    head_part = pack[0, :, 2:4]
    head_first = gather_first(head_part, "x")

    stream = hidden_in.astype(F32)
    scale_one = inverse_rms(stream)
    normed_one = (stream * scale_one * gain_rows[0]).astype(LOW)
    key_raw = dot_nt(normed_one, key_weight)
    value_low = dot_nt(normed_one, value_weight).astype(LOW)
    token_start = (izh * 4 + ix) * OWN
    own_positions = lax.dynamic_slice_in_dim(positions, token_start, OWN)
    own_segments = lax.dynamic_slice_in_dim(segments, token_start, OWN)
    cosine, sine = rotary_tables(own_positions)
    key_rot, key_back = jax.vjp(
        lambda raw, gain: rotate(raw * inverse_rms(raw) * gain, cosine, sine),
        key_raw,
        head_gain[1],
    )
    pair = jnp.concatenate([key_rot.astype(LOW), value_low], axis=1)
    pair_far, head_first, wide_second = lax.optimization_barrier(
        (swap(pair, "zh"), head_first, wide_second)
    )
    near, far = ring_z_last(wide_rows, wide_z, wide_second)
    pair = jnp.stack([pair, pair_far])
    head_part = jnp.stack(gather_second(head_part, head_first, "x"))
    pair_first, head_part, near_first, far = lax.optimization_barrier(
        (gather_first(pair, "x"), head_part, gather_first(near, "y"), far)
    )
    pair = jnp.concatenate(gather_second(pair, pair_first, "x"), axis=0)
    pair = pair.reshape(LEN, 2 * HD)
    keys, values = pair[:, :HD], pair[:, HD:]
    key_start = jnp.stack(
        [((izh + b) % 2 * 4 + (ix + a) % 4) * OWN for a in range(4) for b in range(2)]
    )
    key_order = (key_start[:, None] + jnp.arange(OWN, dtype=jnp.int32)[None, :]).reshape(LEN)
    key_segments = jnp.concatenate(
        [lax.dynamic_slice_in_dim(segments, key_start[k], OWN) for k in range(8)]
    )

    query_weight, out_weight = assemble(place, head_part, swap(head_part, "core"), 2)
    query_raw = jnp.concatenate(
        [dot_nt(normed_one, query_weight[h * HD : (h + 1) * HD]) for h in range(H)], axis=0
    )
    cosine_heads, sine_heads = jnp.tile(cosine, (H, 1)), jnp.tile(sine, (H, 1))
    query_norm, query_back = jax.vjp(
        lambda raw, gain: rotate(raw * inverse_rms(raw) * gain, cosine_heads, sine_heads),
        query_raw,
        head_gain[0],
    )
    query_rot = query_norm.astype(LOW)
    query_order = token_start + jnp.arange(OWN, dtype=jnp.int32)
    allowed = (own_segments[:, None] == key_segments[None, :]) & (
        query_order[:, None] >= key_order[None, :]
    )
    scores = (dot_nt(query_rot, keys) * SCALE).reshape(H, OWN, LEN)
    scores = jnp.where(allowed[None], scores, MASKED)
    exponent = jnp.exp(scores - jnp.max(scores, axis=-1, keepdims=True))
    probs = (exponent / jnp.sum(exponent, axis=-1, keepdims=True)).reshape(H * OWN, LEN)
    probs_low = probs.astype(LOW)
    context = dot_nn(probs_low, values).astype(LOW)
    context = jnp.concatenate([context[h * OWN : (h + 1) * OWN] for h in range(H)], axis=1)

    far_first, context = lax.optimization_barrier((gather_first(far, "y"), context))
    opposite = shift(near_first[0], "y", 1), shift(far_first[1], "y", -1)
    wide_rows = [near, far, near_first[1], far_first[1], *opposite, near_first[0], far_first[0]]
    gate_weight, up_weight, down_weight = (
        jnp.concatenate([part[0, k * PADDED : (k + 1) * PADDED] for part in wide_rows], axis=0)
        for k in range(3)
    )

    def spread_tokens(v):
        mine = jnp.concatenate(gather_ring(v, "x"), axis=0)
        return mine, swap(mine, "core")

    def sum_tokens(own, other):
        own, other = own.reshape(4, OWN, D), other.reshape(4, OWN, D)
        mine = add(own, swap(other, "core")).astype(LOW)
        return scatter_both([mine[0], mine[1], mine[2], mine[3]], "x")

    def gated(gate, up):
        return jax.nn.gelu(gate.astype(F32), approximate=True) * up.astype(F32)

    attn_raw = dot_nn(context, out_weight)
    scale_two = inverse_rms(attn_raw)
    middle = stream + attn_raw * scale_two * gain_rows[1]
    scale_three = inverse_rms(middle)
    normed_two = (middle * scale_three * gain_rows[2]).astype(LOW)
    wide_two = spread_tokens(normed_two)
    gates = [dot_nt(tokens, gate_weight).astype(LOW) for tokens in wide_two]
    ups = [dot_nt(tokens, up_weight).astype(LOW) for tokens in wide_two]
    hidden = [gated(*pair).astype(LOW) for pair in zip(gates, ups)]
    down_raw = sum_tokens(*(dot_nn(part, down_weight).astype(LOW) for part in hidden))
    scale_four = inverse_rms(down_raw)
    result = (middle + down_raw * scale_four * gain_rows[3]).astype(LOW)
    upstream = out_grad.astype(F32)
    down_grad, gain_four = norm_backward(upstream, down_raw, scale_four, gain_rows[3])
    down_wide = spread_tokens(down_grad.astype(LOW))
    gate_low, up_low = [], []
    for tokens, gate, up in zip(down_wide, gates, ups):
        _, gated_back = jax.vjp(gated, gate.astype(F32), up.astype(F32))
        gate_grad, up_grad = gated_back(dot_nt(tokens, down_weight))
        gate_low.append(gate_grad.astype(LOW))
        up_low.append(up_grad.astype(LOW))
    normed_two_grad = sum_tokens(
        *(
            (dot_nn(gate, gate_weight) + dot_nn(up, up_weight)).astype(LOW)
            for gate, up in zip(gate_low, up_low)
        )
    )
    gate_low, up_low, hidden, wide_two, down_wide = (
        jnp.concatenate(halves, axis=0) for halves in (gate_low, up_low, hidden, wide_two, down_wide)
    )
    grad_wide = jnp.concatenate(
        [
            dot_tn(part, tokens).astype(LOW).reshape(8, PADDED, D)
            for part, tokens in ((gate_low, wide_two), (up_low, wide_two), (hidden, down_wide))
        ],
        axis=1,
    )
    grad_wide = list(grad_wide.reshape(4, 2, 3 * PADDED, D))
    wide_first = scatter_first(grad_wide, "y")

    middle_part, gain_three = norm_backward(normed_two_grad, middle, scale_three, gain_rows[2])
    middle_grad = upstream + middle_part
    attn_grad, gain_two = norm_backward(middle_grad, attn_raw, scale_two, gain_rows[1])
    attn_low = attn_grad.astype(LOW)
    context_grad = dot_nt(attn_low, out_weight).astype(LOW)
    context_grad = jnp.concatenate(
        [context_grad[:, h * HD : (h + 1) * HD] for h in range(H)], axis=0
    )
    prob_grad = dot_nt(context_grad, values)
    probs = probs_low.astype(F32)
    centre = jnp.sum(probs * prob_grad, axis=-1, keepdims=True)
    score_low = (probs * (prob_grad - centre)).astype(LOW)
    wide_first, score_low = lax.optimization_barrier((wide_first, score_low))
    wide_parts = scatter_parts(grad_wide, wide_first, "y")
    key_part = dot_tn(score_low, query_rot) * SCALE
    value_part = dot_tn(probs_low, context_grad)
    pair_grad = jnp.concatenate([key_part, value_part], axis=1).astype(LOW)
    pair_grad = pair_grad.reshape(4, 2, OWN, 2 * HD)
    pair_grad = list(pair_grad)
    pair_first = scatter_first(pair_grad, "x")
    query_grad = dot_nn(score_low, keys) * SCALE
    query_raw_grad, query_gain = query_back(query_grad)
    query_low = query_raw_grad.astype(LOW)
    query_low = jnp.concatenate([query_low[h * OWN : (h + 1) * OWN] for h in range(H)], axis=1)
    mine, other = divide(
        place, [dot_tn(query_low, normed_one).astype(LOW), dot_tn(context, attn_low).astype(LOW)]
    )
    mine = add(mine, swap(other, "core")).astype(LOW)
    pair_first, mine = lax.optimization_barrier((pair_first, mine))
    pair_grad = add(*scatter_parts(pair_grad, pair_first, "x"))
    head_rows = scatter_ring(list(mine), "x").astype(LOW)
    pair_grad = add(pair_grad[0], swap(pair_grad[1].astype(LOW), "zh"))
    pair_grad, wide_parts = lax.optimization_barrier((pair_grad, wide_parts))
    wide_rows = sum_z(add(*wide_parts).astype(LOW))
    gate_shard, up_shard = wide_rows[:UNITS].T, wide_rows[PADDED : PADDED + UNITS].T
    down_rows = wide_rows[2 * PADDED : 2 * PADDED + UNITS].astype(LOW)
    key_raw_grad, key_gain = key_back(pair_grad[:, :HD])
    key_low = key_raw_grad.astype(LOW)
    value_grad_low = pair_grad[:, HD:].astype(LOW)
    normed_one_grad = (
        dot_nn(query_low, query_weight)
        + dot_nn(key_low, key_weight)
        + dot_nn(value_grad_low, value_weight)
    )
    stream_part, gain_one = norm_backward(normed_one_grad, stream, scale_one, gain_rows[0])
    input_grad = (middle_grad + stream_part).astype(LOW)

    gains_grad = jnp.concatenate([gain_one, gain_two, gain_three, gain_four], axis=0)
    head_grad = jnp.concatenate([query_gain, key_gain]).reshape(1, 2 * HD)
    head_grad = jnp.pad(head_grad, ((0, 0), (0, HALF - 2 * HD)))
    misc = jnp.concatenate(
        [gains_grad, jnp.concatenate([head_grad, head_grad], axis=1), jnp.zeros((11, D), F32)],
        axis=0,
    )
    mine, other = divide(
        place,
        [dot_tn(key_low, normed_one).astype(LOW), dot_tn(value_grad_low, normed_one).astype(LOW)],
        misc.astype(LOW),
    )
    mine = add(mine[0], swap(other[0], "core")).astype(LOW)
    rows = jnp.concatenate([mine, head_rows], axis=1).reshape(4, 2, 5, 16, D)
    rows = sum_z(scatter_ring(list(rows), "y").astype(LOW))
    query_shard = rows[3].T
    down_rows = jnp.concatenate([down_rows, rows[4].astype(LOW)], axis=0)
    down_rows = down_rows.reshape(UNITS + 16, 16, 36).transpose(1, 0, 2)
    down_rows = lax.all_to_all(down_rows, groups, 0, 0, tiled=True).astype(F32)
    down_shard = down_rows[:, :UNITS].reshape(16 * UNITS, 36)
    out_shard = down_rows[:, UNITS:].reshape(HD, 36)
    pair_rows = add(*gather_direct(rows[:3].astype(LOW), "x"))
    key_shard, value_shard = pair_rows[0].T, pair_rows[1].T
    gains_shard = lax.dynamic_slice(pair_rows[2], (0, gain_place), (4, 9))
    head_shard = lax.dynamic_slice(
        pair_rows[2, 4, : 2 * HD].reshape(2, HD), (0, head_place), (2, 16)
    )
    return (
        result,
        input_grad,
        query_shard,
        key_shard,
        value_shard,
        out_shard,
        gate_shard,
        up_shard,
        down_shard,
        gains_shard,
        head_shard,
    )


def solution(mesh):
    split = Mesh(mesh.devices.reshape(4, 2, 2, 2, 4), ("y", "zl", "core", "zh", "x"))
    dp = ("y", "zl", "core")
    weights = (
        P("zh", ("x",) + dp),
        P("zh", dp),
        P("zh", dp),
        P("x", ("zh",) + dp),
        P("zh", ("x",) + dp),
        P("zh", ("x",) + dp),
        P("x", ("zh",) + dp),
        P(None, ("zh", "x") + dp),
        P(None, dp),
    )
    tokens = P(dp + ("zh", "x"), None)
    return jax.shard_map(
        on_device,
        mesh=split,
        in_specs=(tokens, P(dp), P(dp), tokens) + weights,
        out_specs=(tokens, tokens) + weights,
        check_vma=False,
    )
```
